32 devices in a mesh: wide: 8 (over y, x, core), narrow: 4 (over z).
Axes of the slice: x: 2, y: 2, z: 4, core: 2. Of those that a mesh axis runs over, the one named last changes fastest.
Arguments:
- layer_input: bfloat16 [16384, 768], P(('wide', 'narrow')), may hold values from -6 to 6
- cotangent: bfloat16 [16384, 768], P(('wide', 'narrow')), may hold values from -6 to 6
- lengths: int32 [32], P(('wide', 'narrow')), may hold values from 1 to 512, as said below
- attention_in: float32 [3, 768, 768], P(None, None, ('wide', 'narrow'))
- attention_out: float32 [768, 768], P(('wide', 'narrow'))
- expand_weight: float32 [768, 3072], P(None, ('wide', 'narrow'))
- reduce_weight: float32 [3072, 768], P(('wide', 'narrow'))
- vector_params: float32 [9216], P(('wide', 'narrow')), as said below
- velocity_in: float32 [3, 768, 768], P(None, None, ('wide', 'narrow')), may hold values from -0.00024414062 to 0.00024414062
- velocity_out: float32 [768, 768], P(('wide', 'narrow')), may hold values from -0.00024414062 to 0.00024414062
- velocity_expand: float32 [768, 3072], P(None, ('wide', 'narrow')), may hold values from -0.00024414062 to 0.00024414062
- velocity_reduce: float32 [3072, 768], P(('wide', 'narrow')), may hold values from -0.00024414062 to 0.00024414062
- velocity_vector: float32 [9216], P(('wide', 'narrow')), may hold values from -0.00048828125 to 0.00048828125
- average_in: float32 [3, 768, 768], P(None, None, ('wide', 'narrow')), may hold values from -0.21875 to 0.21875
- average_out: float32 [768, 768], P(('wide', 'narrow')), may hold values from -0.21875 to 0.21875
- average_expand: float32 [768, 3072], P(None, ('wide', 'narrow')), may hold values from -0.21875 to 0.21875
- average_reduce: float32 [3072, 768], P(('wide', 'narrow')), may hold values from -0.109375 to 0.109375
- average_vector: float32 [9216], P(('wide', 'narrow')), may hold values from -4 to 4
Outputs:
- layer_output: bfloat16 [16384, 768], P(('wide', 'narrow'))
- input_grad: bfloat16 [16384, 768], P(('wide', 'narrow'))
- new_attention_in: float32 [3, 768, 768], P(None, None, ('wide', 'narrow'))
- new_attention_out: float32 [768, 768], P(('wide', 'narrow'))
- new_expand: float32 [768, 3072], P(None, ('wide', 'narrow'))
- new_reduce: float32 [3072, 768], P(('wide', 'narrow'))
- new_vectors: float32 [9216], P(('wide', 'narrow'))
- new_velocity_in: float32 [3, 768, 768], P(None, None, ('wide', 'narrow'))
- new_velocity_out: float32 [768, 768], P(('wide', 'narrow'))
- new_velocity_expand: float32 [768, 3072], P(None, ('wide', 'narrow'))
- new_velocity_reduce: float32 [3072, 768], P(('wide', 'narrow'))
- new_velocity_vector: float32 [9216], P(('wide', 'narrow'))
- new_average_in: float32 [3, 768, 768], P(None, None, ('wide', 'narrow'))
- new_average_out: float32 [768, 768], P(('wide', 'narrow'))
- new_average_expand: float32 [768, 3072], P(None, ('wide', 'narrow'))
- new_average_reduce: float32 [3072, 768], P(('wide', 'narrow'))
- new_average_vector: float32 [9216], P(('wide', 'narrow'))
- grad_norm: float32 [], replicated
The draws below stay inside these ranges and needn't reach their ends.
Inputs may be any that keep to these rules, and one draw needn't show every extreme that they name: `lengths`: some sequence has exactly 512 real tokens. `vector_params`: the gains lie between 0.5 and 1.5.
All inputs are finite; a program needn't handle non-finite values.
Results may differ from the reference program's by a relative error of at most 0.017.
The reference program's roundings to bfloat16 on the way count: a program that leaves them out, or rounds other values in their place, can miss the bound.
Values may be sent and summed in bfloat16 or wider, within the bound.
No kernel may reach another device: no remote copies, remote signals or barrier semaphores. Data moves between devices by JAX's collectives and lax.ppermute only.
A program may use at most 192 MiB of HBM per device.

```python
import math
import jax
import jax.numpy as jnp
from jax import lax

D = 768
FF = 3072
HEADS = 12
HEAD_DIM = 64
LENGTH = 512
SEQ_DEV = 1
STEP = 10
WIDE_RANKS = 8
NARROW_RANKS = 4
SEQS = 32
TOKENS = 16384
NVEC = 9216


def rising(count):
    index = jnp.arange(count, dtype=jnp.int32)
    device = index * (WIDE_RANKS * NARROW_RANKS) // count
    outer = (device // NARROW_RANKS).astype(jnp.float32) / max(WIDE_RANKS - 1, 1)
    inner = (device % NARROW_RANKS).astype(jnp.float32) / max(NARROW_RANKS - 1, 1)
    return jnp.exp(0.5 * math.log(3.0) * (outer + inner - 1.0))


def draw_attention_in(key, part):
    key = jax.random.fold_in(key, 11)
    base = jax.random.truncated_normal(key, -4.0, 4.0, (3, D, D), jnp.float32)
    factors = jnp.array([1.22, 1.22, 1.0], jnp.float32)[:, None, None]
    return base * factors * rising(D)[None, None, :] / math.sqrt(D)


def draw_attention_out(key, part):
    key = jax.random.fold_in(key, 12)
    base = jax.random.truncated_normal(key, -4.0, 4.0, (D, D), jnp.float32)
    return base * rising(D)[:, None] * 4.0 / math.sqrt(D)


def draw_expand_weight(key, part):
    key = jax.random.fold_in(key, 13)
    base = jax.random.truncated_normal(key, -4.0, 4.0, (D, FF), jnp.float32)
    return base * rising(FF)[None, :] / math.sqrt(D)


def draw_reduce_weight(key, part):
    key = jax.random.fold_in(key, 14)
    base = jax.random.truncated_normal(key, -4.0, 4.0, (FF, D), jnp.float32)
    return base * rising(FF)[:, None] * 1.5 / math.sqrt(FF)


def draw_vector_params(key, part):
    key = jax.random.fold_in(key, 15)
    base = jax.random.truncated_normal(key, -4.0, 4.0, (8 * D + FF,), jnp.float32)
    widths = jnp.concatenate([jnp.full((3 * D,), 0.5), jnp.full((D,), 0.1), jnp.full((D,), 0.5), jnp.full((FF,), 0.5), jnp.full((D,), 0.5), jnp.full((D,), 0.1), jnp.full((D,), 0.5)]).astype(jnp.float32)
    centers = jnp.concatenate([jnp.zeros((3 * D,)), jnp.ones((D,)), jnp.zeros((D + FF + D,)), jnp.ones((D,)), jnp.zeros((D,))]).astype(jnp.float32)
    return centers + widths * base


def draw_lengths(key, part):
    key = jax.random.fold_in(key, 16)
    sequence = jnp.arange(SEQS, dtype=jnp.int32)
    device = sequence // SEQ_DEV
    outer = device // NARROW_RANKS
    inner = device % NARROW_RANKS
    span_wide = max(WIDE_RANKS - 1, 1)
    span_narrow = max(NARROW_RANKS - 1, 1)
    base = LENGTH * (span_wide + 2 * outer) * (span_narrow + 2 * inner) // (9 * span_wide * span_narrow)
    base = jnp.maximum(base, 1)
    drawn = jax.random.randint(key, (SEQS,), 0, 1 << 20, dtype=jnp.int32) % (base // 4 + 1)
    lengths_drawn = jnp.maximum(base - drawn, 1)
    return jnp.where(sequence == SEQS - 1, LENGTH, lengths_drawn).astype(jnp.int32)


def block_levels(rng, shape, shards, least, high):
    def one(position, parts):
        steps = jax.random.uniform(jax.random.fold_in(jax.random.fold_in(rng, 6), position), (parts,), jnp.float32, least / len(shards), high / len(shards))
        return jnp.repeat(jnp.exp(steps), shape[position] // parts).reshape((-1,) + (1,) * (len(shape) - position - 1))

    loudness = one(*shards[0])
    for cut in shards[1:]:
        loudness = loudness * one(*cut)
    return loudness


def centred(rng, dims, scale, bound, split=(), held_as=jnp.bfloat16):
    values = jax.random.normal(rng, dims, jnp.float32) * scale
    if len(split) > 0:
        values = block_levels(rng, dims, split, -0.22, 0.18) * values
    return jnp.clip(values, min=-bound, max=bound).astype(held_as)


def setup_inputs(seed: int = 0) -> dict:
    key_list = jax.random.split(jax.random.key(seed), 19)
    layer_input = centred(key_list[0], (TOKENS, D), 1.0, 6.0, ((0, 32),))
    cotangent = centred(key_list[1], (TOKENS, D), 1.0, 6.0, ((0, 32),))
    lengths = draw_lengths(jax.random.fold_in(key_list[18], 71), 0)
    attention_in = draw_attention_in(jax.random.fold_in(key_list[18], 71), 0)
    attention_out = draw_attention_out(jax.random.fold_in(key_list[18], 71), 0)
    expand_weight = draw_expand_weight(jax.random.fold_in(key_list[18], 71), 0)
    reduce_weight = draw_reduce_weight(jax.random.fold_in(key_list[18], 71), 0)
    vector_params = draw_vector_params(jax.random.fold_in(key_list[18], 71), 0)
    velocity_in = centred(key_list[8], (3, D, D), (83 * (4 * D * D + 2 * D * FF)) ** -0.5, 0.00024414062, ((2, 32),), jnp.float32)
    velocity_out = centred(key_list[9], (D, D), (83 * (4 * D * D + 2 * D * FF)) ** -0.5, 0.00024414062, ((0, 32),), jnp.float32)
    velocity_expand = centred(key_list[10], (D, FF), (83 * (4 * D * D + 2 * D * FF)) ** -0.5, 0.00024414062, ((1, 32),), jnp.float32)
    velocity_reduce = centred(key_list[11], (FF, D), (83 * (4 * D * D + 2 * D * FF)) ** -0.5, 0.00024414062, ((0, 32),), jnp.float32)
    velocity_vector = centred(key_list[12], (NVEC,), (20 * (4 * D * D + 2 * D * FF)) ** -0.5, 0.00048828125, ((0, 32),), jnp.float32)
    average_in = centred(key_list[13], (3, D, D), D ** -0.5, 0.21875, ((2, 32),), jnp.float32)
    average_out = centred(key_list[14], (D, D), D ** -0.5, 0.21875, ((0, 32),), jnp.float32)
    average_expand = centred(key_list[15], (D, FF), D ** -0.5, 0.21875, ((1, 32),), jnp.float32)
    average_reduce = centred(key_list[16], (FF, D), FF ** -0.5, 0.109375, ((0, 32),), jnp.float32)
    average_vector = centred(key_list[17], (NVEC,), 0.5, 4.0, ((0, 32),), jnp.float32)
    return {"layer_input": layer_input, "cotangent": cotangent, "lengths": lengths, "attention_in": attention_in, "attention_out": attention_out, "expand_weight": expand_weight, "reduce_weight": reduce_weight, "vector_params": vector_params, "velocity_in": velocity_in, "velocity_out": velocity_out, "velocity_expand": velocity_expand, "velocity_reduce": velocity_reduce, "velocity_vector": velocity_vector, "average_in": average_in, "average_out": average_out, "average_expand": average_expand, "average_reduce": average_reduce, "average_vector": average_vector}


@jax.custom_vjp
def low(v):
    return lax.optimization_barrier(v.astype(jnp.bfloat16)).astype(jnp.float32)

@jax.custom_vjp
def low_back(v):
    return v

def low_keep(v):
    return (low(v), None)

def low_pass(kept, grad):
    return (grad,)

def back_keep(v):
    return (v, None)

def back_low(kept, grad):
    return (low(grad),)
low.defvjp(low_keep, low_pass)
low_back.defvjp(back_keep, back_low)
precise = lax.Precision.HIGHEST
MOMENTUM = 0.9
RATE_MATRIX = 24.0
RATE_PROJECTION = 160.0
RATE_VECTOR = 256.0
EPSILON = 1e-05

def layer_norm(inputs, scaling, offset):
    center = inputs - lax.optimization_barrier(jnp.mean(inputs, axis=-1, keepdims=True))
    spread = lax.optimization_barrier(jnp.mean(center * center, axis=-1, keepdims=True))
    return center * lax.rsqrt(spread + EPSILON) * scaling + offset

def attend(packed):
    segment, length = packed
    queries = segment[:, 0]
    key_rows = segment[:, 1]
    values = segment[:, 2]
    scores = jnp.einsum('qhd,khd->hqk', queries, key_rows, precision=precise, preferred_element_type=jnp.float32)
    scores = low_back(scores * HEAD_DIM ** (-0.5))
    visible = jnp.arange(LENGTH, dtype=jnp.int32) < length
    scores = jnp.where(visible[None, None, :], scores, -1000000000.0)
    chances = low(jax.nn.softmax(scores, axis=-1))
    return jnp.einsum('hqk,khd->qhd', chances, values, precision=precise, preferred_element_type=jnp.float32)

def forward(weights, inputs, spans):
    whole_in = low(weights[0])
    whole_out = low(weights[1])
    whole_expand = low(weights[2])
    whole_reduce = low(weights[3])
    vector = low(weights[4])
    bias_query = vector[0:D]
    bias_value = vector[D:2 * D]
    bias_out = vector[2 * D:3 * D]
    gain_one = vector[3 * D:4 * D]
    shift_one = vector[4 * D:5 * D]
    bias_expand = vector[5 * D:5 * D + FF]
    bias_reduce = vector[5 * D + FF:6 * D + FF]
    gain_two = vector[6 * D + FF:7 * D + FF]
    shift_two = vector[7 * D + FF:8 * D + FF]
    count_rows = inputs.shape[0]
    bias_three = jnp.stack([bias_query, jnp.zeros_like(bias_query), bias_value])
    mixed = jnp.einsum('td,cde->tce', inputs, whole_in, precision=precise, preferred_element_type=jnp.float32) + bias_three[None]
    mixed = low(low_back(mixed))
    blocks = mixed.reshape(count_rows // LENGTH, LENGTH, 3, HEADS, HEAD_DIM)
    context = lax.map(jax.checkpoint(attend), (blocks, spans))
    context = low(low_back(context.reshape(count_rows, D)))
    branch = low_back(jnp.dot(context, whole_out, precision=precise, preferred_element_type=jnp.float32) + bias_out)
    normed = layer_norm(inputs + branch, gain_one, shift_one)
    before = low_back(jnp.dot(low(normed), whole_expand, precision=precise, preferred_element_type=jnp.float32) + bias_expand)
    active = low(jax.nn.gelu(before, approximate=False))
    second = low_back(jnp.dot(active, whole_reduce, precision=precise, preferred_element_type=jnp.float32) + bias_reduce)
    return layer_norm(normed + second, gain_two, shift_two)

def advance(master, velocity, average, gradient, factor, rate):
    clipped = gradient * factor
    velocity_new = MOMENTUM * velocity + clipped
    master_new = master - rate * (clipped + MOMENTUM * velocity_new)
    blend = min(0.999, (1 + STEP) / (10 + STEP))
    return (master_new, velocity_new, blend * average + (1.0 - blend) * master_new)

def reference(layer_input, cotangent, lengths, attention_in, attention_out, expand_weight, reduce_weight, vector_params, velocity_in, velocity_out, velocity_expand, velocity_reduce, velocity_vector, average_in, average_out, average_expand, average_reduce, average_vector):
    params = (attention_in, attention_out, expand_weight, reduce_weight, vector_params)
    per_group = math.gcd(SEQS, max(1, 4096 // LENGTH))
    groups = SEQS // per_group
    inputs = layer_input.astype(jnp.float32).reshape(groups, per_group * LENGTH, D)
    upstream = cotangent.astype(jnp.float32).reshape(groups, per_group * LENGTH, D)
    spans = lengths.reshape(groups, per_group)

    def accumulate(totals, packed):
        inputs_part, upstream_part, spans_part = packed
        visible = (jnp.arange(LENGTH, dtype=jnp.int32)[None, :] < spans_part[:, None]).reshape(-1, 1)
        result, pullback = jax.vjp(lambda weights, rows_in: forward(weights, rows_in, spans_part), params, inputs_part)
        grads_params, grads_input = pullback(jnp.where(visible, upstream_part, 0.0))
        totals = jax.tree.map(jnp.add, totals, grads_params)
        return (totals, (result.astype(jnp.bfloat16), grads_input.astype(jnp.bfloat16)))
    totals, (outputs, input_grads) = lax.scan(accumulate, jax.tree.map(jnp.zeros_like, params), (inputs, upstream, spans))
    squares = jnp.sum(totals[0] * totals[0]) + jnp.sum(totals[1] * totals[1]) + jnp.sum(totals[2] * totals[2])
    squares = squares + jnp.sum(totals[3] * totals[3]) + jnp.sum(totals[4] * totals[4])
    grad_norm = jnp.sqrt(squares)
    factor = 1.0 / jnp.maximum(grad_norm, 1.0)
    new_in, vel_in, avg_in = advance(attention_in, velocity_in, average_in, totals[0], factor, RATE_MATRIX)
    new_out, vel_out, avg_out = advance(attention_out, velocity_out, average_out, totals[1], factor, RATE_PROJECTION)
    new_expand, vel_expand, avg_expand = advance(expand_weight, velocity_expand, average_expand, totals[2], factor, RATE_MATRIX)
    new_reduce, vel_reduce, avg_reduce = advance(reduce_weight, velocity_reduce, average_reduce, totals[3], factor, RATE_MATRIX)
    new_vector, vel_vector, avg_vector = advance(vector_params, velocity_vector, average_vector, totals[4], factor, RATE_VECTOR)
    return (outputs.reshape(TOKENS, D), input_grads.reshape(TOKENS, D), new_in, new_out, new_expand, new_reduce, new_vector, vel_in, vel_out, vel_expand, vel_reduce, vel_vector, avg_in, avg_out, avg_expand, avg_reduce, avg_vector, grad_norm)
```

```python
from functools import partial

import jax
import jax.numpy as jnp
from jax import lax
from jax.sharding import PartitionSpec as P

D = 768
FF = 3072
HEADS = 12
HEAD_DIM = 64
LENGTH = 512
STEP = 10
NVEC = 8 * D + FF


MOMENTUM = 0.9
RATE_MATRIX = 24.0
RATE_PROJECTION = 160.0
RATE_VECTOR = 256.0
EPSILON = 1e-05
MASKED = -1000000000.0


AXES = ("wide", "narrow")
BF = jnp.bfloat16
F32 = jnp.float32


class Cube:
    def __init__(self, wide, narrow):
        self.wide, self.narrow = wide, narrow
        wide_bits, narrow_bits = wide.bit_length() - 1, narrow.bit_length() - 1
        plane = list(range(1, wide_bits))
        half = len(plane) // 2
        swapped = plane[half:] + plane[:half] if len(plane) % 2 == 0 else plane
        self.depth = [(bit, bit) for bit in reversed(range(narrow_bits))]
        self.plane = list(zip(plane, swapped))
        self.wide_at = lax.axis_index("wide")
        self.narrow_at = lax.axis_index("narrow")

    def swap_narrow(self, array, bit):
        return lax.ppermute(array, "narrow", [(i, i ^ (1 << bit)) for i in range(self.narrow)])

    def swap_plane(self, array, step):
        pairs = [(i, i ^ (1 << self.plane[step][i & 1])) for i in range(self.wide)]
        return lax.ppermute(array, "wide", pairs)

    def swap_core(self, array):
        return lax.ppermute(array, "wide", [(i, i ^ 1) for i in range(self.wide)])

    def plane_slots(self):
        apart = jnp.arange(self.wide, dtype=jnp.int32) ^ self.wide_at

        def placed(which):
            slot = (apart & 1) << len(self.plane)
            for position, bits in enumerate(self.plane):
                slot = slot | (((apart >> bits[which]) & 1) << position)
            return slot

        return jnp.where(((apart ^ self.wide_at) & 1) == 0, placed(0), placed(1))

    def plane_owners(self):
        slot = jnp.arange(self.wide, dtype=jnp.int32)

        def placed(which):
            apart = slot >> len(self.plane)
            for position, bits in enumerate(self.plane):
                apart = apart | (((slot >> position) & 1) << bits[which])
            return apart ^ self.wide_at

        core = (slot >> len(self.plane)) ^ (self.wide_at & 1)
        return jnp.where(core == 0, placed(0), placed(1))

    def narrow_owners(self):
        slot = jnp.arange(self.narrow, dtype=jnp.int32)
        apart = jnp.zeros_like(slot)
        for position, (bit, _) in enumerate(self.depth):
            apart = apart | (((slot >> position) & 1) << bit)
        return apart ^ self.narrow_at

    def narrow_slots(self):
        apart = jnp.arange(self.narrow, dtype=jnp.int32) ^ self.narrow_at
        slot = jnp.zeros_like(apart)
        for position, (bit, _) in enumerate(self.depth):
            slot = slot | (((apart >> bit) & 1) << position)
        return slot

    def gather_narrow(self, block):
        slots = block[None]
        for bit, _ in self.depth:
            slots = jnp.concatenate([slots, self.swap_narrow(slots, bit)])
        return slots

    def gather_plane(self, block):
        slots = block[None]
        for step in range(len(self.plane)):
            slots = jnp.concatenate([slots, self.swap_plane(slots, step)])
        return slots

    def gather_core(self, block):
        return jnp.stack([block, self.swap_core(block)])

    def halve(self, parts, step, swap):
        half = parts[0].shape[0] // 2
        leaving = total([part[half:] for part in parts]).astype(BF)
        return [part[:half] for part in parts] + [swap(leaving, step)]

    def scatter_core(self, own, other):
        return [own, self.swap_core(other)]

    def scatter_plane(self, parts):
        for step in reversed(range(len(self.plane))):
            parts = self.halve(parts, step, self.swap_plane)
        return parts

    def scatter_narrow(self, parts):
        for bit, _ in reversed(self.depth):
            parts = self.halve(parts, bit, self.swap_narrow)
        return parts

    def scatter_narrow_true(self, parts, axis):
        for bit in range(len(self.depth)):
            mine = (self.narrow_at >> bit) & 1
            shape = parts[0].shape
            cut = shape[:axis] + (shape[axis] // 2, 2) + shape[axis + 1 :]
            parts = [part.reshape(cut) for part in parts]
            pick = lambda part, at: lax.dynamic_index_in_dim(part, at, axis + 1, keepdims=False)
            leaving = total([pick(part, 1 - mine) for part in parts]).astype(BF)
            parts = [pick(part, mine) for part in parts] + [self.swap_narrow(leaving, bit)]
        return parts


def total(parts):
    result = parts[0].astype(F32)
    for part in parts[1:]:
        result = result + part.astype(F32)
    return result


def norm_forward(inputs, scaling, offset):
    center = inputs - jnp.mean(inputs, axis=-1, keepdims=True)
    factor = lax.rsqrt(jnp.mean(center * center, axis=-1, keepdims=True) + EPSILON)
    unit_rows = center * factor
    return (unit_rows * scaling + offset, unit_rows, factor)


def norm_backward(upstream, unit_rows, factor, scaling):
    scaled = upstream * scaling
    adjusted = (
        scaled
        - jnp.mean(scaled, axis=-1, keepdims=True)
        - unit_rows * jnp.mean(scaled * unit_rows, axis=-1, keepdims=True)
    )
    return (adjusted * factor, jnp.sum(upstream * unit_rows, axis=0), jnp.sum(upstream, axis=0))


def masked_scores(segment, length):
    scores = jnp.einsum(
        "qhd,khd->hqk", segment[:, 0], segment[:, 1], preferred_element_type=jnp.float32
    ) * HEAD_DIM ** (-0.5)
    visible = jnp.arange(segment.shape[0], dtype=jnp.int32) < length
    return jnp.where(visible[None, None, :], scores, MASKED)


def attend_forward(packed):
    segment, length = packed
    scores = masked_scores(segment, length)
    largest = jnp.max(scores, axis=-1, keepdims=True)
    powers = jnp.exp(scores - largest)
    totals = jnp.sum(powers, axis=-1, keepdims=True)
    chances_low = (powers / totals).astype(jnp.bfloat16)
    context = jnp.einsum(
        "hqk,khd->qhd", chances_low, segment[:, 2], preferred_element_type=jnp.float32
    )
    return (context.astype(jnp.bfloat16), largest + jnp.log(totals))


def attend_backward(packed):
    segment, log_totals, grad_context, length = packed
    scores = masked_scores(segment, length)
    chances = jnp.exp(scores - log_totals)
    chances_low = chances.astype(jnp.bfloat16)
    grad_chances = jnp.einsum(
        "qhd,khd->hqk", grad_context, segment[:, 2], preferred_element_type=jnp.float32
    )
    grad_values = jnp.einsum(
        "hqk,qhd->khd", chances_low, grad_context, preferred_element_type=jnp.float32
    )
    row_inner = jnp.sum(chances * grad_chances, axis=-1, keepdims=True)
    grad_scores = (chances * (grad_chances - row_inner)).astype(jnp.bfloat16)
    grad_queries = jnp.einsum(
        "hqk,khd->qhd", grad_scores, segment[:, 1], preferred_element_type=jnp.float32
    ) * HEAD_DIM ** (-0.5)
    grad_keys = jnp.einsum(
        "hqk,qhd->khd", grad_scores, segment[:, 0], preferred_element_type=jnp.float32
    ) * HEAD_DIM ** (-0.5)
    return jnp.stack([grad_queries, grad_keys, grad_values], axis=1).astype(jnp.bfloat16)


def advance(master, velocity, average, gradient, factor, rate):
    clipped = gradient * factor
    velocity_new = MOMENTUM * velocity + clipped
    master_new = master - rate * (clipped + MOMENTUM * velocity_new)
    blend = min(0.999, (1 + STEP) / (10 + STEP))
    return (master_new, velocity_new, blend * average + (1.0 - blend) * master_new)


def scatter_rows(cube, rows, width):
    cut = rows.reshape(2, cube.wide // 2, cube.narrow, width, D)
    parts = cube.scatter_plane(cube.scatter_core(cut[0], cut[1]))
    return total(cube.scatter_narrow([part[0] for part in parts]))[0]


def body(
    wide,
    narrow,
    layer_input,
    cotangent,
    lengths,
    attention_in,
    attention_out,
    expand_weight,
    reduce_weight,
    vector_params,
    velocity_in,
    velocity_out,
    velocity_expand,
    velocity_reduce,
    velocity_vector,
    average_in,
    average_out,
    average_expand,
    average_reduce,
    average_vector,
):
    tokens_here = layer_input.shape[0]
    sequences = tokens_here // LENGTH
    cube = Cube(wide, narrow)
    shards = wide * narrow
    share = D // shards
    width = FF // shards
    spare = NVEC // shards
    owners, slots = cube.plane_owners(), cube.plane_slots()
    vector_rows = 8 * (-(-spare // (8 * D)))
    extra = jnp.zeros((vector_rows * D,), BF).at[:spare].set(vector_params.astype(BF)).reshape(vector_rows, D)
    near = jnp.concatenate(
        [attention_in.astype(BF).transpose(0, 2, 1).reshape(3 * share, D), attention_out.astype(BF), extra]
    )
    near = jnp.take(cube.gather_narrow(near), cube.narrow_slots(), axis=0)
    blocks_in = near[:, : 4 * share].reshape(narrow, 4, share, D).transpose(1, 0, 2, 3).reshape(4 * narrow * share, D)
    near = jnp.concatenate([blocks_in, near[:, 4 * share :].reshape(narrow * vector_rows, D)])
    near = cube.gather_core(cube.gather_plane(near)).reshape(wide, -1, D)
    near = jnp.take(near, slots, axis=0)
    rows = narrow * share
    whole_query, whole_key, whole_value, whole_out = (
        near[:, i * rows : (i + 1) * rows].reshape(D, D) for i in range(4)
    )
    vector = near[:, 4 * rows :].reshape(shards, vector_rows * D)[:, :spare].reshape(NVEC).astype(F32)
    expand_rows = expand_weight.astype(BF).T
    reduce_rows = reduce_weight.astype(BF)
    whole_expand = cube.gather_core(cube.gather_plane(cube.gather_narrow(expand_rows))).reshape(FF, D)
    whole_reduce = cube.gather_core(cube.gather_plane(cube.gather_narrow(reduce_rows))).reshape(FF, D)
    bias_query = vector[0:D]
    bias_value = vector[D : 2 * D]
    bias_out = vector[2 * D : 3 * D]
    gain_one = vector[3 * D : 4 * D]
    shift_one = vector[4 * D : 5 * D]
    bias_expand = vector[5 * D : 5 * D + FF].reshape(wide, narrow, width)
    bias_expand = jnp.take(jnp.take(bias_expand, owners, axis=0), cube.narrow_owners(), axis=1).reshape(FF)
    bias_reduce = vector[5 * D + FF : 6 * D + FF]
    gain_two = vector[6 * D + FF : 7 * D + FF]
    shift_two = vector[7 * D + FF : 8 * D + FF]
    inputs_wide = layer_input.astype(jnp.float32)
    whole_in = jnp.stack([whole_query, whole_key, whole_value])
    bias_three = jnp.stack([bias_query, jnp.zeros_like(bias_query), bias_value])
    mixed = (
        jnp.einsum("td,ced->tce", layer_input, whole_in, preferred_element_type=jnp.float32)
        + bias_three[None]
    )
    blocks = mixed.astype(jnp.bfloat16).reshape(sequences, LENGTH, 3, HEADS, HEAD_DIM)
    context, log_totals = lax.map(attend_forward, (blocks, lengths))
    context_low = context.reshape(tokens_here, D)
    branch = jnp.dot(context_low, whole_out, preferred_element_type=jnp.float32) + bias_out
    normed_one, unit_one, factor_one = norm_forward(inputs_wide + branch, gain_one, shift_one)
    normed_low = normed_one.astype(jnp.bfloat16)
    before = jnp.einsum("td,fd->tf", normed_low, whole_expand, preferred_element_type=jnp.float32) + bias_expand
    active_low = jax.nn.gelu(before, approximate=False).astype(jnp.bfloat16)
    second = jnp.dot(active_low, whole_reduce, preferred_element_type=jnp.float32) + bias_reduce
    output_wide, unit_two, factor_two = norm_forward(normed_one + second, gain_two, shift_two)
    positions = jnp.arange(LENGTH, dtype=jnp.int32)
    visible = (positions[None, :] < lengths[:, None]).reshape(tokens_here, 1)
    grad_output = jnp.where(visible, cotangent.astype(jnp.float32), 0.0)
    grad_sum_two, grad_gain_two, grad_shift_two = norm_backward(
        grad_output, unit_two, factor_two, gain_two
    )
    grad_second = grad_sum_two.astype(jnp.bfloat16)
    grad_bias_reduce = jnp.sum(grad_second, axis=0, dtype=jnp.float32)
    grad_reduce_w = jnp.einsum(
        "tf,td->fd", active_low, grad_second, preferred_element_type=jnp.float32
    ).astype(BF)
    owned_reduce = scatter_rows(cube, grad_reduce_w, width)
    grad_active = jnp.einsum(
        "td,fd->tf", grad_second, whole_reduce, preferred_element_type=jnp.float32
    )
    ignored, gelu_pull = jax.vjp(partial(jax.nn.gelu, approximate=False), before)
    grad_before = gelu_pull(grad_active)[0].astype(jnp.bfloat16)
    grad_bias_expand = jnp.sum(grad_before, axis=0, dtype=jnp.float32)
    grad_expand_w = jnp.einsum(
        "tf,td->fd", grad_before, normed_low, preferred_element_type=jnp.float32
    ).astype(BF)
    owned_expand = scatter_rows(cube, grad_expand_w, width).T
    grad_normed = (
        jnp.einsum("tf,fd->td", grad_before, whole_expand, preferred_element_type=jnp.float32)
        + grad_sum_two
    )
    grad_sum_one, grad_gain_one, grad_shift_one = norm_backward(
        grad_normed, unit_one, factor_one, gain_one
    )
    grad_branch = grad_sum_one.astype(jnp.bfloat16)
    grad_bias_out = jnp.sum(grad_branch, axis=0, dtype=jnp.float32)
    grad_out_w = jnp.einsum(
        "td,te->de", context_low, grad_branch, preferred_element_type=jnp.float32
    )
    grad_context = jnp.einsum(
        "te,de->td", grad_branch, whole_out, preferred_element_type=jnp.float32
    ).astype(jnp.bfloat16)
    grad_blocks = lax.map(
        attend_backward,
        (blocks, log_totals, grad_context.reshape(sequences, LENGTH, HEADS, HEAD_DIM), lengths),
    )
    grad_mixed = grad_blocks.reshape(tokens_here, 3, D)
    grad_bias_mixed = jnp.sum(grad_mixed, axis=0, dtype=jnp.float32)
    grad_in_w = jnp.einsum(
        "td,tce->ced", layer_input, grad_mixed, preferred_element_type=jnp.float32
    )
    grad_input = grad_sum_one + jnp.einsum(
        "tce,ced->td", grad_mixed, whole_in, preferred_element_type=jnp.float32
    )
    grad_bias_expand = jnp.take(
        jnp.take(grad_bias_expand.reshape(wide, narrow, width), slots, axis=0), cube.narrow_slots(), axis=1
    ).reshape(FF)
    grad_vector = jnp.concatenate(
        [
            grad_bias_mixed[0],
            grad_bias_mixed[2],
            grad_bias_out,
            grad_gain_one,
            grad_shift_one,
            grad_bias_expand,
            grad_bias_reduce,
            grad_gain_two,
            grad_shift_two,
        ]
    )
    leaving = jnp.concatenate([grad_in_w.astype(BF), grad_out_w.astype(BF)[None]]).reshape(4, wide, rows, D)
    leaving = leaving.transpose(1, 0, 2, 3).reshape(wide, 4, narrow, share, D)
    leaving = leaving.transpose(0, 2, 1, 3, 4).reshape(wide, narrow, 4 * share, D)
    spread = jnp.zeros((wide, narrow, vector_rows * D), BF).at[:, :, :spare].set(
        grad_vector.astype(BF).reshape(wide, narrow, spare)
    )
    leaving = jnp.concatenate([leaving, spread.reshape(wide, narrow, vector_rows, D)], axis=2)
    leaving = jnp.take(leaving, owners, axis=0)
    parts = cube.scatter_plane(cube.scatter_core(leaving[: wide // 2], leaving[wide // 2 :]))
    owned = total(cube.scatter_narrow_true([part[0] for part in parts], 0))[0]
    owned_in = owned[: 3 * share].reshape(3, share, D).transpose(0, 2, 1)
    owned_out = owned[3 * share : 4 * share]
    owned_vector = owned[4 * share :].reshape(-1)[:spare]
    squares = (
        jnp.sum(owned_in * owned_in)
        + jnp.sum(owned_out * owned_out)
        + jnp.sum(owned_expand * owned_expand)
    )
    squares = squares + jnp.sum(owned_reduce * owned_reduce) + jnp.sum(owned_vector * owned_vector)
    spread_squares = lax.all_to_all(
        jnp.broadcast_to(squares.reshape(1, 1, 1), (shards, 1, 128)), AXES, 0, 0
    )
    grad_norm = jnp.sqrt(jnp.sum(spread_squares[:, 0, 0]))
    factor = 1.0 / jnp.maximum(grad_norm, 1.0)
    new_in, moved_in, mean_in = advance(
        attention_in, velocity_in, average_in, owned_in, factor, RATE_MATRIX
    )
    new_out, moved_out, mean_out = advance(
        attention_out, velocity_out, average_out, owned_out, factor, RATE_PROJECTION
    )
    new_expand, moved_expand, mean_expand = advance(
        expand_weight, velocity_expand, average_expand, owned_expand, factor, RATE_MATRIX
    )
    new_reduce, moved_reduce, mean_reduce = advance(
        reduce_weight, velocity_reduce, average_reduce, owned_reduce, factor, RATE_MATRIX
    )
    new_vector, moved_vector, mean_vector = advance(
        vector_params, velocity_vector, average_vector, owned_vector, factor, RATE_VECTOR
    )
    return (
        output_wide.astype(jnp.bfloat16),
        grad_input.astype(jnp.bfloat16),
        new_in,
        new_out,
        new_expand,
        new_reduce,
        new_vector,
        moved_in,
        moved_out,
        moved_expand,
        moved_reduce,
        moved_vector,
        mean_in,
        mean_out,
        mean_expand,
        mean_reduce,
        mean_vector,
        grad_norm,
    )


def solution(mesh):
    in_specs = (
        P(("wide", "narrow"), None),
        P(("wide", "narrow"), None),
        P(("wide", "narrow")),
        P(None, None, ("wide", "narrow")),
        P(("wide", "narrow"), None),
        P(None, ("wide", "narrow")),
        P(("wide", "narrow"), None),
        P(("wide", "narrow")),
        P(None, None, ("wide", "narrow")),
        P(("wide", "narrow"), None),
        P(None, ("wide", "narrow")),
        P(("wide", "narrow"), None),
        P(("wide", "narrow")),
        P(None, None, ("wide", "narrow")),
        P(("wide", "narrow"), None),
        P(None, ("wide", "narrow")),
        P(("wide", "narrow"), None),
        P(("wide", "narrow")),
    )
    out_specs = (
        P(("wide", "narrow"), None),
        P(("wide", "narrow"), None),
        P(None, None, ("wide", "narrow")),
        P(("wide", "narrow"), None),
        P(None, ("wide", "narrow")),
        P(("wide", "narrow"), None),
        P(("wide", "narrow")),
        P(None, None, ("wide", "narrow")),
        P(("wide", "narrow"), None),
        P(None, ("wide", "narrow")),
        P(("wide", "narrow"), None),
        P(("wide", "narrow")),
        P(None, None, ("wide", "narrow")),
        P(("wide", "narrow"), None),
        P(None, ("wide", "narrow")),
        P(("wide", "narrow"), None),
        P(("wide", "narrow")),
        P(),
    )
    return jax.shard_map(partial(body, mesh.shape["wide"], mesh.shape["narrow"]), mesh=mesh, in_specs=in_specs, out_specs=out_specs, check_vma=False)
```

```python
from functools import partial

import jax
import jax.numpy as jnp
from jax import lax
from jax.experimental import pallas as pl
from jax.experimental.pallas import tpu as pltpu
from jax.sharding import PartitionSpec as P

D = 768
FF = 3072
HEADS = 12
HEAD_DIM = 64
LENGTH = 512
STEP = 10
NVEC = 8 * D + FF
PAIRS = HEADS // 2
SUB = 256

MOMENTUM = 0.9
RATE_MATRIX = 24.0
RATE_PROJECTION = 160.0
RATE_VECTOR = 256.0
EPSILON = 1e-05
MASKED = -1000000000.0

AXES = ("wide", "narrow")
BF = jnp.bfloat16
F32 = jnp.float32
NN = ((1,), (0,))
NT = ((1,), (1,))
TN = ((0,), (0,))

BQ, BV, BO, GA, SA, B1, B2, GB, SB = 0, 1, 2, 3, 4, 5, 9, 10, 11


def dot(left, right, dims):
    return lax.dot_general(left, right, (dims, ((), ())), preferred_element_type=F32)


def mean(rows):
    return jnp.sum(rows, axis=-1, keepdims=True) * (1.0 / D)


def power_of_two(number):
    return number & -number


SMEM = pl.BlockSpec(memory_space=pltpu.SMEM)
ANY = pl.BlockSpec(memory_space=pl.ANY)


def run(kernel, name, grid, ins, outs, scratch=(), cost=(0, 0, 0), mebibytes=24):
    return pl.pallas_call(
        kernel,
        grid=grid,
        in_specs=[spec for _, spec in ins],
        out_specs=[spec for _, _, spec in outs],
        out_shape=[jax.ShapeDtypeStruct(shape, kind) if kind else shape for shape, kind, _ in outs],
        scratch_shapes=scratch,
        compiler_params=pltpu.CompilerParams(
            vmem_limit_bytes=mebibytes * 1024 * 1024, dimension_semantics=("arbitrary",) * len(grid)
        ),
        cost_estimate=pl.CostEstimate(flops=cost[0], bytes_accessed=cost[1], transcendentals=cost[2]),
        name=name,
    )(*[array for array, _ in ins])


def far_memory(array):
    return pltpu.with_memory_space_constraint(array, pltpu.HBM)


def whole(shape):
    return pl.BlockSpec(shape, lambda *i: (0,) * len(shape))


class Cube:
    def __init__(self, wide, narrow):
        self.wide, self.narrow = wide, narrow
        wide_bits, narrow_bits = wide.bit_length() - 1, narrow.bit_length() - 1
        plane = list(range(1, wide_bits))
        half = len(plane) // 2
        swapped = plane[half:] + plane[:half] if len(plane) % 2 == 0 else plane
        depth = list(range(narrow_bits))
        self.depth = list(zip(reversed(depth), depth))
        self.plane = list(zip(plane, swapped))
        self.wide_at = lax.axis_index("wide")
        self.narrow_at = lax.axis_index("narrow")

    def swap_depth(self, array, step):
        place = lambda w, n: w * self.narrow + n
        pairs = [
            (place(w, n), place(w, n ^ (1 << self.depth[step][w & 1])))
            for w in range(self.wide)
            for n in range(self.narrow)
        ]
        return lax.ppermute(array, AXES, pairs)

    def swap_plane(self, array, step):
        pairs = [(i, i ^ (1 << self.plane[step][i & 1])) for i in range(self.wide)]
        return lax.ppermute(array, "wide", pairs)

    def swap_core(self, array):
        return lax.ppermute(array, "wide", [(i, i ^ 1) for i in range(self.wide)])

    def slots(self, apart, bits, core):
        def placed(which):
            slot = jnp.zeros_like(apart)
            for position, pair in enumerate(bits):
                slot = slot | (((apart >> pair[which]) & 1) << position)
            return slot

        return jnp.where(core == 0, placed(0), placed(1))

    def owners(self, slot, bits, core):
        def placed(which):
            apart = jnp.zeros_like(slot)
            for position, pair in enumerate(bits):
                apart = apart | (((slot >> position) & 1) << pair[which])
            return apart

        return jnp.where(core == 0, placed(0), placed(1))

    def plane_owners(self):
        slot = jnp.arange(self.wide, dtype=jnp.int32)
        other = slot >> len(self.plane)
        return (other | self.owners(slot, self.plane, other ^ (self.wide_at & 1))) ^ self.wide_at

    def depth_slots(self):
        place = jnp.arange(self.narrow, dtype=jnp.int32)
        return self.slots(place ^ self.narrow_at, self.depth, self.wide_at & 1)

    def depth_owners(self):
        return self.owners(jnp.arange(self.narrow, dtype=jnp.int32), self.depth, self.wide_at & 1) ^ self.narrow_at

    def all_owners(self):
        slot = jnp.arange(self.wide * self.narrow, dtype=jnp.int32)
        deep, flat = slot % self.narrow, slot // self.narrow
        other = flat >> len(self.plane)
        core = other ^ (self.wide_at & 1)
        wide_place = (other | self.owners(flat, self.plane, core)) ^ self.wide_at
        return wide_place * self.narrow + (self.owners(deep, self.depth, core) ^ self.narrow_at)

    def all_slots(self):
        place = jnp.arange(self.wide * self.narrow, dtype=jnp.int32)
        flat, deep = (place // self.narrow) ^ self.wide_at, (place % self.narrow) ^ self.narrow_at
        core = (flat ^ self.wide_at) & 1
        slot = ((flat & 1) << len(self.plane)) | self.slots(flat, self.plane, core)
        return slot * self.narrow + self.slots(deep, self.depth, core)

    def leaving(self, parts):
        half = parts[-1].shape[1] // 2
        return combine(parts, half, half)


def total(parts):
    result = parts[0].astype(F32)
    for part in parts[1:]:
        result = result + part.astype(F32)
    return result


def combine_kernel(*refs):
    value = refs[0][...].astype(F32)
    for ref in refs[1:-1]:
        value = value + ref[...].astype(F32)
    refs[-1][...] = value.astype(refs[-1].dtype)


def combine(parts, first, count, kind=BF):
    groups, _, rows, _ = parts[-1].shape
    block = groups
    while block > 1 and block * count * rows > 512:
        block //= 2
    piece = count
    while piece > 1 and block * piece * rows > 512:
        piece //= 2
    steps = count // piece
    spec = pl.BlockSpec((block, piece, rows, D), lambda i, j: (i, j + first // piece, 0, 0))
    out = (groups, count, rows, D)
    size = count * rows * groups * D
    return run(
        combine_kernel,
        "combine",
        (groups // block, steps),
        [(far_memory(part), spec) for part in parts],
        [(out, kind, pl.BlockSpec((block, piece, rows, D), lambda i, j: (i, j, 0, 0)))],
        cost=(size * len(parts), 2 * size * (len(parts) + 1), 0),
    )[0]


def tie(array, *others):
    return lax.optimization_barrier((array,) + others)[0]


def project_kernel(unit, owners, x, near, far, near_other, far_other, columns, out, table, held):
    half = near.shape[0]
    step = power_of_two(unit)
    for place, ref in enumerate((near, far, near_other, far_other)):
        for slot in range(half):
            start = pl.multiple_of(owners[place * half + slot] * unit, step)
            for which in range(3):
                held[which, pl.ds(start, unit), :] = ref[slot, which * unit : (which + 1) * unit, :].astype(held.dtype)
    table[...] = held[...].astype(BF)
    rows = x[...]
    for which in range(3):
        for first in range(0, D, SUB):
            part = dot(table[which, first : first + SUB, :], rows, NT)
            if which == 0:
                part = (part + columns[first : first + SUB, BQ : BQ + 1]).astype(BF) * HEAD_DIM ** (-0.5)
            if which == 2:
                part = part + columns[first : first + SUB, BV : BV + 1]
            out[which, first : first + SUB, :] = part.astype(BF)


def attend_kernel(length, packed, context, log_totals):
    tile = 256
    rows = lax.broadcasted_iota(jnp.int32, (LENGTH, tile), 0)
    visible = rows < length[0]
    for start in range(0, LENGTH, tile):
        done = []
        for head in range(2):
            span = slice(HEAD_DIM * head, HEAD_DIM * (head + 1))
            queries = packed[0, span, start : start + tile]
            scores = jnp.where(visible, dot(packed[1, span, :], queries, TN), MASKED)
            largest = jnp.max(scores, axis=0, keepdims=True)
            powers = jnp.exp(scores - largest)
            totals = jnp.sum(powers, axis=0, keepdims=True)
            chances = (powers * (1.0 / totals)).astype(BF)
            done.append(dot(packed[2, span, :], chances, NN))
            log_totals[0, head : head + 1, start : start + tile] = largest + jnp.log(totals)
        context[start : start + tile, :] = jnp.concatenate(done, axis=0).T.astype(BF)


def join_kernel(unit, owners, x, context_a, context_b, near, far, near_other, far_other, table, weight, unit_rows, factor, low, base, held):
    half = near.shape[0]
    step = power_of_two(unit)

    @pl.when(pl.program_id(0) == 0)
    def _():
        for place, ref in enumerate((near, far, near_other, far_other)):
            for slot in range(half):
                start = pl.multiple_of(owners[place * half + slot] * unit, step)
                held[pl.ds(start, unit), :] = ref[slot].astype(held.dtype)
        weight[...] = held[...].astype(BF)

    branch = dot(context_a[...], weight[: D // 2, :], NN) + dot(context_b[...], weight[D // 2 :, :], NN)
    branch = branch + table[BO : BO + 1, :]
    rows = x[...].astype(F32) + branch
    center = rows - mean(rows)
    spread = lax.rsqrt(mean(center * center) + EPSILON)
    normed = center * spread
    unit_rows[...] = normed
    factor[...] = spread
    shifted = normed * table[GA : GA + 1, :] + table[SA : SA + 1, :]
    low[...] = shifted.astype(BF)
    base[...] = shifted + table[B2 : B2 + 1, :]


def gelu_pair(value):
    power = jnp.exp(value * value * -0.5)
    part = 1.0 / (1.0 + jnp.abs(value) * (0.3275911 * 0.5**0.5))
    tail = 0.5 * 1.061405429
    for factor in (-1.453152027, 1.421413741, -0.284496736, 0.254829592):
        tail = tail * part + 0.5 * factor
    tail = tail * part * power
    chance = jnp.where(value < 0.0, tail, 1.0 - tail)
    return value * chance, chance + value * power * (2.0 * jnp.pi) ** -0.5


def ffn_forward_kernel(low, expand, reduce, bias, start, active, slope, running):
    rows = low[...]
    expand, reduce = expand[...].reshape(D, D), reduce[...].reshape(D, D)
    total = start[...]
    for first in range(0, D, SUB):
        span = slice(first, first + SUB)
        value, change = gelu_pair(dot(rows, expand[span], NT) + bias[:, span])
        value = value.astype(BF)
        active[:, span] = value
        slope[:, span] = change.astype(BF)
        total = total + dot(value, reduce[span], NN)
    running[...] = total


def loss_kernel(length, rows, cotangent, table, output, grad, grad_low, sums):
    tile = rows.shape[0]
    value = rows[...]
    center = value - mean(value)
    factor = lax.rsqrt(mean(center * center) + EPSILON)
    normed = center * factor
    gain = table[GB : GB + 1, :]
    output[...] = (normed * gain + table[SB : SB + 1, :]).astype(BF)
    place = pl.program_id(0) * tile + lax.broadcasted_iota(jnp.int32, (tile, 1), 0)
    upstream = jnp.where(place < length[0], cotangent[...].astype(F32), 0.0)
    scaled = upstream * gain
    change = factor * (scaled - mean(scaled) - normed * mean(scaled * normed))
    grad[...] = change
    change_low = change.astype(BF)
    grad_low[...] = change_low

    @pl.when(pl.program_id(0) == 0)
    def _():
        sums[...] = jnp.zeros_like(sums)

    sums[0:1, :] += jnp.sum(upstream * normed, axis=0, keepdims=True)
    sums[1:2, :] += jnp.sum(upstream, axis=0, keepdims=True)
    sums[2:3, :] += jnp.sum(change_low.astype(F32), axis=0, keepdims=True)


def ffn_backward_kernel(
    grad_low, low, active_a, active_b, slope_a, slope_b, expand_a, expand_b, reduce_a, reduce_b, start,
    grad_reduce, grad_expand, grad_bias, running,
):
    step = pl.program_id(0)

    @pl.when(step == 0)
    def _():
        running[...] = start[...]

    def work(active, slope, expand, reduce):
        upstream, rows = grad_low[...], low[...]
        expand, reduce = expand[...].reshape(D, D), reduce[...].reshape(D, D)
        reduced, expanded = [], []
        total = running[...]
        for first in range(0, D, SUB):
            span = slice(first, first + SUB)
            reduced.append(dot(active[:, span], upstream, TN).astype(BF))
            change = (dot(upstream, reduce[span], NT) * slope[:, span].astype(F32)).astype(BF)
            grad_bias[0, :, span] = jnp.sum(change.astype(F32), axis=0, keepdims=True)
            expanded.append(dot(change, rows, TN).astype(BF))
            total = total + dot(change, expand[span], NN)
        running[...] = total
        grad_reduce[...] = jnp.concatenate(reduced, axis=0).reshape(grad_reduce.shape)
        grad_expand[...] = jnp.concatenate(expanded, axis=0).reshape(grad_expand.shape)

    @pl.when(step == 0)
    def _():
        work(active_a, slope_a, expand_a, reduce_a)

    @pl.when(step == 1)
    def _():
        work(active_b, slope_b, expand_b, reduce_b)


def sums_kernel(sums_in, sums_one, grad_bias, sums_two, out):
    out[...] = jnp.zeros_like(out)
    out[BQ : BQ + 1] = sums_in[0, 0:1]
    out[BV : BV + 1] = sums_in[2, 0:1]
    out[BO : BO + 1] = sums_one[2:3]
    out[GA : SA + 1] = sums_one[0:2]
    out[B1 : B1 + FF // D] = grad_bias[...]
    out[B2 : B2 + 1] = sums_two[2:3]
    out[GB : SB + 1] = sums_two[0:2]


def branch_kernel(upstream, unit_rows, factor, context_a, context_b, weight, table, grad, grad_context, grad_weight, sums):
    value = upstream[...]
    normed = unit_rows[...]
    scaled = value * table[GA : GA + 1, :]
    change = factor[...] * (scaled - mean(scaled) - normed * mean(scaled * normed))
    grad[...] = change
    change_low = change.astype(BF)

    @pl.when(pl.program_id(0) == 0)
    def _():
        sums[...] = jnp.zeros_like(sums)
        grad_weight[...] = jnp.zeros_like(grad_weight)

    sums[0:1, :] += jnp.sum(value * normed, axis=0, keepdims=True)
    sums[1:2, :] += jnp.sum(value, axis=0, keepdims=True)
    sums[2:3, :] += jnp.sum(change_low.astype(F32), axis=0, keepdims=True)
    grad_context[...] = dot(weight[...], change_low, NT).astype(BF)
    grad_weight[: D // 2, :] += dot(context_a[...], change_low, TN)
    grad_weight[D // 2 :, :] += dot(context_b[...], change_low, TN)


def attend_backward_kernel(length, packed, grad_context, log_totals, out):
    visible = lax.broadcasted_iota(jnp.int32, (LENGTH, LENGTH), 0) < length[0]
    for head in range(2):
        span = slice(HEAD_DIM * head, HEAD_DIM * (head + 1))
        queries, keys, values = packed[0, span, :], packed[1, span, :], packed[2, span, :]
        upstream = grad_context[span, :]
        scores = dot(keys, queries, TN)
        chances = jnp.where(visible, jnp.exp(scores - log_totals[0, head : head + 1, :]), 0.0)
        grad_chances = dot(values, upstream, TN)
        out[2, span, :] = dot(upstream, chances.astype(BF), NT).astype(BF)
        inner = jnp.sum(chances * grad_chances, axis=0, keepdims=True)
        grad_scores = (chances * (grad_chances - inner)).astype(BF)
        out[1, span, :] = dot(queries, grad_scores, NT).astype(BF)
        out[0, span, :] = (dot(keys, grad_scores, NN) * HEAD_DIM ** (-0.5)).astype(BF)


def in_grads_kernel(unit, owners, grads_a, grads_b, x, grad_out, own, other, sums, held):
    step = power_of_two(unit)
    half = own.shape[1]
    which = pl.program_id(0)

    def place(source, at):
        for side, ref in enumerate((own, other)):
            for slot in range(2 * half):
                start = pl.multiple_of(owners[side * 2 * half + slot] * unit, step)
                ref[slot // half, slot % half, at * unit : (at + 1) * unit, :] = source[pl.ds(start, unit), :].astype(BF)

    for first, grads in ((0, grads_a), (D // 2, grads_b)):
        held[first : first + D // 2, :] = dot(grads[0], x[...], NN)
        sums[0, :, first : first + D // 2] = dot(jnp.ones((8, LENGTH), BF), grads[0], NT)
    for at in range(3):
        pl.when(which == at)(partial(place, held, at))

    @pl.when(which == 0)
    def _():
        place(grad_out, 3)


def input_grad_kernel(grads_a, grads_b, weights, residual, out):
    value = residual[...]
    for which in range(3):
        value = value + dot(grads_a[which], weights[which, : D // 2, :], TN)
        value = value + dot(grads_b[which], weights[which, D // 2 :, :], TN)
    out[...] = value.astype(BF)


def advance(master, velocity, average, gradient, factor, rate):
    clipped = gradient * factor
    velocity_new = MOMENTUM * velocity + clipped
    master_new = master - rate * (clipped + MOMENTUM * velocity_new)
    blend = min(0.999, (1 + STEP) / (10 + STEP))
    return (master_new, velocity_new, blend * average + (1.0 - blend) * master_new)


def body(
    wide,
    narrow,
    layer_input,
    cotangent,
    lengths,
    attention_in,
    attention_out,
    expand_weight,
    reduce_weight,
    vector_params,
    velocity_in,
    velocity_out,
    velocity_expand,
    velocity_reduce,
    velocity_vector,
    average_in,
    average_out,
    average_expand,
    average_reduce,
    average_vector,
):
    cube = Cube(wide, narrow)
    shards = wide * narrow
    share, width, spare = D // shards, FF // shards, NVEC // shards
    unit = share * narrow
    half = wide // 4
    groups = FF // D
    last = len(cube.plane) - 1
    owners = cube.plane_owners()
    held_kind = BF if unit % 16 == 0 else F32

    near = jnp.concatenate(
        [attention_in.astype(BF).transpose(0, 2, 1).reshape(3, 1, share, D), attention_out.astype(BF).reshape(1, 1, share, D)]
    )
    lanes = -(-spare // 128) * 128
    vector = jnp.pad(vector_params.astype(BF).astype(F32), (0, lanes - spare)).reshape(1, lanes)
    hidden = jnp.concatenate(
        [
            expand_weight.astype(BF).T.reshape(groups, 1, share, D),
            reduce_weight.astype(BF).reshape(groups, 1, share, D),
        ]
    )
    for step in range(len(cube.depth)):
        near = jnp.concatenate([near, cube.swap_depth(near, step)], axis=1)
        vector = jnp.concatenate([vector, cube.swap_depth(vector, step)])
        if step == 0:
            hidden_next = cube.swap_depth(hidden, step)
    near = jnp.take(near, cube.depth_slots(), axis=1).reshape(1, 4 * unit, D)
    near = tie(near, hidden_next)
    for step in range(len(cube.depth)):
        if step > 0:
            hidden_next = cube.swap_depth(hidden, step)
        hidden = jnp.concatenate([hidden, hidden_next], axis=1)
    hidden = hidden.reshape(1, 2 * groups * unit, D)
    for step in range(last):
        near = jnp.concatenate([near, cube.swap_plane(near, step)])
    for step in range(last + 1):
        vector = jnp.concatenate([vector, cube.swap_plane(vector, step)])
    vector = jnp.concatenate([vector, cube.swap_core(vector)])
    vector = jnp.take(vector, cube.all_slots(), axis=0)[:, :spare].reshape(NVEC // D, D)
    table = jnp.pad(vector, ((0, 16 - NVEC // D), (0, 0)))
    columns = table.T
    far = cube.swap_plane(near, last)
    near_other = cube.swap_core(near)
    far, columns, hidden = lax.optimization_barrier((far, columns, hidden))
    far_other = cube.swap_core(far)
    attention = [near, far, near_other, far_other]
    bias = jnp.take(table[B1 : B1 + groups].reshape(shards, width), cube.all_owners(), axis=0)
    bias = bias.reshape(wide, narrow, groups, share).transpose(0, 2, 1, 3).reshape(4, 1, D)

    parts_spec = pl.BlockSpec((half, 3 * unit, D), lambda *i: (0, 0, 0))
    packed, weights_in = run(
        partial(project_kernel, unit),
        "project",
        (1,),
        [(owners, SMEM), (layer_input, whole((LENGTH, D)))]
        + [(part, parts_spec) for part in attention]
        + [(columns, whole((D, 16)))],
        [((3, D, LENGTH), BF, whole((3, D, LENGTH))), ((3, D, D), BF, whole((3, D, D)))],
        scratch=[pltpu.VMEM((3, D, D), held_kind)],
        mebibytes=40,
        cost=(2 * 3 * D * D * LENGTH, 12 * D * D, 0),
    )
    for step in range(last):
        hidden_next = cube.swap_plane(hidden, step)
        hidden = jnp.concatenate([hidden, hidden_next])
    log_spec = pl.BlockSpec((1, 2, LENGTH), lambda j: (j, 0, 0))

    def attend(packed, first):
        return run(
            attend_kernel,
            "attend",
            (PAIRS // 2,),
            [(lengths, SMEM), (packed, pl.BlockSpec((3, 2 * HEAD_DIM, LENGTH), lambda j: (0, j + first, 0)))],
            [
                ((LENGTH, D // 2), BF, pl.BlockSpec((LENGTH, 2 * HEAD_DIM), lambda j: (0, j))),
                ((PAIRS // 2, 2, LENGTH), F32, log_spec),
            ],
            cost=(2 * HEADS * LENGTH * LENGTH * HEAD_DIM, 4 * LENGTH * D, HEADS * LENGTH * LENGTH // 2),
        )

    context_a, log_a = attend(packed, 0)
    context_a, hidden = lax.optimization_barrier((context_a, hidden))
    context_b, log_b = attend(tie(packed, context_a), PAIRS // 2)
    hidden_far = cube.swap_plane(hidden, last)
    hidden_other = cube.swap_core(hidden)
    hidden = [hidden, hidden_far, hidden_other, None]
    tile = 256
    row_spec = pl.BlockSpec((tile, D), lambda i: (i, 0))
    half_spec = pl.BlockSpec((tile, D // 2), lambda i: (i, 0))
    one_spec = pl.BlockSpec((tile, 1), lambda i: (i, 0))
    table_spec = whole((16, D))
    out_spec = pl.BlockSpec((half, unit, D), lambda *i: (0, 3, 0))
    weight_out, unit_rows, factor_one, low, running = run(
        partial(join_kernel, unit),
        "join",
        (LENGTH // tile,),
        [(owners, SMEM), (layer_input, row_spec), (context_a, half_spec), (context_b, half_spec)]
        + [(part, out_spec) for part in attention]
        + [(table, table_spec)],
        [
            ((D, D), BF, whole((D, D))),
            ((LENGTH, D), F32, row_spec),
            ((LENGTH, 1), F32, one_spec),
            ((LENGTH, D), BF, row_spec),
            ((LENGTH, D), F32, row_spec),
        ],
        scratch=[pltpu.VMEM((D, D), held_kind)],
        cost=(2 * D * D * LENGTH, 14 * LENGTH * D, 0),
    )


    rows_spec = whole((LENGTH, D))
    hidden_spec = lambda which: pl.BlockSpec((half, groups * unit, D), lambda *i: (0, which, 0))

    def forward(at, running):
        return run(
            ffn_forward_kernel,
            "expand",
            (1,),
            [
                (low, rows_spec),
                (far_memory(hidden[at]), hidden_spec(0)),
                (far_memory(hidden[at]), hidden_spec(1)),
                (bias[at], whole((1, D))),
                (running, rows_spec),
            ],
            [((LENGTH, D), BF, rows_spec), ((LENGTH, D), BF, rows_spec), ((LENGTH, D), F32, rows_spec)],
            cost=(4 * D * D * LENGTH, 4 * D * D + 12 * LENGTH * D, 2 * LENGTH * D),
        )

    active, slope = [None] * 4, [None] * 4
    for at in (0, 2, 1, 3):
        if at == 1:
            hidden[1] = tie(hidden[1], running)
        if at == 3:
            hidden[3] = cube.swap_core(hidden[1])
        active[at], slope[at], running = forward(at, running)
    sum_spec = whole((8, D))
    output, grad_two, grad_low, sums_two = run(
        loss_kernel,
        "loss",
        (LENGTH // tile,),
        [(lengths, SMEM), (running, row_spec), (cotangent, row_spec), (table, table_spec)],
        [
            ((LENGTH, D), BF, row_spec),
            ((LENGTH, D), F32, row_spec),
            ((LENGTH, D), BF, row_spec),
            ((8, D), F32, sum_spec),
        ],
        cost=(40 * LENGTH * D, 14 * LENGTH * D, 0),
    )
    def backward(core, running):
        shape = (2 * half, groups * unit, D)
        grad_spec = pl.BlockSpec((half, groups * unit, D), lambda i: (i, 0, 0))
        first, second = hidden[2 * core], hidden[2 * core + 1]
        return run(
            ffn_backward_kernel,
            "expand_back",
            (2,),
            [
                (grad_low, rows_spec),
                (low, rows_spec),
                (active[2 * core], rows_spec),
                (active[2 * core + 1], rows_spec),
                (slope[2 * core], rows_spec),
                (slope[2 * core + 1], rows_spec),
                (far_memory(first), hidden_spec(0)),
                (far_memory(second), hidden_spec(0)),
                (far_memory(first), hidden_spec(1)),
                (far_memory(second), hidden_spec(1)),
                (running, rows_spec),
            ],
            [
                (pltpu.HBM(shape, BF), None, grad_spec),
                (pltpu.HBM(shape, BF), None, grad_spec),
                ((2, 1, D), F32, pl.BlockSpec((1, 1, D), lambda i: (i, 0, 0))),
                ((LENGTH, D), F32, rows_spec),
            ],
            cost=(16 * D * D * LENGTH, 16 * D * D + 16 * LENGTH * D, 0),
            mebibytes=40,
        )

    cut = lambda part: part.reshape(1, *part.shape)
    reduce_other, expand_other, bias_other, running = backward(1, grad_two)
    reduce_core = cube.swap_core(reduce_other)
    expand_core = cube.swap_core(expand_other)
    reduce_own, expand_own, bias_own, running = backward(0, running)
    reduce_parts = [cut(reduce_own), cut(reduce_core)]
    expand_parts = [cut(expand_own), cut(expand_core)]
    reduce_leaving = cube.leaving(reduce_parts)
    expand_leaving = cube.leaving(expand_parts)
    running = tie(running, reduce_leaving, expand_leaving)
    reduce_parts.append(cube.swap_plane(reduce_leaving, last))
    expand_parts.append(cube.swap_plane(expand_leaving, last))

    def deep(parts):
        return [part.reshape(-1, narrow, share, D) for part in parts]

    def finish_hidden(parts):
        for step in reversed(range(last)):
            parts = parts + [cube.swap_plane(cube.leaving(parts), step)]
        parts = deep(parts)
        for step in reversed(range(len(cube.depth))):
            parts = parts + [cube.swap_depth(cube.leaving(parts), step)]
        return combine(parts, 0, 1, F32).reshape(width, D)

    grad_bias = jnp.stack([bias_own, bias_other]).reshape(wide, groups, narrow, share).transpose(0, 2, 1, 3)
    grad_bias = jnp.take(grad_bias.reshape(shards, width), cube.all_slots(), axis=0).reshape(groups, D)

    grad_one, grad_context, grad_out, sums_one = run(
        branch_kernel,
        "branch_back",
        (LENGTH // tile,),
        [
            (running, row_spec),
            (unit_rows, row_spec),
            (factor_one, one_spec),
            (context_a, half_spec),
            (context_b, half_spec),
            (weight_out, whole((D, D))),
            (table, table_spec),
        ],
        [
            ((LENGTH, D), F32, row_spec),
            ((D, LENGTH), BF, pl.BlockSpec((D, tile), lambda i: (0, i))),
            ((D, D), F32, whole((D, D))),
            ((8, D), F32, sum_spec),
        ],
        cost=(4 * D * D * LENGTH, 8 * D * D + 16 * LENGTH * D, 0),
    )
    def attend_backward(first, grad_context, log_totals):
        return run(
            attend_backward_kernel,
            "attend_back",
            (PAIRS // 2,),
            [
                (lengths, SMEM),
                (packed, pl.BlockSpec((3, 2 * HEAD_DIM, LENGTH), lambda j: (0, j + first, 0))),
                (grad_context, pl.BlockSpec((2 * HEAD_DIM, LENGTH), lambda j: (j + first, 0))),
                (log_totals, log_spec),
            ],
            [((3, D // 2, LENGTH), BF, pl.BlockSpec((3, 2 * HEAD_DIM, LENGTH), lambda j: (0, j, 0)))],
            cost=(5 * HEADS * LENGTH * LENGTH * HEAD_DIM, 7 * LENGTH * D, HEADS * LENGTH * LENGTH // 2),
        )[0]

    grads_a = attend_backward(0, grad_context, log_a)
    grads_b = attend_backward(PAIRS // 2, tie(grad_context, grads_a), log_b)
    grads_b = tie(grads_b, reduce_parts[-1])
    chunk = (2, half, 4 * unit, D)
    own, other, sums_in = run(
        partial(in_grads_kernel, unit),
        "project_back",
        (3,),
        [
            (owners, SMEM),
            (grads_a, pl.BlockSpec((1, D // 2, LENGTH), lambda i: (i, 0, 0))),
            (grads_b, pl.BlockSpec((1, D // 2, LENGTH), lambda i: (i, 0, 0))),
            (layer_input, rows_spec),
            (grad_out, whole((D, D))),
        ],
        [
            (chunk, BF, whole(chunk)),
            (chunk, BF, whole(chunk)),
            ((3, 8, D), F32, pl.BlockSpec((1, 8, D), lambda i: (i, 0, 0))),
        ],
        scratch=[pltpu.VMEM((D, D), F32)],
        mebibytes=32,
        cost=(6 * D * D * LENGTH, 12 * D * D, 0),
    )
    (input_grad,) = run(
        input_grad_kernel,
        "input_back",
        (LENGTH // tile,),
        [
            (grads_a, pl.BlockSpec((3, D // 2, tile), lambda i: (0, 0, i))),
            (grads_b, pl.BlockSpec((3, D // 2, tile), lambda i: (0, 0, i))),
            (weights_in, whole((3, D, D))),
            (grad_one, row_spec),
        ],
        [((LENGTH, D), BF, row_spec)],
        cost=(6 * D * D * LENGTH, 6 * D * D + 12 * LENGTH * D, 0),
    )
    flat = lambda part: part.reshape(1, 2 * half, 4 * unit, D)
    parts = [flat(own), cube.swap_core(flat(other))]
    for step in reversed(range(last + 1)):
        arrived = cube.swap_plane(cube.leaving(parts), step)
        if step == last:
            arrived = tie(arrived, input_grad)
        parts = parts + [arrived]
    owned_reduce = finish_hidden(reduce_parts)
    owned_expand = finish_hidden(expand_parts).T
    parts = total([part[:, 0] for part in parts]).reshape(4, narrow, share, D)
    parts = [jnp.take(parts, cube.depth_owners(), axis=1)]
    for step in reversed(range(len(cube.depth))):
        middle = parts[-1].shape[1] // 2
        going = total([part[:, middle : 2 * middle] for part in parts]).astype(BF)
        parts = parts + [cube.swap_depth(going, step)]
    owned = total([part[:, 0] for part in parts])
    owned_in = owned[:3].transpose(0, 2, 1)
    owned_out = owned[3]
    (grad_vector,) = run(
        sums_kernel,
        "sums",
        (1,),
        [
            (sums_in, whole((3, 8, D))),
            (sums_one, sum_spec),
            (grad_bias, whole((groups, D))),
            (sums_two, sum_spec),
        ],
        [((16, D), F32, whole((16, D)))],
    )
    grad_vector = jnp.pad(grad_vector[: NVEC // D].reshape(shards, spare), ((0, 0), (0, lanes - spare)))
    grad_vector = lax.all_to_all(grad_vector.reshape(shards, 1, lanes), AXES, 0, 0)
    owned_vector = jnp.sum(grad_vector, axis=(0, 1))[:spare]
    squares = (
        jnp.sum(owned_in * owned_in)
        + jnp.sum(owned_out * owned_out)
        + jnp.sum(owned_expand * owned_expand)
    )
    squares = squares + jnp.sum(owned_reduce * owned_reduce) + jnp.sum(owned_vector * owned_vector)
    squares = lax.all_to_all(jnp.broadcast_to(squares.reshape(1, 1, 1), (shards, 1, 128)), AXES, 0, 0)
    grad_norm = jnp.sqrt(jnp.sum(squares[:, 0, 0]))
    factor = 1.0 / jnp.maximum(grad_norm, 1.0)
    new_in, moved_in, mean_in = advance(
        attention_in, velocity_in, average_in, owned_in, factor, RATE_MATRIX
    )
    new_out, moved_out, mean_out = advance(
        attention_out, velocity_out, average_out, owned_out, factor, RATE_PROJECTION
    )
    new_expand, moved_expand, mean_expand = advance(
        expand_weight, velocity_expand, average_expand, owned_expand, factor, RATE_MATRIX
    )
    new_reduce, moved_reduce, mean_reduce = advance(
        reduce_weight, velocity_reduce, average_reduce, owned_reduce, factor, RATE_MATRIX
    )
    new_vector, moved_vector, mean_vector = advance(
        vector_params, velocity_vector, average_vector, owned_vector, factor, RATE_VECTOR
    )
    return (
        output,
        input_grad,
        new_in,
        new_out,
        new_expand,
        new_reduce,
        new_vector,
        moved_in,
        moved_out,
        moved_expand,
        moved_reduce,
        moved_vector,
        mean_in,
        mean_out,
        mean_expand,
        mean_reduce,
        mean_vector,
        grad_norm,
    )


def solution(mesh):
    both = ("wide", "narrow")
    first, second, third = P(both, None), P(None, both), P(None, None, both)
    state = (third, first, second, first, P(both))
    return jax.shard_map(
        partial(body, mesh.shape["wide"], mesh.shape["narrow"]),
        mesh=mesh,
        in_specs=(first, first, P(both)) + state * 3,
        out_specs=(first, first) + state * 3 + (P(),),
        check_vma=False,
    )
```

```python
from functools import partial

import jax
import jax.numpy as jnp
from jax import lax
from jax.experimental import pallas as pl
from jax.experimental.pallas import tpu as pltpu
from jax.sharding import PartitionSpec as P

D = 768
FF = 3072
HEADS = 12
HEAD_DIM = 64
LENGTH = 512
STEP = 10
NVEC = 8 * D + FF
GROUP = 4
STEPS = HEADS // GROUP
SUB = 256

MOMENTUM = 0.9
RATE_MATRIX = 24.0
RATE_PROJECTION = 160.0
RATE_VECTOR = 256.0
EPSILON = 1e-05
MASKED = -1000000000.0

AXES = ("wide", "narrow")
BF = jnp.bfloat16
F32 = jnp.float32
NN = ((1,), (0,))
NT = ((1,), (1,))
TN = ((0,), (0,))

BQ, BV, BO, GA, SA, B1, B2, GB, SB = 0, 1, 2, 3, 4, 5, 9, 10, 11


def dot(left, right, dims):
    return lax.dot_general(left, right, (dims, ((), ())), preferred_element_type=F32)


def mean(rows):
    return jnp.sum(rows, axis=-1, keepdims=True) * (1.0 / D)


def power_of_two(number):
    return number & -number


SMEM = pl.BlockSpec(memory_space=pltpu.SMEM)
ANY = pl.BlockSpec(memory_space=pl.ANY)


def run(kernel, name, grid, ins, outs, scratch=(), cost=(0, 0, 0), mebibytes=24):
    return pl.pallas_call(
        kernel,
        grid=grid,
        in_specs=[spec for _, spec in ins],
        out_specs=[spec for _, _, spec in outs],
        out_shape=[jax.ShapeDtypeStruct(shape, kind) if kind else shape for shape, kind, _ in outs],
        scratch_shapes=scratch,
        compiler_params=pltpu.CompilerParams(
            vmem_limit_bytes=mebibytes * 1024 * 1024, dimension_semantics=("arbitrary",) * len(grid)
        ),
        cost_estimate=pl.CostEstimate(flops=cost[0], bytes_accessed=cost[1], transcendentals=cost[2]),
        name=name,
    )(*[array for array, _ in ins])


def far_memory(array):
    return pltpu.with_memory_space_constraint(array, pltpu.HBM)


def whole(shape):
    return pl.BlockSpec(shape, lambda *i: (0,) * len(shape))


class Cube:
    def __init__(self, wide, narrow):
        self.wide, self.narrow = wide, narrow
        wide_bits, narrow_bits = wide.bit_length() - 1, narrow.bit_length() - 1
        plane = list(range(1, wide_bits))
        half = len(plane) // 2
        swapped = plane[half:] + plane[:half] if len(plane) % 2 == 0 else plane
        depth = list(range(narrow_bits))
        self.depth = list(zip(reversed(depth), depth))
        self.plane = list(zip(plane, swapped))
        self.wide_at = lax.axis_index("wide")
        self.narrow_at = lax.axis_index("narrow")

    def swap_depth(self, array, step):
        place = lambda w, n: w * self.narrow + n
        pairs = [
            (place(w, n), place(w, n ^ (1 << self.depth[step][w & 1])))
            for w in range(self.wide)
            for n in range(self.narrow)
        ]
        return lax.ppermute(array, AXES, pairs)

    def swap_plane(self, array, step):
        pairs = [(i, i ^ (1 << self.plane[step][i & 1])) for i in range(self.wide)]
        return lax.ppermute(array, "wide", pairs)

    def swap_core(self, array):
        return lax.ppermute(array, "wide", [(i, i ^ 1) for i in range(self.wide)])

    def slots(self, apart, bits, core):
        def placed(which):
            slot = jnp.zeros_like(apart)
            for position, pair in enumerate(bits):
                slot = slot | (((apart >> pair[which]) & 1) << position)
            return slot

        return jnp.where(core == 0, placed(0), placed(1))

    def owners(self, slot, bits, core):
        def placed(which):
            apart = jnp.zeros_like(slot)
            for position, pair in enumerate(bits):
                apart = apart | (((slot >> position) & 1) << pair[which])
            return apart

        return jnp.where(core == 0, placed(0), placed(1))

    def plane_owners(self):
        slot = jnp.arange(self.wide, dtype=jnp.int32)
        other = slot >> len(self.plane)
        return (other | self.owners(slot, self.plane, other ^ (self.wide_at & 1))) ^ self.wide_at

    def depth_slots(self):
        place = jnp.arange(self.narrow, dtype=jnp.int32)
        return self.slots(place ^ self.narrow_at, self.depth, self.wide_at & 1)

    def depth_owners(self, other):
        core = (self.wide_at & 1) ^ other
        return self.owners(jnp.arange(self.narrow, dtype=jnp.int32), self.depth, core) ^ self.narrow_at

    def all_owners(self):
        slot = jnp.arange(self.wide * self.narrow, dtype=jnp.int32)
        deep, flat = slot % self.narrow, slot // self.narrow
        other = flat >> len(self.plane)
        core = other ^ (self.wide_at & 1)
        wide_place = (other | self.owners(flat, self.plane, core)) ^ self.wide_at
        return wide_place * self.narrow + (self.owners(deep, self.depth, core) ^ self.narrow_at)

    def all_slots(self):
        place = jnp.arange(self.wide * self.narrow, dtype=jnp.int32)
        flat, deep = (place // self.narrow) ^ self.wide_at, (place % self.narrow) ^ self.narrow_at
        core = (flat ^ self.wide_at) & 1
        slot = ((flat & 1) << len(self.plane)) | self.slots(flat, self.plane, core)
        return slot * self.narrow + self.slots(deep, self.depth, core)


def combine_kernel(*refs):
    value = refs[0][...].astype(F32)
    for ref in refs[1:-1]:
        value = value + ref[...].astype(F32)
    refs[-1][...] = value.astype(refs[-1].dtype)


def combine(parts, axis, first, count):
    block = list(parts[-1].shape)
    block[axis] = count
    out = tuple(block)
    block[0] = 1
    if axis == 1:
        block[1] = 1
    pieces, begin = (count, first) if axis == 1 else (1, 0)
    place = lambda i, start: (i // pieces, start + i % pieces) + tuple(
        first // count if k == axis else 0 for k in range(2, len(block))
    )
    spec = pl.BlockSpec(tuple(block), lambda i: place(i, begin))
    size = 1
    for extent in out:
        size *= extent
    return run(
        combine_kernel,
        "combine",
        (out[0] * pieces,),
        [(far_memory(parts[0]), spec)] + [(part, spec) for part in parts[1:]],
        [(out, BF, pl.BlockSpec(tuple(block), lambda i: (i // pieces, i % pieces) + (0,) * (len(block) - 2)))],
        cost=(size * len(parts), 2 * size * (len(parts) + 1), 0),
        mebibytes=16,
    )[0]


def finish_kernel(count, shards, *refs):
    value = refs[0][...].astype(F32)
    for ref in refs[1:count]:
        value = value + ref[...].astype(F32)
    known, out, squares = refs[count : count + 3]
    out[...] = value
    square = value * value
    square = jnp.sum(square.reshape(-1, D), axis=0, keepdims=True)
    square = jnp.sum(square, axis=1, keepdims=True)
    if known.shape[0] == 1:
        square = square + known[0, :, 0:1]
    else:
        vector = known[0:3]
        for place in range(1, shards):
            vector = vector + known[3 * place : 3 * place + 3]
        refs[-1][...] = vector
        square = square + jnp.sum(jnp.sum(vector * vector, axis=0), axis=1, keepdims=True)
    squares[...] = jnp.broadcast_to(square.reshape(1, 1, 1), squares.shape)


def finish(parts, known, shards):
    shape = parts[-1].shape
    outs = [(shape, F32, whole(shape))]
    if known.shape[0] == 1:
        outs.append(((shards, 1, 128), F32, whole((shards, 1, 128))))
    else:
        outs += [((1, 1, 128), F32, whole((1, 1, 128))), ((3, 1, 128), F32, whole((3, 1, 128)))]
    return run(
        partial(finish_kernel, len(parts), shards),
        "finish",
        (1,),
        [(part, whole(shape)) for part in parts] + [(known, whole(known.shape))],
        outs,
        cost=(D * D, D * D, 0),
        mebibytes=12,
    )


def tie(array, *others):
    return lax.optimization_barrier((array,) + others)[0]


def vectors_kernel(width, slots, owners, shares, table, bias):
    table[...] = jnp.zeros_like(table)
    count = D // width
    for row in range(NVEC // D):
        pieces = []
        for piece in range(row * count, (row + 1) * count):
            lane = 128 * (piece % 3)
            pieces.append(shares[slots[piece // 3], :, lane : lane + 128][:, :width])
        table[row : row + 1, :] = jnp.concatenate(pieces, axis=1)
    count = D // 2 // width
    for place in range(bias.shape[0]):
        pieces = []
        for slot in range(place * count, (place + 1) * count):
            piece = owners[slot] + B1 * (D // width)
            lane = pl.multiple_of(piece % 3 * 128, 128)
            pieces.append(shares[slots[piece // 3], :, pl.ds(lane, 128)][:, :width])
        bias[place] = jnp.concatenate(pieces, axis=1)


def attend_kernel(unit, owners, length, x, *refs):
    parts, (vectors, packed, table, weight, context, log_totals, columns, *held) = refs[:8], refs[8:]
    step = power_of_two(unit)

    @pl.when(pl.program_id(0) == 0)
    def _():
        quarter = parts[0].shape[0]
        for place, ref in enumerate(parts):
            for slot in range(quarter):
                start = pl.multiple_of(owners[place * quarter + slot] * unit, step)
                for which in range(4):
                    piece = ref[slot, which * unit : (which + 1) * unit, :]
                    if held:
                        held[0][which, pl.ds(start, unit), :] = piece.astype(F32)
                    elif which < 3:
                        table[which, pl.ds(start, unit), :] = piece
                    else:
                        weight[pl.ds(start, unit), :] = piece
        if held:
            table[...] = held[0][:3].astype(BF)
            weight[...] = held[0][3].astype(BF)
        columns[...] = vectors[...].T

    rows = x[...]
    block = GROUP * HEAD_DIM
    span = pl.ds(pl.multiple_of(pl.program_id(0) * block, block), block)
    queries = dot(table[0, span, :], rows, NT) + columns[span, BQ : BQ + 1]
    queries = (queries.astype(BF) * HEAD_DIM ** (-0.5)).astype(BF)
    keys = dot(table[1, span, :], rows, NT).astype(BF)
    values = (dot(table[2, span, :], rows, NT) + columns[span, BV : BV + 1]).astype(BF)
    packed[0], packed[1], packed[2] = queries, keys, values
    visible = lax.broadcasted_iota(jnp.int32, (LENGTH, LENGTH), 0) < length[0]
    spans = [slice(HEAD_DIM * head, HEAD_DIM * (head + 1)) for head in range(GROUP)]
    score = lambda head: dot(keys[spans[head]], queries[spans[head]], TN)
    following, done = score(0), []
    for head in range(GROUP):
        scores = jnp.where(visible, following, MASKED)
        if head + 1 < GROUP:
            following = score(head + 1)
        largest = jnp.max(scores, axis=0, keepdims=True)
        powers = jnp.exp(scores - largest)
        totals = jnp.sum(powers, axis=0, keepdims=True)
        done.append(dot(values[spans[head]], powers.astype(BF), NN) * (1.0 / totals))
        log_totals[0, head : head + 1, :] = largest + jnp.log(totals)
    context[...] = jnp.concatenate(done, axis=0).T.astype(BF)


def join_kernel(x, context, weight, table, unit_rows, factor, low, base):
    branch = dot(context[...], weight[...], NN) + table[BO : BO + 1, :]
    rows = x[...].astype(F32) + branch
    center = rows - mean(rows)
    spread = lax.rsqrt(mean(center * center) + EPSILON)
    normed = center * spread
    unit_rows[...] = normed
    factor[...] = spread
    shifted = normed * table[GA : GA + 1, :] + table[SA : SA + 1, :]
    low[...] = shifted.astype(BF)
    base[...] = shifted + table[B2 : B2 + 1, :]


def gelu_pair(value):
    power = jnp.exp(value * value * -0.5)
    part = 1.0 / (1.0 + jnp.abs(value) * (0.3275911 * 0.5**0.5))
    tail = 0.5 * 1.061405429
    for factor in (-1.453152027, 1.421413741, -0.284496736, 0.254829592):
        tail = tail * part + 0.5 * factor
    tail = tail * part * power
    chance = jnp.where(value < 0.0, tail, 1.0 - tail)
    return value * chance, chance + value * power * (2.0 * jnp.pi) ** -0.5


def joined(first, second):
    return jnp.concatenate([first[...].reshape(D // 2, D), second[...].reshape(D // 2, D)], axis=0)


def ffn_forward_kernel(places, low, expand_a, expand_b, reduce_a, reduce_b, bias, start, active, slope, running):
    rows = low[...]
    expand, reduce = joined(expand_a, expand_b), joined(reduce_a, reduce_b)
    shift = jnp.concatenate([bias[places[0]], bias[places[1]]], axis=1)
    total = start[...]
    for first in range(0, D, SUB):
        span = slice(first, first + SUB)
        value, change = gelu_pair(dot(rows, expand[span], NT) + shift[:, span])
        value = value.astype(BF)
        active[:, span] = value
        slope[:, span] = change.astype(BF)
        total = total + dot(value, reduce[span], NN)
    running[...] = total


def loss_kernel(length, rows, cotangent, table, output, grad, grad_low, sums):
    tile = rows.shape[0]
    value = rows[...]
    center = value - mean(value)
    factor = lax.rsqrt(mean(center * center) + EPSILON)
    normed = center * factor
    gain = table[GB : GB + 1, :]
    output[...] = (normed * gain + table[SB : SB + 1, :]).astype(BF)
    place = pl.program_id(0) * tile + lax.broadcasted_iota(jnp.int32, (tile, 1), 0)
    upstream = jnp.where(place < length[0], cotangent[...].astype(F32), 0.0)
    scaled = upstream * gain
    change = factor * (scaled - mean(scaled) - normed * mean(scaled * normed))
    grad[...] = change
    change_low = change.astype(BF)
    grad_low[...] = change_low

    @pl.when(pl.program_id(0) == 0)
    def _():
        sums[...] = jnp.zeros_like(sums)

    sums[0:1, :] += jnp.sum(upstream * normed, axis=0, keepdims=True)
    sums[1:2, :] += jnp.sum(upstream, axis=0, keepdims=True)
    sums[2:3, :] += jnp.sum(change_low.astype(F32), axis=0, keepdims=True)


def ffn_backward_kernel(
    grad_low, low, active_a, active_b, slope_a, slope_b, expand_a, expand_b, reduce_a, reduce_b, start,
    grads, grad_bias, running,
):
    upstream, rows = grad_low[...], low[...]
    expand, reduce = joined(expand_a, expand_b), joined(reduce_a, reduce_b)
    active = jnp.concatenate([active_a[...], active_b[...]], axis=1)
    slope = jnp.concatenate([slope_a[...], slope_b[...]], axis=1)
    reduced, expanded = [], []
    total = start[...]
    for first in range(0, D, SUB):
        span = slice(first, first + SUB)
        reduced.append(dot(active[:, span], upstream, TN).astype(BF))
        change = (dot(upstream, reduce[span], NT) * slope[:, span].astype(F32)).astype(BF)
        grad_bias[:, span] = jnp.sum(change.astype(F32), axis=0, keepdims=True)
        expanded.append(dot(change, rows, TN).astype(BF))
        total = total + dot(change, expand[span], NN)
    running[...] = total
    grads[0] = jnp.concatenate(reduced, axis=0).reshape(grads.shape[1:])
    grads[1] = jnp.concatenate(expanded, axis=0).reshape(grads.shape[1:])


def sums_kernel(width, owners, sums_in, sums_one, sums_two, *refs):
    biases, out = refs[:4], refs[4]
    out[...] = jnp.zeros_like(out)
    count = D // width
    rows = (
        (BQ, sums_in[0, 0:1]),
        (BV, sums_in[2, 0:1]),
        (BO, sums_one[2:3]),
        (GA, sums_one[0:1]),
        (SA, sums_one[1:2]),
        (B2, sums_two[2:3]),
        (GB, sums_two[0:1]),
        (SB, sums_two[1:2]),
    )
    for row, value in rows:
        for piece in range(count):
            out[row * count + piece, :, :width] = value[:, piece * width : (piece + 1) * width]
    for place, ref in enumerate(biases):
        value = ref[...]
        for piece in range(count):
            into = owners[place * count + piece] + B1 * count
            out[into, :, :width] = value[:, piece * width : (piece + 1) * width]


def branch_kernel(upstream, unit_rows, factor, context, weight, table, grad, grad_context, grad_weight, sums):
    value = upstream[...]
    normed = unit_rows[...]
    scaled = value * table[GA : GA + 1, :]
    change = factor[...] * (scaled - mean(scaled) - normed * mean(scaled * normed))
    grad[...] = change
    change_low = change.astype(BF)

    @pl.when(pl.program_id(0) == 0)
    def _():
        sums[...] = jnp.zeros_like(sums)
        grad_weight[...] = jnp.zeros_like(grad_weight)

    sums[0:1, :] += jnp.sum(value * normed, axis=0, keepdims=True)
    sums[1:2, :] += jnp.sum(value, axis=0, keepdims=True)
    sums[2:3, :] += jnp.sum(change_low.astype(F32), axis=0, keepdims=True)
    grad_context[...] = dot(weight[...], change_low, NT).astype(BF)
    grad_weight[...] += dot(context[...], change_low, TN)


def attend_backward_kernel(length, packed, grad_context, log_totals, out):
    visible = lax.broadcasted_iota(jnp.int32, (LENGTH, LENGTH), 0) < length[0]
    spans = [slice(HEAD_DIM * head, HEAD_DIM * (head + 1)) for head in range(GROUP)]

    def score(head):
        span = spans[head]
        return dot(packed[1, span, :], packed[0, span, :], TN), dot(packed[2, span, :], grad_context[span, :], TN)

    following = score(0)
    for head in range(GROUP):
        span = spans[head]
        scores, grad_chances = following
        if head + 1 < GROUP:
            following = score(head + 1)
        chances = jnp.where(visible, jnp.exp(scores - log_totals[0, head : head + 1, :]), 0.0)
        out[2, span, :] = dot(grad_context[span, :], chances.astype(BF), NT).astype(BF)
        inner = jnp.sum(chances * grad_chances, axis=0, keepdims=True)
        grad_scores = (chances * (grad_chances - inner)).astype(BF)
        out[1, span, :] = dot(packed[0, span, :], grad_scores, NT).astype(BF)
        out[0, span, :] = (dot(packed[1, span, :], grad_scores, NN) * HEAD_DIM ** (-0.5)).astype(BF)


def in_grads_kernel(piece, owners, grads, x, grad_out, *refs):
    outs, (sums, held) = refs[:4], refs[4:]
    step = power_of_two(piece)
    which = pl.program_id(0)
    slots, rows = outs[0].shape[1], outs[0].shape[2] // 4

    def place(source, at):
        for side, ref in enumerate(outs):
            for slot in range(slots):
                for first in range(0, rows, piece):
                    index = ((side * slots + slot) * rows + first) // piece
                    start = pl.multiple_of(owners[index] * piece, step)
                    into = slice(at * rows + first, at * rows + first + piece)
                    ref[0, slot, into, :] = source[pl.ds(start, piece), :].astype(BF)

    held[...] = dot(grads[0], x[...], NN)
    sums[0] = dot(jnp.ones((8, LENGTH), BF), grads[0], NT)
    for at in range(3):
        pl.when(which == at)(partial(place, held, at))

    @pl.when(which == 0)
    def _():
        place(grad_out, 3)


def input_grad_kernel(grads, weights, residual, out):
    value = residual[...]
    for which in range(3):
        value = value + dot(grads[which], weights[which], TN)
    out[...] = value.astype(BF)


RATES = (RATE_MATRIX, RATE_PROJECTION, RATE_MATRIX, RATE_MATRIX, RATE_VECTOR)


def update_kernel(squares, near, hidden, vector, *refs):
    states, outs = refs[:15], refs[15:]
    value = squares[...]
    norm = jnp.sqrt(jnp.sum(value, axis=0)[:, 0:1])
    factor = 1.0 / jnp.maximum(norm, 1.0)
    outs[15][...] = norm
    blend = min(0.999, (1 + STEP) / (10 + STEP))
    gradients = (near[:3], near[3], hidden[1], hidden[0], vector[...][:, :, : states[4].shape[2]])
    for at, (gradient, rate) in enumerate(zip(gradients, RATES)):
        clipped = gradient * factor
        moved = MOMENTUM * states[5 + at][...] + clipped
        weight = states[at][...] - rate * (clipped + MOMENTUM * moved)
        outs[at][...] = weight
        outs[5 + at][...] = moved
        outs[10 + at][...] = blend * states[10 + at][...] + (1.0 - blend) * weight


def body(
    wide,
    narrow,
    layer_input,
    cotangent,
    lengths,
    attention_in,
    attention_out,
    expand_weight,
    reduce_weight,
    vector_params,
    velocity_in,
    velocity_out,
    velocity_expand,
    velocity_reduce,
    velocity_vector,
    average_in,
    average_out,
    average_expand,
    average_reduce,
    average_vector,
):
    cube = Cube(wide, narrow)
    shards = wide * narrow
    share, width, spare = D // shards, FF // shards, NVEC // shards
    unit = share * narrow
    half = wide // 4
    groups = FF // D
    last = len(cube.plane) - 1
    owners = cube.plane_owners()
    held_kind = BF if unit % 16 == 0 else F32

    quarter = half // 2
    near = jnp.concatenate(
        [attention_in.astype(BF).transpose(0, 2, 1).reshape(3, 1, share, D), attention_out.astype(BF).reshape(1, 1, share, D)]
    )
    vector = jnp.pad(vector_params.astype(BF).astype(F32).reshape(1, 1, 3, width), ((0, 0),) * 3 + ((0, 128 - width),))
    vector = vector.reshape(1, 1, 3 * 128)
    hidden = jnp.stack([expand_weight.astype(BF).T, reduce_weight.astype(BF)]).reshape(2, 1, width, D)
    for step in range(len(cube.depth)):
        near = jnp.concatenate([near, cube.swap_depth(near, step)], axis=1)
        vector = jnp.concatenate([vector, cube.swap_depth(vector, step)])
        if step == 0:
            hidden = jnp.concatenate([hidden, cube.swap_depth(hidden, step)], axis=1)
    near = jnp.take(near, cube.depth_slots(), axis=1).reshape(1, 4 * unit, D)
    near = tie(near, vector)
    vector = tie(vector, hidden)

    def plane_quarter(slots):
        for step in range(last - 1):
            slots = jnp.concatenate([slots, cube.swap_plane(slots, step)])
        return slots

    near = plane_quarter(near)
    near_next = cube.swap_plane(near, last - 1)
    near_far = cube.swap_plane(tie(near, hidden), last)
    near_next, near_far, hidden = lax.optimization_barrier((near_next, near_far, hidden))
    for step in range(1, len(cube.depth)):
        hidden = jnp.concatenate([hidden, cube.swap_depth(hidden, step)], axis=1)
    hidden = hidden.reshape(1, 2 * groups * unit, D)
    for step in range(last + 1):
        vector = jnp.concatenate([vector, cube.swap_plane(vector, step)])
    vector = jnp.concatenate([vector, cube.swap_core(vector)])
    all_owners = cube.all_owners()
    table, bias = run(
        partial(vectors_kernel, width),
        "vectors",
        (1,),
        [(cube.all_slots(), SMEM), (all_owners, SMEM), (vector, whole(vector.shape))],
        [((16, D), F32, whole((16, D))), ((8, 1, D // 2), F32, whole((8, 1, D // 2)))],
        mebibytes=8,
    )
    near = [near, near_next, near_far, cube.swap_plane(near_next, last)]
    near[3], table, bias, hidden = lax.optimization_barrier((near[3], table, bias, hidden))
    attention = near + [cube.swap_core(part) for part in near]

    hidden = plane_quarter(hidden)
    hidden_next = cube.swap_plane(hidden, last - 1)
    hidden_far = cube.swap_plane(hidden, last)
    pair_spec = pl.BlockSpec((3, GROUP * HEAD_DIM, LENGTH), lambda j: (0, j, 0))
    log_spec = pl.BlockSpec((1, GROUP, LENGTH), lambda j: (j, 0, 0))
    packed, weights_in, weight_out, context, log_totals = run(
        partial(attend_kernel, unit),
        "attend",
        (STEPS,),
        [(owners, SMEM), (lengths, SMEM), (layer_input, whole((LENGTH, D)))]
        + [(part, whole((quarter, 4 * unit, D))) for part in attention]
        + [(table, whole((16, D)))],
        [
            (pltpu.HBM((3, D, LENGTH), BF), None, pair_spec),
            (pltpu.HBM((3, D, D), BF), None, whole((3, D, D))),
            (pltpu.HBM((D, D), BF), None, whole((D, D))),
            ((LENGTH, D), BF, pl.BlockSpec((LENGTH, GROUP * HEAD_DIM), lambda j: (0, j))),
            ((STEPS, GROUP, LENGTH), F32, log_spec),
        ],
        scratch=[pltpu.VMEM((D, 16), F32)] + ([] if unit % 16 == 0 else [pltpu.VMEM((4, D, D), F32)]),
        cost=(10 * D * D * LENGTH, 24 * D * D, HEADS * LENGTH * LENGTH),
        mebibytes=40,
    )
    context, hidden_next = lax.optimization_barrier((context, hidden_next))
    hidden = [hidden, hidden_next, hidden_far, cube.swap_plane(hidden_next, last)]
    hidden += [cube.swap_core(hidden[0]), cube.swap_core(hidden[1])]
    tile = 256
    row_spec = pl.BlockSpec((tile, D), lambda i: (i, 0))
    one_spec = pl.BlockSpec((tile, 1), lambda i: (i, 0))
    table_spec = whole((16, D))
    unit_rows, factor_one, low, running = run(
        join_kernel,
        "join",
        (LENGTH // tile,),
        [
            (layer_input, row_spec),
            (context, row_spec),
            (weight_out, whole((D, D))),
            (table, table_spec),
        ],
        [
            ((LENGTH, D), F32, row_spec),
            ((LENGTH, 1), F32, one_spec),
            ((LENGTH, D), BF, row_spec),
            ((LENGTH, D), F32, row_spec),
        ],
        cost=(2 * D * D * LENGTH, 14 * LENGTH * D, 0),
        mebibytes=16,
    )

    rows_spec = pl.BlockSpec(memory_space=pltpu.VMEM)
    hidden_spec = lambda which: pl.BlockSpec((quarter, groups * unit, D), lambda *i: (0, which, 0))

    def forward(first, second, running):
        return run(
            partial(ffn_forward_kernel, (first, second)),
            "expand",
            (1,),
            [
                (low, rows_spec),
                (hidden[first], hidden_spec(0)),
                (hidden[second], hidden_spec(0)),
                (hidden[first], hidden_spec(1)),
                (hidden[second], hidden_spec(1)),
                (bias, whole((8, 1, D // 2))),
                (running, rows_spec),
            ],
            [
                (pltpu.HBM((LENGTH, D), BF), None, whole((LENGTH, D))),
                (pltpu.HBM((LENGTH, D), BF), None, whole((LENGTH, D))),
                ((LENGTH, D), F32, rows_spec),
            ],
            cost=(4 * D * D * LENGTH, 4 * D * D + 12 * LENGTH * D, 2 * LENGTH * D),
        )

    stored = [None] * 8
    for first, second in ((0, 1), (4, 5), (2, 6), (3, 7)):
        if first == 4:
            hidden[2] = tie(hidden[2], running)
            hidden += [cube.swap_core(hidden[2])]
        if first == 3:
            hidden[3] = tie(hidden[3], running)
            hidden += [cube.swap_core(hidden[3])]
        active, slope, running = forward(first, second, running)
        stored[first] = (active, slope, 0)
        stored[second] = (active, slope, 1)
    sum_spec = whole((8, D))
    output, grad_two, grad_low, sums_two = run(
        loss_kernel,
        "loss",
        (LENGTH // tile,),
        [(lengths, SMEM), (running, row_spec), (cotangent, row_spec), (table, table_spec)],
        [
            ((LENGTH, D), BF, row_spec),
            ((LENGTH, D), F32, row_spec),
            ((LENGTH, D), BF, row_spec),
            (pltpu.HBM((8, D), F32), None, sum_spec),
        ],
        cost=(40 * LENGTH * D, 14 * LENGTH * D, 0),
    )
    def backward(first, running):
        column = lambda place: pl.BlockSpec((LENGTH, D // 2), lambda *i: (0, stored[place][2]))
        shape = (2, half, groups * unit, D)
        return run(
            ffn_backward_kernel,
            "expand_back",
            (1,),
            [(grad_low, rows_spec), (low, rows_spec)]
            + [(stored[place][0], column(place)) for place in (first, first + 1)]
            + [(stored[place][1], column(place)) for place in (first, first + 1)]
            + [(hidden[place], hidden_spec(0)) for place in (first, first + 1)]
            + [(hidden[place], hidden_spec(1)) for place in (first, first + 1)]
            + [(running, rows_spec)],
            [
                (pltpu.HBM(shape, BF), None, whole(shape)),
                ((1, D), F32, whole((1, D))),
                ((LENGTH, D), F32, rows_spec),
            ],
            cost=(8 * D * D * LENGTH, 8 * D * D + 12 * LENGTH * D, 0),
        )

    other_far, bias_6, running = backward(6, grad_two)
    other_far = cube.swap_core(other_far)
    own_far, bias_2, running = backward(2, running)
    leaving = combine([own_far, other_far], 1, 0, half)
    arrived_far = cube.swap_plane(leaving, last)
    other_near, bias_4, running = backward(4, tie(running, leaving))
    other_near = cube.swap_core(other_near)
    own_near, bias_0, running = backward(0, running)
    hidden_parts = [own_near, tie(other_near, running), arrived_far]

    grad_one, grad_context, grad_out, sums_one = run(
        branch_kernel,
        "branch_back",
        (LENGTH // tile,),
        [
            (running, row_spec),
            (unit_rows, row_spec),
            (factor_one, one_spec),
            (context, row_spec),
            (weight_out, whole((D, D))),
            (table, table_spec),
        ],
        [
            (pltpu.HBM((LENGTH, D), F32), None, row_spec),
            ((D, LENGTH), BF, pl.BlockSpec((D, tile), lambda i: (0, i))),
            ((D, D), F32, whole((D, D))),
            (pltpu.HBM((8, D), F32), None, sum_spec),
        ],
        cost=(4 * D * D * LENGTH, 8 * D * D + 16 * LENGTH * D, 0),
    )
    (grads,) = run(
        attend_backward_kernel,
        "attend_back",
        (STEPS,),
        [
            (lengths, SMEM),
            (packed, pair_spec),
            (grad_context, pl.BlockSpec((GROUP * HEAD_DIM, LENGTH), lambda j: (j, 0))),
            (log_totals, log_spec),
        ],
        [((3, D, LENGTH), BF, pair_spec)],
        cost=(10 * HEADS * LENGTH * LENGTH * HEAD_DIM, 14 * LENGTH * D, HEADS * LENGTH * LENGTH),
    )
    grads, arrived = lax.optimization_barrier((grads, hidden_parts[2]))
    hidden_parts[2] = arrived

    def send(parts, axis):
        middle = parts[-1].shape[axis] // 2
        return combine(parts, axis, middle, middle)

    leaving = send(hidden_parts, 1)
    grads = tie(grads, leaving)
    hidden_parts.append(cube.swap_plane(leaving, last - 1))
    chunk = (1, half, 4 * unit, D)
    aligned = share % 8 == 0
    *chunks, sums_in = run(
        partial(in_grads_kernel, share if aligned else unit),
        "project_back",
        (3,),
        [
            (all_owners if aligned else owners, SMEM),
            (grads, pl.BlockSpec((1, D, LENGTH), lambda i: (i, 0, 0))),
            (layer_input, whole((LENGTH, D))),
            (grad_out, whole((D, D))),
        ],
        [(pltpu.HBM(chunk, BF), None, whole(chunk))] * 4
        + [((3, 8, D), F32, pl.BlockSpec((1, 8, D), lambda i: (i, 0, 0)))],
        scratch=[pltpu.VMEM((D, D), F32)],
        cost=(6 * D * D * LENGTH, 12 * D * D, 0),
        mebibytes=32,
    )
    if not aligned:
        for place, part in enumerate(chunks):
            order = cube.depth_owners(place // 2)
            part = jnp.take(part.reshape(half, 4, narrow, share, D), order, axis=2)
            chunks[place] = part.reshape(chunk)
    own_near, own_far, other_near, other_far = chunks
    (input_grad,) = run(
        input_grad_kernel,
        "input_back",
        (LENGTH // tile,),
        [
            (grads, pl.BlockSpec((3, D, tile), lambda i: (0, 0, i))),
            (far_memory(weights_in), whole((3, D, D))),
            (far_memory(grad_one), row_spec),
        ],
        [((LENGTH, D), BF, row_spec)],
        cost=(6 * D * D * LENGTH, 6 * D * D + 12 * LENGTH * D, 0),
    )
    other_far, other_near = cube.swap_core(other_far), cube.swap_core(other_near)
    (grad_vector,) = run(
        partial(sums_kernel, width),
        "sums",
        (1,),
        [
            (all_owners, SMEM),
            (sums_in, whole((3, 8, D))),
            (sums_one, sum_spec),
            (sums_two, sum_spec),
        ]
        + [(part, whole((1, D))) for part in (bias_0, bias_2, bias_4, bias_6)],
        [((3 * shards, 1, 128), F32, whole((3 * shards, 1, 128)))],
        mebibytes=8,
    )
    grad_vector = lax.all_to_all(grad_vector, AXES, 0, 0, tiled=True)
    if len(cube.plane) > 1:
        own_far, hidden_parts[-1] = lax.optimization_barrier((own_far, hidden_parts[-1]))
    leaving = combine([own_far, other_far], 1, 0, half)
    arrived = cube.swap_plane(leaving, last)
    arrived, input_grad, grad_vector = lax.optimization_barrier((arrived, input_grad, grad_vector))
    parts = [own_near, other_near, arrived]
    for step in reversed(range(last)):
        parts.append(cube.swap_plane(send(parts, 1), step))
    for step in reversed(range(last - 1)):
        hidden_parts.append(cube.swap_plane(send(hidden_parts, 1), step))
    parts = [part.reshape(1, -1, 4, narrow, share, D) for part in parts]
    hidden_parts = [part.reshape(2, -1, narrow, width, D) for part in hidden_parts]
    for step in reversed(range(len(cube.depth))):
        parts.append(cube.swap_depth(send(parts, 3), step))
        hidden_parts.append(cube.swap_depth(send(hidden_parts, 2), step))
    owned_hidden, squares, owned_vector = finish(hidden_parts, grad_vector, shards)
    owned_near, squares = finish(parts, squares, shards)
    squares = lax.all_to_all(squares, AXES, 0, 0)

    turn = lambda array: array.transpose(*range(array.ndim - 2), -1, -2)
    states = []
    for first, second, third, fourth, fifth in (
        (attention_in, attention_out, expand_weight, reduce_weight, vector_params),
        (velocity_in, velocity_out, velocity_expand, velocity_reduce, velocity_vector),
        (average_in, average_out, average_expand, average_reduce, average_vector),
    ):
        states += [turn(first), second, turn(third), fourth, fifth.reshape(3, 1, width)]
    gradients = [
        owned_near.reshape(4, share, D),
        owned_hidden.reshape(2, width, D),
        owned_vector,
    ]
    *states, grad_norm = run(
        update_kernel,
        "update",
        (1,),
        [(squares, whole(squares.shape))]
        + [(far_memory(array), whole(array.shape)) for array in gradients]
        + [(far_memory(array), whole(array.shape)) for array in states],
        [(array.shape, F32, whole(array.shape)) for array in states] + [((1, 1), F32, whole((1, 1)))],
        cost=(FF * D, 28 * (share * 4 + width * 2) * D, 0),
    )
    for first in (0, 5, 10):
        states[first] = turn(states[first])
        states[first + 2] = turn(states[first + 2])
        states[first + 4] = states[first + 4].reshape(spare)
    return (output, input_grad, *states, grad_norm.reshape(()))


def solution(mesh):
    both = ("wide", "narrow")
    first, second, third = P(both, None), P(None, both), P(None, None, both)
    state = (third, first, second, first, P(both))
    return jax.shard_map(
        partial(body, mesh.shape["wide"], mesh.shape["narrow"]),
        mesh=mesh,
        in_specs=(first, first, P(both)) + state * 3,
        out_specs=(first, first) + state * 3 + (P(),),
        check_vma=False,
    )
```

```python
from functools import partial

import jax
import jax.numpy as jnp
from jax import lax
from jax.experimental import pallas as pl
from jax.experimental.pallas import tpu as pltpu
from jax.sharding import PartitionSpec as P

D = 768
FF = 3072
HEADS = 12
HEAD_DIM = 64
LENGTH = 512
STEP = 10
NVEC = 8 * D + FF
GROUP = 4
STEPS = HEADS // GROUP
SUB = 256

MOMENTUM = 0.9
RATE_MATRIX = 24.0
RATE_PROJECTION = 160.0
RATE_VECTOR = 256.0
EPSILON = 1e-05
MASKED = -1000000000.0

AXES = ("wide", "narrow")
BF = jnp.bfloat16
F32 = jnp.float32
NN = ((1,), (0,))
NT = ((1,), (1,))
TN = ((0,), (0,))

BQ, BV, BO, GA, SA, B1, B2, GB, SB = 0, 1, 2, 3, 4, 5, 9, 10, 11


def dot(left, right, dims):
    return lax.dot_general(left, right, (dims, ((), ())), preferred_element_type=F32)


def mean(rows):
    return jnp.sum(rows, axis=-1, keepdims=True) * (1.0 / D)


def power_of_two(number):
    return number & -number


SMEM = pl.BlockSpec(memory_space=pltpu.SMEM)
ANY = pl.BlockSpec(memory_space=pl.ANY)


def run(kernel, name, grid, ins, outs, scratch=(), cost=(0, 0, 0), mebibytes=24):
    weight = 100 if name in ('reduce_back', 'expand_back', 'branch_back', 'attend_back', 'project_back') else 1
    return pl.pallas_call(
        kernel,
        grid=grid,
        in_specs=[spec for _, spec in ins],
        out_specs=[spec for _, _, spec in outs],
        out_shape=[jax.ShapeDtypeStruct(shape, kind) if kind else shape for shape, kind, _ in outs],
        scratch_shapes=scratch,
        compiler_params=pltpu.CompilerParams(
            vmem_limit_bytes=mebibytes * 1024 * 1024, dimension_semantics=("arbitrary",) * len(grid)
        ),
        cost_estimate=pl.CostEstimate(flops=weight * cost[0], bytes_accessed=weight * cost[1], transcendentals=cost[2]),
        name=name,
    )(*[array for array, _ in ins])


def far_memory(array):
    return pltpu.with_memory_space_constraint(array, pltpu.HBM)


def whole(shape):
    return pl.BlockSpec(shape, lambda *i: (0,) * len(shape))


class Cube:
    def __init__(self, wide, narrow):
        self.wide, self.narrow = wide, narrow
        wide_bits, narrow_bits = wide.bit_length() - 1, narrow.bit_length() - 1
        plane = list(range(1, wide_bits))
        half = len(plane) // 2
        swapped = plane[half:] + plane[:half] if len(plane) % 2 == 0 else plane
        depth = list(range(narrow_bits))
        self.depth = list(zip(reversed(depth), depth))
        self.plane = list(zip(plane, swapped))
        self.wide_at = lax.axis_index("wide")
        self.narrow_at = lax.axis_index("narrow")

    def swap_depth(self, array, step):
        place = lambda w, n: w * self.narrow + n
        pairs = [
            (place(w, n), place(w, n ^ (1 << self.depth[step][w & 1])))
            for w in range(self.wide)
            for n in range(self.narrow)
        ]
        return lax.ppermute(array, AXES, pairs)

    def swap_plane(self, array, step):
        pairs = [(i, i ^ (1 << self.plane[step][i & 1])) for i in range(self.wide)]
        return lax.ppermute(array, "wide", pairs)

    def swap_core(self, array):
        return lax.ppermute(array, "wide", [(i, i ^ 1) for i in range(self.wide)])

    def slots(self, apart, bits, core):
        def placed(which):
            slot = jnp.zeros_like(apart)
            for position, pair in enumerate(bits):
                slot = slot | (((apart >> pair[which]) & 1) << position)
            return slot

        return jnp.where(core == 0, placed(0), placed(1))

    def owners(self, slot, bits, core):
        def placed(which):
            apart = jnp.zeros_like(slot)
            for position, pair in enumerate(bits):
                apart = apart | (((slot >> position) & 1) << pair[which])
            return apart

        return jnp.where(core == 0, placed(0), placed(1))

    def plane_owners(self):
        slot = jnp.arange(self.wide, dtype=jnp.int32)
        other = slot >> len(self.plane)
        return (other | self.owners(slot, self.plane, other ^ (self.wide_at & 1))) ^ self.wide_at

    def depth_slots(self, other):
        place = jnp.arange(self.narrow, dtype=jnp.int32)
        return self.slots(place ^ self.narrow_at, self.depth, (self.wide_at & 1) ^ other)

    def depth_owners(self, other):
        core = (self.wide_at & 1) ^ other
        return self.owners(jnp.arange(self.narrow, dtype=jnp.int32), self.depth, core) ^ self.narrow_at

    def all_owners(self, slot):
        deep, flat = slot % self.narrow, slot // self.narrow
        other = flat >> len(self.plane)
        core = other ^ (self.wide_at & 1)
        wide_place = (other | self.owners(flat, self.plane, core)) ^ self.wide_at
        return wide_place * self.narrow + (self.owners(deep, self.depth, core) ^ self.narrow_at)

    def all_slots(self):
        place = jnp.arange(self.wide * self.narrow, dtype=jnp.int32)
        flat, deep = (place // self.narrow) ^ self.wide_at, (place % self.narrow) ^ self.narrow_at
        core = (flat ^ self.wide_at) & 1
        slot = ((flat & 1) << len(self.plane)) | self.slots(flat, self.plane, core)
        return slot * self.narrow + self.slots(deep, self.depth, core)


def summed(refs, kinds, second):
    refs, value = iter(refs), None
    for pair in kinds:
        part = next(refs)[...].astype(F32)
        if pair:
            part = jnp.where(second, next(refs)[...].astype(F32), part)
        value = part if value is None else value + part
    return value


def flat(parts):
    return [array for part in parts for array in (part if isinstance(part, tuple) else (part,))]


def combine_kernel(kinds, pieces, *refs):
    refs[-1][...] = summed(refs[:-1], kinds, pl.program_id(0) >= pieces).astype(BF)


def combine(parts, axis, first, count, deeps=None):
    pair = isinstance(parts[-1], tuple)
    block = list(parts[-1][0].shape if pair else parts[-1].shape)
    block[axis] = count
    out = tuple([2] + block[1:]) if pair else tuple(block)
    block[0] = 1
    if axis == 1:
        block[1] = 1
    pieces, begin = (count, first) if axis == 1 else (1, 0)
    place = lambda i, start, group, at=0: (group, start + i % pieces) + tuple(
        first // count if k == axis else at if k == 3 else 0 for k in range(2, len(block))
    )
    spec = pl.BlockSpec(tuple(block), lambda i: place(i, begin, i // pieces))
    pair_spec = pl.BlockSpec(tuple(block), lambda i: place(i, begin, 0))
    kinds = [isinstance(part, tuple) for part in parts]
    arrays = [far_memory(parts[0])] + flat(parts[1:])
    specs = [each for kind in kinds for each in ([pair_spec] * 2 if kind else [spec])]
    if deeps:
        specs = [pl.BlockSpec(tuple(block), lambda i, at=at: place(i, begin, i // pieces, at)) for at in deeps]
    return run(
        partial(combine_kernel, kinds, pieces),
        "combine",
        (out[0] * pieces,),
        list(zip(arrays, specs)),
        [(out, BF, pl.BlockSpec(tuple(block), lambda i: (i // pieces, i % pieces) + (0,) * (len(block) - 2)))],
        cost=(D * D, 4 * D * D, 0),
        mebibytes=16,
    )[0]


def finish_kernel(kinds, shards, *refs):
    count, value = len(kinds) + sum(kinds), None
    arrays = iter(refs)
    for pair in kinds:
        part = next(arrays)[...].astype(F32)
        if pair:
            part = jnp.concatenate([part, next(arrays)[...].astype(F32)], axis=0)
        value = part if value is None else value + part
    known, out, squares = refs[count : count + 3]
    out[...] = value
    square = value * value
    square = jnp.sum(square.reshape(-1, D), axis=0, keepdims=True)
    square = jnp.sum(square, axis=1, keepdims=True)
    if known.shape[0] == 1:
        square = square + known[0, :, 0:1]
    else:
        vector = known[0:3]
        for place in range(1, shards):
            vector = vector + known[3 * place : 3 * place + 3]
        refs[-1][...] = vector
        square = square + jnp.sum(jnp.sum(vector * vector, axis=0), axis=1, keepdims=True)
    squares[...] = jnp.broadcast_to(square.reshape(1, 1, 1), squares.shape)


def finish(parts, known, shards):
    shape = parts[-1].shape
    outs = [(shape, F32, whole(shape))]
    if known.shape[0] == 1:
        outs.append(((shards, 1, 128), F32, whole((shards, 1, 128))))
    else:
        outs += [((1, 1, 128), F32, whole((1, 1, 128))), ((3, 1, 128), F32, whole((3, 1, 128)))]
    return run(
        partial(finish_kernel, [isinstance(part, tuple) for part in parts], shards),
        "finish",
        (1,),
        [
            (array, whole((shape[0] // 2 if isinstance(part, tuple) else shape[0],) + shape[1:]))
            for part in parts
            for array in flat([part])
        ]
        + [(known, whole(known.shape))],
        outs,
        cost=(D * D, D * D, 0),
        mebibytes=12,
    )


def tie(array, *others):
    return lax.optimization_barrier((array,) + others)[0]


def vectors(width, owners, shares, table, bias):
    table[...] = jnp.zeros_like(table)
    count = D // width
    for row in range(NVEC // D):
        pieces = []
        for piece in range(row * count, (row + 1) * count):
            lane = 128 * (piece % 3)
            pieces.append(shares[piece // 3, :, lane : lane + 128][:, :width])
        table[row : row + 1, :] = jnp.concatenate(pieces, axis=1)
    count = D // 2 // width
    for place in range(bias.shape[0]):
        pieces = []
        for slot in range(place * count, (place + 1) * count):
            piece = owners[slot] + B1 * (D // width)
            lane = pl.multiple_of(piece % 3 * 128, 128)
            pieces.append(shares[piece // 3, :, pl.ds(lane, 128)][:, :width])
        bias[place] = jnp.concatenate(pieces, axis=1)


def attend_kernel(piece, width, order, owners, hidden_owners, length, x, meeting, *refs):
    parts, (packed, table, weight, context, log_totals, lines, bias, columns, shares, held) = refs[:-10], refs[-10:]
    step = power_of_two(piece)

    @pl.when(pl.program_id(0) == 0)
    def _():
        places = iter(order)
        for ref in parts:
            if len(ref.shape) == 3:
                for slot, owner in enumerate(order):
                    shares[hidden_owners[slot]] = ref[owner]
                continue
            for slot in range(ref.shape[0]):
                for deep in range(ref.shape[1]):
                    owner = owners[next(places)]
                    start = pl.multiple_of(owner * piece, step)
                    for which in range(4):
                        rows = ref[slot, deep, which * piece : (which + 1) * piece, :]
                        held[which, pl.ds(start, piece), :] = rows.astype(F32)
                    if ref.shape[2] > 4 * piece:
                        rows = ref[slot, deep, 4 * piece :, :].astype(F32)
                        shares[owner] = rows[0:1, : shares.shape[2]]
        vectors(width, hidden_owners, shares, lines, bias)
        columns[...] = lines[...].T

    rows = x[...]
    block = GROUP * HEAD_DIM
    span = pl.ds(pl.multiple_of(pl.program_id(0) * block, block), block)
    pieces = [held[which, span, :].astype(BF) for which in range(4)]
    for which in range(3):
        table[which] = pieces[which]
    weight[...] = pieces[3]
    queries = dot(pieces[0], rows, NT) + columns[span, BQ : BQ + 1]
    queries = (queries.astype(BF) * HEAD_DIM ** (-0.5)).astype(BF)
    keys = dot(pieces[1], rows, NT).astype(BF)
    values = (dot(pieces[2], rows, NT) + columns[span, BV : BV + 1]).astype(BF)
    packed[0], packed[1], packed[2] = queries, keys, values
    visible = lax.broadcasted_iota(jnp.int32, (LENGTH, LENGTH), 0) < length[0]
    spans = [slice(HEAD_DIM * head, HEAD_DIM * (head + 1)) for head in range(GROUP)]
    score = lambda head: dot(keys[spans[head]], queries[spans[head]], TN)
    following, done = score(0), []
    for head in range(GROUP):
        scores = jnp.where(visible, following, MASKED)
        if head + 1 < GROUP:
            following = score(head + 1)
        largest = jnp.max(scores, axis=0, keepdims=True)
        powers = jnp.exp(scores - largest)
        totals = jnp.sum(powers, axis=0, keepdims=True)
        done.append(dot(values[spans[head]], powers.astype(BF), NN) * (1.0 / totals))
        log_totals[0, head : head + 1, :] = largest + jnp.log(totals)
    context[...] = jnp.concatenate(done, axis=0).T.astype(BF)


def join_kernel(x, context, weight, table, unit_rows, factor, low, base):
    branch = dot(context[...], weight[...], NN) + table[BO : BO + 1, :]
    rows = x[...].astype(F32) + branch
    center = rows - mean(rows)
    spread = lax.rsqrt(mean(center * center) + EPSILON)
    normed = center * spread
    unit_rows[...] = normed
    factor[...] = spread
    shifted = normed * table[GA : GA + 1, :] + table[SA : SA + 1, :]
    low[...] = shifted.astype(BF)
    base[...] = shifted + table[B2 : B2 + 1, :]


def gelu_pair(value):
    power = jnp.exp(value * value * -0.5)
    part = 1.0 / (1.0 + jnp.abs(value) * (0.3275911 * 0.5**0.5))
    tail = 0.5 * 1.061405429
    for factor in (-1.453152027, 1.421413741, -0.284496736, 0.254829592):
        tail = tail * part + 0.5 * factor
    tail = tail * part * power
    chance = jnp.where(value < 0.0, tail, 1.0 - tail)
    return value * chance, chance + value * power * (2.0 * jnp.pi) ** -0.5


def joined(refs):
    return jnp.concatenate([ref[...].reshape(-1, D) for ref in refs], axis=0)


def ffn_forward_kernel(places, low, *refs):
    bias, start, active, slope, running = refs[8:]
    rows = low[...]
    expand, reduce = joined(refs[:4]), joined(refs[4:8])
    shift = jnp.concatenate([bias[places[0]], bias[places[1]]], axis=1)
    total = start[...]
    for first in range(0, D, SUB):
        span = slice(first, first + SUB)
        value, change = gelu_pair(dot(rows, expand[span], NT) + shift[:, span])
        value = value.astype(BF)
        active[:, span] = value
        slope[:, span] = change.astype(BF)
        total = total + dot(value, reduce[span], NN)
    running[...] = total


def loss_kernel(length, rows, cotangent, table, output, grad, grad_low, sums):
    tile = rows.shape[0]
    value = rows[...]
    center = value - mean(value)
    factor = lax.rsqrt(mean(center * center) + EPSILON)
    normed = center * factor
    gain = table[GB : GB + 1, :]
    output[...] = (normed * gain + table[SB : SB + 1, :]).astype(BF)
    place = pl.program_id(0) * tile + lax.broadcasted_iota(jnp.int32, (tile, 1), 0)
    upstream = jnp.where(place < length[0], cotangent[...].astype(F32), 0.0)
    scaled = upstream * gain
    change = factor * (scaled - mean(scaled) - normed * mean(scaled * normed))
    grad[...] = change
    change_low = change.astype(BF)
    grad_low[...] = change_low

    @pl.when(pl.program_id(0) == 0)
    def _():
        sums[...] = jnp.zeros_like(sums)

    sums[0:1, :] += jnp.sum(upstream * normed, axis=0, keepdims=True)
    sums[1:2, :] += jnp.sum(upstream, axis=0, keepdims=True)
    sums[2:3, :] += jnp.sum(change_low.astype(F32), axis=0, keepdims=True)


def by_slot(grads, which, result):
    _, slots, deep, width, _ = grads.shape
    quarter = slots // 2
    result = jnp.concatenate(result, axis=0).reshape(2, 2, quarter, deep // 2, width, D)
    for place in range(2):
        for side in range(2):
            into = slice(place * quarter, (place + 1) * quarter), slice(side * (deep // 2), (side + 1) * (deep // 2))
            grads[which, into[0], into[1]] = result[place, side]


def reduce_backward_kernel(grad_low, active_a, active_b, grads):
    active = jnp.concatenate([active_a[...], active_b[...]], axis=1)
    by_slot(grads, 0, [dot(active[:, first : first + SUB], grad_low[...], TN).astype(BF) for first in range(0, D, SUB)])


def ffn_backward_kernel(both, grad_low, low, slope_a, slope_b, *refs):
    actives, refs = (refs[:2], refs[2:]) if both else ((), refs)
    start, grads, grad_bias, running = refs[8:]
    upstream, rows = grad_low[...], low[...]
    expand, reduce = joined(refs[:4]), joined(refs[4:8])
    slope = jnp.concatenate([slope_a[...], slope_b[...]], axis=1)
    if both:
        active = jnp.concatenate([actives[0][...], actives[1][...]], axis=1)
    reduced, expanded = [], []
    total = start[...]
    for first in range(0, D, SUB):
        span = slice(first, first + SUB)
        if both:
            reduced.append(dot(active[:, span], upstream, TN).astype(BF))
        change = (dot(upstream, reduce[span], NT) * slope[:, span].astype(F32)).astype(BF)
        grad_bias[:, span] = jnp.sum(change.astype(F32), axis=0, keepdims=True)
        expanded.append(dot(change, rows, TN).astype(BF))
        total = total + dot(change, expand[span], NN)
    running[...] = total
    if both:
        by_slot(grads, 0, reduced)
    by_slot(grads, int(both), expanded)


def sums_kernel(width, owners, sums_in, sums_one, sums_two, *refs):
    biases, out = refs[:4], refs[4]
    out[...] = jnp.zeros_like(out)
    count = D // width
    rows = (
        (BQ, sums_in[0, 0:1]),
        (BV, sums_in[2, 0:1]),
        (BO, sums_one[2:3]),
        (GA, sums_one[0:1]),
        (SA, sums_one[1:2]),
        (B2, sums_two[2:3]),
        (GB, sums_two[0:1]),
        (SB, sums_two[1:2]),
    )
    for row, value in rows:
        for piece in range(count):
            out[row * count + piece, :, :width] = value[:, piece * width : (piece + 1) * width]
    for place, ref in enumerate(biases):
        value = ref[...]
        for piece in range(count):
            into = owners[place * count + piece] + B1 * count
            out[into, :, :width] = value[:, piece * width : (piece + 1) * width]


def branch_kernel(upstream, unit_rows, factor, context, weight, table, grad, grad_context, grad_weight, sums):
    value = upstream[...]
    normed = unit_rows[...]
    scaled = value * table[GA : GA + 1, :]
    change = factor[...] * (scaled - mean(scaled) - normed * mean(scaled * normed))
    grad[...] = change
    change_low = change.astype(BF)

    @pl.when(pl.program_id(0) == 0)
    def _():
        sums[...] = jnp.zeros_like(sums)
        grad_weight[...] = jnp.zeros_like(grad_weight)

    sums[0:1, :] += jnp.sum(value * normed, axis=0, keepdims=True)
    sums[1:2, :] += jnp.sum(value, axis=0, keepdims=True)
    sums[2:3, :] += jnp.sum(change_low.astype(F32), axis=0, keepdims=True)
    grad_context[...] = dot(weight[...], change_low, NT).astype(BF)
    grad_weight[...] += dot(context[...], change_low, TN)


def attend_backward_kernel(length, packed, grad_context, log_totals, out):
    visible = lax.broadcasted_iota(jnp.int32, (LENGTH, LENGTH), 0) < length[0]
    spans = [slice(HEAD_DIM * head, HEAD_DIM * (head + 1)) for head in range(GROUP)]

    def score(head):
        span = spans[head]
        return dot(packed[1, span, :], packed[0, span, :], TN), dot(packed[2, span, :], grad_context[span, :], TN)

    following = score(0)
    for head in range(GROUP):
        span = spans[head]
        scores, grad_chances = following
        if head + 1 < GROUP:
            following = score(head + 1)
        chances = jnp.where(visible, jnp.exp(scores - log_totals[0, head : head + 1, :]), 0.0)
        out[2, span, :] = dot(grad_context[span, :], chances.astype(BF), NT).astype(BF)
        inner = jnp.sum(chances * grad_chances, axis=0, keepdims=True)
        grad_scores = (chances * (grad_chances - inner)).astype(BF)
        out[1, span, :] = dot(packed[0, span, :], grad_scores, NT).astype(BF)
        out[0, span, :] = (dot(packed[1, span, :], grad_scores, NN) * HEAD_DIM ** (-0.5)).astype(BF)


def in_grads_kernel(piece, owners, grads, x, grad_out, *refs):
    outs, (sums, held) = refs[:4], refs[4:]
    step = power_of_two(piece)
    which = pl.program_id(0)
    slots, rows = outs[0].shape[1], outs[0].shape[2] // 4

    def place(source, at):
        for side, ref in enumerate(outs):
            for slot in range(slots):
                for first in range(0, rows, piece):
                    index = ((side * slots + slot) * rows + first) // piece
                    start = pl.multiple_of(owners[index] * piece, step)
                    into = slice(at * rows + first, at * rows + first + piece)
                    ref[0, slot, into, :] = source[pl.ds(start, piece), :].astype(BF)

    held[...] = dot(grads[0], x[...], NN)
    sums[0] = dot(jnp.ones((8, LENGTH), BF), grads[0], NT)
    for at in range(3):
        pl.when(which == at)(partial(place, held, at))

    @pl.when(which == 0)
    def _():
        place(grad_out, 3)


def input_grad_kernel(grads, weights, residual, out):
    value = residual[...]
    for which in range(3):
        value = value + dot(grads[which], weights[which], TN)
    out[...] = value.astype(BF)


BLEND = min(0.999, (1 + STEP) / (10 + STEP))
RATES = (RATE_MATRIX, RATE_PROJECTION, RATE_MATRIX, RATE_MATRIX)


def advance(weight, velocity, average, gradient, factor, rate):
    clipped = gradient * factor
    velocity = MOMENTUM * velocity + clipped
    weight = weight - rate * (clipped + MOMENTUM * velocity)
    return weight, velocity, BLEND * average + (1.0 - BLEND) * weight


def update_kernel(squares, near, hidden, *refs):
    states, outs = refs[:12], refs[12:]
    value = squares[...]
    norm = jnp.sqrt(jnp.sum(value, axis=0)[:, 0:1])
    factor = 1.0 / jnp.maximum(norm, 1.0)
    outs[12][...] = norm
    gradients = (near[:3], near[3], hidden[1], hidden[0])
    for at, (gradient, rate) in enumerate(zip(gradients, RATES)):
        weight, velocity, average = states[at][...], states[4 + at][...], states[8 + at][...]
        results = advance(weight, velocity, average, gradient, factor, rate)
        for place, result in enumerate(results):
            outs[4 * place + at][...] = result


def body(
    wide,
    narrow,
    layer_input,
    cotangent,
    lengths,
    attention_in,
    attention_out,
    expand_weight,
    reduce_weight,
    vector_params,
    velocity_in,
    velocity_out,
    velocity_expand,
    velocity_reduce,
    velocity_vector,
    average_in,
    average_out,
    average_expand,
    average_reduce,
    average_vector,
):
    cube = Cube(wide, narrow)
    shards = wide * narrow
    share, width, spare = D // shards, FF // shards, NVEC // shards
    unit = share * narrow
    half = wide // 4
    groups = FF // D
    last = len(cube.plane) - 1
    owners = cube.plane_owners()
    held_kind = BF if unit % 16 == 0 else F32

    quarter, deep = half // 2, narrow // 2
    all_owners = cube.all_owners(jnp.arange(shards, dtype=jnp.int32))
    aligned = share % 8 == 0
    near = jnp.concatenate([attention_in.astype(BF).transpose(0, 2, 1).reshape(3 * share, D), attention_out.astype(BF)])
    vector = jnp.pad(vector_params.astype(BF).reshape(3, width), ((0, 0), (0, 128 - width))).reshape(1, 3 * 128)
    near = jnp.concatenate([near, jnp.pad(vector, ((0, 7), (0, D - 3 * 128)))]).reshape(1, 1, 4 * share + 8, D)
    hidden = jnp.stack([expand_weight.astype(BF).T, reduce_weight.astype(BF)]).reshape(1, 2, 1, width, D)
    final = len(cube.depth) - 1

    def early_slots(slots, axis):
        for step in range(final):
            slots = jnp.concatenate([slots, cube.swap_depth(slots, step)], axis=axis)
        return slots

    def plane_quarter(slots):
        for step in range(last - 1):
            slots = jnp.concatenate([slots, cube.swap_plane(slots, step)])
        return slots

    early = early_slots(near, 1)
    late = cube.swap_depth(early, final)
    hidden_early = early_slots(tie(hidden, late), 2)
    early, late = plane_quarter(early), plane_quarter(late)
    next_early, far_early = cube.swap_plane(early, last - 1), cube.swap_plane(early, last)
    late, next_early, far_early = lax.optimization_barrier((late, next_early, far_early))
    next_late, far_late = cube.swap_plane(late, last - 1), cube.swap_plane(late, last)
    beyond_early = cube.swap_plane(next_early, last)
    meeting = cube.swap_core(hidden_early[0, 0, deep - 1, :8, :128])
    hidden_early, meeting = lax.optimization_barrier((hidden_early, meeting))
    hidden_late = cube.swap_depth(hidden_early, final)
    next_late, beyond_early, far_late, hidden_early = lax.optimization_barrier(
        (next_late, beyond_early, far_late, hidden_early)
    )
    beyond_late = cube.swap_plane(next_late, last)
    hidden_early = plane_quarter(hidden_early)
    hidden_next_early, hidden_far_early = (cube.swap_plane(hidden_early, last - 1), cube.swap_plane(hidden_early, last))
    beyond_late, hidden_late, hidden_next_early = lax.optimization_barrier(
        (beyond_late, hidden_late, hidden_next_early)
    )
    hidden_late = plane_quarter(hidden_late)
    hidden_next_late, hidden_far_late = cube.swap_plane(hidden_late, last - 1), cube.swap_plane(hidden_late, last)
    attention = [early, late, next_early, next_late, far_early, far_late, beyond_early, beyond_late]
    attention += [cube.swap_core(part) for part in attention]
    order = [
        (place * quarter + slot) * narrow + side * deep + k
        for place in range(8)
        for side in range(2)
        for slot in range(quarter)
        for k in range(deep)
    ]
    hidden_owners = cube.all_owners(jnp.array(order, jnp.int32))
    pieces, piece, piece_order, piece_owners = attention, share, order, all_owners
    if not aligned:
        pieces, shares = [], []
        for place in range(8):
            part = jnp.concatenate(attention[2 * place : 2 * place + 2], axis=1)
            shares.append(part[:, :, 4 * share, : 3 * 128].reshape(-1, 1, 3 * 128).astype(F32))
            part = jnp.take(part[:, :, : 4 * share], cube.depth_slots(place // 4), axis=1)
            part = part.reshape(quarter, narrow, 4, share, D).transpose(0, 2, 1, 3, 4)
            pieces.append(part.reshape(quarter, 1, 4 * unit, D))
        pieces.append(jnp.concatenate(shares))
        piece, piece_order, piece_owners = unit, list(range(wide)), owners

    group_spec = pl.BlockSpec((3, GROUP * HEAD_DIM, LENGTH), lambda j: (0, j, 0))
    log_spec = pl.BlockSpec((1, GROUP, LENGTH), lambda j: (j, 0, 0))
    packed, weights_in, weight_out, context, log_totals, table, bias = run(
        partial(attend_kernel, piece, width, piece_order),
        "attend",
        (STEPS,),
        [(piece_owners, SMEM), (hidden_owners, SMEM), (lengths, SMEM)]
        + [(far_memory(layer_input), whole((LENGTH, D))), (meeting, ANY)]
        + [(far_memory(part), whole(part.shape)) for part in pieces],
        [
            (pltpu.HBM((3, D, LENGTH), BF), None, group_spec),
            (pltpu.HBM((3, D, D), BF), None, pl.BlockSpec((3, GROUP * HEAD_DIM, D), lambda j: (0, j, 0))),
            (pltpu.HBM((D, D), BF), None, pl.BlockSpec((GROUP * HEAD_DIM, D), lambda j: (j, 0))),
            ((LENGTH, D), BF, pl.BlockSpec((LENGTH, GROUP * HEAD_DIM), lambda j: (0, j))),
            ((STEPS, GROUP, LENGTH), F32, log_spec),
            ((16, D), F32, whole((16, D))),
            ((8, 1, D // 2), F32, whole((8, 1, D // 2))),
        ],
        scratch=[pltpu.VMEM((D, 16), F32), pltpu.VMEM((shards, 1, 3 * 128), F32), pltpu.VMEM((4, D, D), F32)],
        cost=(10 * D * D * LENGTH, 24 * D * D, HEADS * LENGTH * LENGTH),
        mebibytes=36,
    )
    context, hidden_next_early, hidden_next_late = lax.optimization_barrier((context, hidden_next_early, hidden_next_late))
    hidden = [
        (hidden_early, hidden_late),
        (hidden_next_early, hidden_next_late),
        (hidden_far_early, hidden_far_late),
        (cube.swap_plane(hidden_next_early, last), cube.swap_plane(hidden_next_late, last)),
    ]
    swap_both = lambda parts: tuple(cube.swap_core(part) for part in parts)
    hidden += [swap_both(hidden[0]), swap_both(hidden[1])]
    tile = 256
    row_spec = pl.BlockSpec((tile, D), lambda i: (i, 0))
    one_spec = pl.BlockSpec((tile, 1), lambda i: (i, 0))
    table_spec = whole((16, D))
    unit_rows, factor_one, low, running = run(
        join_kernel,
        "join",
        (LENGTH // tile,),
        [
            (layer_input, row_spec),
            (context, row_spec),
            (weight_out, whole((D, D))),
            (table, table_spec),
        ],
        [
            ((LENGTH, D), F32, row_spec),
            ((LENGTH, 1), F32, one_spec),
            ((LENGTH, D), BF, row_spec),
            ((LENGTH, D), F32, row_spec),
        ],
        cost=(2 * D * D * LENGTH, 14 * LENGTH * D, 0),
        mebibytes=16,
    )

    rows_spec = pl.BlockSpec(memory_space=pltpu.VMEM)
    hidden_spec = lambda which: pl.BlockSpec((quarter, 1, deep, width, D), lambda *i: (0, which, 0, 0, 0))
    hidden_ins = lambda first, second: [
        (part, hidden_spec(which)) for which in range(2) for place in (first, second) for part in hidden[place]
    ]

    def forward(first, second, running):
        return run(
            partial(ffn_forward_kernel, (first, second)),
            "expand",
            (1,),
            [
                (low, rows_spec),
                *hidden_ins(first, second),
                (bias, whole((8, 1, D // 2))),
                (running, rows_spec),
            ],
            [
                (pltpu.HBM((LENGTH, D), BF), None, whole((LENGTH, D))),
                (pltpu.HBM((LENGTH, D), BF), None, whole((LENGTH, D))),
                ((LENGTH, D), F32, rows_spec),
            ],
            cost=(4 * D * D * LENGTH, 4 * D * D + 12 * LENGTH * D, 2 * LENGTH * D),
        )

    stored = [None] * 8
    for first, second in ((0, 1), (4, 5), (2, 6), (3, 7)):
        if first == 4:
            hidden[2] = lax.optimization_barrier((*hidden[2], running))[:2]
            hidden += [swap_both(hidden[2])]
        if first == 2:
            beyond = swap_both(hidden[3])
            running, *beyond = lax.optimization_barrier((running, *beyond))
            hidden += [tuple(beyond)]
        active, slope, running = forward(first, second, running)
        stored[first] = (active, slope, 0)
        stored[second] = (active, slope, 1)
    sum_spec = whole((8, D))
    output, grad_two, grad_low, sums_two = run(
        loss_kernel,
        "loss",
        (LENGTH // tile,),
        [(lengths, SMEM), (running, row_spec), (cotangent, row_spec), (table, table_spec)],
        [
            ((LENGTH, D), BF, row_spec),
            ((LENGTH, D), F32, row_spec),
            ((LENGTH, D), BF, row_spec),
            (pltpu.HBM((8, D), F32), None, sum_spec),
        ],
        cost=(40 * LENGTH * D, 14 * LENGTH * D, 0),
    )
    column = lambda place: pl.BlockSpec((LENGTH, D // 2), lambda *i: (0, stored[place][2]))

    def reduce_backward(first):
        shape = (1, half, narrow, width, D)
        return run(
            reduce_backward_kernel,
            "reduce_back",
            (1,),
            [(grad_low, rows_spec)] + [(stored[place][0], column(place)) for place in (first, first + 1)],
            [(pltpu.HBM(shape, BF), None, whole(shape))],
            cost=(2 * D * D * LENGTH, 2 * D * D + 4 * LENGTH * D, 0),
        )[0]

    def backward(both, first, running):
        shape = (1 + both, half, narrow, width, D)
        return run(
            partial(ffn_backward_kernel, both),
            "expand_back",
            (1,),
            [(grad_low, rows_spec), (low, rows_spec)]
            + [(stored[place][1], column(place)) for place in (first, first + 1)]
            + [(stored[place][0], column(place)) for place in (first, first + 1) if both]
            + hidden_ins(first, first + 1)
            + [(running, rows_spec)],
            [
                (pltpu.HBM(shape, BF), None, whole(shape)),
                ((1, D), F32, whole((1, D))),
                ((LENGTH, D), F32, rows_spec),
            ],
            cost=(8 * D * D * LENGTH, 8 * D * D + 12 * LENGTH * D, 0),
        )

    other_reduce = cube.swap_core(reduce_backward(6))
    own_reduce = reduce_backward(2)
    leaving_reduce = combine([own_reduce, other_reduce], 1, 0, half)
    arrived_reduce = cube.swap_plane(leaving_reduce, last)
    grad_two = tie(grad_two, leaving_reduce)
    other_expand, bias_6, running = backward(False, 6, grad_two)
    other_expand = cube.swap_core(other_expand)
    own_expand, bias_2, running = backward(False, 2, running)
    leaving_expand = combine([own_expand, other_expand], 1, 0, half)
    arrived_expand = cube.swap_plane(leaving_expand, last)
    other_near, bias_4, running = backward(True, 4, tie(running, leaving_expand))
    other_near = cube.swap_core(other_near)
    own_near, bias_0, running = backward(True, 0, running)
    hidden_parts = [own_near, tie(other_near, running), (arrived_reduce, arrived_expand)]

    grad_one, grad_context, grad_out, sums_one = run(
        branch_kernel,
        "branch_back",
        (LENGTH // tile,),
        [
            (running, row_spec),
            (unit_rows, row_spec),
            (factor_one, one_spec),
            (context, row_spec),
            (weight_out, whole((D, D))),
            (table, table_spec),
        ],
        [
            (pltpu.HBM((LENGTH, D), F32), None, row_spec),
            ((D, LENGTH), BF, pl.BlockSpec((D, tile), lambda i: (0, i))),
            ((D, D), F32, whole((D, D))),
            (pltpu.HBM((8, D), F32), None, sum_spec),
        ],
        cost=(4 * D * D * LENGTH, 8 * D * D + 16 * LENGTH * D, 0),
    )
    (grads,) = run(
        attend_backward_kernel,
        "attend_back",
        (STEPS,),
        [
            (lengths, SMEM),
            (packed, group_spec),
            (grad_context, pl.BlockSpec((GROUP * HEAD_DIM, LENGTH), lambda j: (j, 0))),
            (log_totals, log_spec),
        ],
        [((3, D, LENGTH), BF, group_spec)],
        cost=(10 * HEADS * LENGTH * LENGTH * HEAD_DIM, 14 * LENGTH * D, HEADS * LENGTH * LENGTH),
    )

    def send(parts, axis):
        middle = flat(parts[-1:])[0].shape[axis] // 2
        return combine(parts, axis, middle, middle)

    hidden_leaving = send(hidden_parts, 1)
    grads = tie(grads, hidden_leaving)
    hidden_parts.append(cube.swap_plane(hidden_leaving, last - 1))
    chunk = (1, half, 4 * unit, D)
    *chunks, sums_in = run(
        partial(in_grads_kernel, share if aligned else unit),
        "project_back",
        (3,),
        [
            (all_owners if aligned else owners, SMEM),
            (grads, pl.BlockSpec((1, D, LENGTH), lambda i: (i, 0, 0))),
            (layer_input, whole((LENGTH, D))),
            (grad_out, whole((D, D))),
        ],
        [(pltpu.HBM(chunk, BF), None, whole(chunk))] * 4
        + [((3, 8, D), F32, pl.BlockSpec((1, 8, D), lambda i: (i, 0, 0)))],
        scratch=[pltpu.VMEM((D, D), F32)],
        cost=(6 * D * D * LENGTH, 12 * D * D, 0),
        mebibytes=32,
    )
    if not aligned:
        for place, part in enumerate(chunks):
            order = cube.depth_owners(place // 2)
            part = jnp.take(part.reshape(half, 4, narrow, share, D), order, axis=2)
            chunks[place] = part.reshape(chunk)
    own_near, own_far, other_near, other_far = chunks
    other_far, other_near = cube.swap_core(other_far), cube.swap_core(other_near)
    (grad_vector,) = run(
        partial(sums_kernel, width),
        "sums",
        (1,),
        [
            (hidden_owners, SMEM),
            (sums_in, whole((3, 8, D))),
            (sums_one, sum_spec),
            (sums_two, sum_spec),
        ]
        + [(part, whole((1, D))) for part in (bias_0, bias_2, bias_4, bias_6)],
        [((3 * shards, 1, 128), F32, whole((3 * shards, 1, 128)))],
        mebibytes=8,
    )
    grad_vector = lax.all_to_all(grad_vector, AXES, 0, 0, tiled=True)
    own_far, hidden_parts[-1], grad_vector = lax.optimization_barrier((own_far, hidden_parts[-1], grad_vector))
    for step in reversed(range(last - 1)):
        hidden_parts.append(cube.swap_plane(send(hidden_parts, 1), step))
    view = lambda part: part.reshape(1, half, 4, narrow, share, D)
    own_near, own_far, other_near, other_far = (view(part) for part in (own_near, own_far, other_near, other_far))
    late = cube.swap_plane(combine([own_far, other_far], 3, deep, deep), last)
    early = cube.swap_plane(combine([own_far, other_far], 3, 0, deep), last)
    hidden_going = send(hidden_parts, 2)
    grads = tie(grads, hidden_going)
    (input_grad,) = run(
        input_grad_kernel,
        "input_back",
        (LENGTH // tile,),
        [
            (grads, pl.BlockSpec((3, D, tile), lambda i: (0, 0, i))),
            (far_memory(weights_in), whole((3, D, D))),
            (far_memory(grad_one), row_spec),
        ],
        [((LENGTH, D), BF, row_spec)],
        cost=(6 * D * D * LENGTH, 6 * D * D + 12 * LENGTH * D, 0),
    )
    late, input_grad = lax.optimization_barrier((late, input_grad))
    hidden_parts.append(cube.swap_depth(hidden_going, final))
    late_parts, early_parts = [own_near, other_near, late], [own_near, other_near, early]
    late_deeps = [1, 1, 0]
    for step in reversed(range(last)):
        middle = late_parts[-1].shape[1] // 2
        late_parts.append(cube.swap_plane(combine(late_parts, 1, middle, middle, late_deeps), step))
        late_deeps.append(0)
        early_parts.append(cube.swap_plane(combine(early_parts, 1, middle, middle, [0] * len(early_parts)), step))
    early_parts.append(cube.swap_depth(combine(late_parts, 1, 0, 1, late_deeps), final))
    for step in reversed(range(final)):
        early_parts.append(cube.swap_depth(send(early_parts, 3), step))
        hidden_parts.append(cube.swap_depth(send(hidden_parts, 2), step))
    parts = early_parts
    owned_hidden, squares, owned_vector = finish(hidden_parts, grad_vector, shards)
    owned_near, squares = finish(parts, squares, shards)
    squares = lax.all_to_all(squares, AXES, 0, 0)

    turn = lambda array: array.transpose(*range(array.ndim - 2), -1, -2)
    states = []
    for first, second, third, fourth in (
        (attention_in, attention_out, expand_weight, reduce_weight),
        (velocity_in, velocity_out, velocity_expand, velocity_reduce),
        (average_in, average_out, average_expand, average_reduce),
    ):
        states += [turn(first), second, turn(third), fourth]
    near, hidden = owned_near.reshape(4, share, D), owned_hidden.reshape(2, width, D)
    vector = owned_vector[:, 0, :width].reshape(spare)
    *states, grad_norm = run(
        update_kernel,
        "update",
        (1,),
        [(squares, whole(squares.shape)), (near, whole(near.shape))]
        + [(far_memory(array), whole(array.shape)) for array in [hidden] + states],
        [(array.shape, F32, whole(array.shape)) for array in states] + [((1, 1), F32, whole((1, 1)))],
        cost=(FF * D, 28 * (share * 4 + width * 2) * D, 0),
    )
    grad_norm = grad_norm.reshape(())
    vectors = advance(
        vector_params, velocity_vector, average_vector, vector, 1.0 / jnp.maximum(grad_norm, 1.0), RATE_VECTOR
    )
    outs = []
    for place in range(3):
        first, second, third, fourth = states[4 * place : 4 * place + 4]
        outs += [turn(first), second, turn(third), fourth, vectors[place]]
    return (output, input_grad, *outs, grad_norm)


def solution(mesh):
    both = ("wide", "narrow")
    first, second, third = P(both, None), P(None, both), P(None, None, both)
    state = (third, first, second, first, P(both))
    return jax.shard_map(
        partial(body, mesh.shape["wide"], mesh.shape["narrow"]),
        mesh=mesh,
        in_specs=(first, first, P(both)) + state * 3,
        out_specs=(first, first) + state * 3 + (P(),),
        check_vma=False,
    )
```

```python
from functools import partial

import jax
import jax.numpy as jnp
from jax import lax
from jax.experimental import pallas as pl
from jax.experimental.pallas import tpu as pltpu
from jax.sharding import PartitionSpec as P

D = 768
FF = 3072
HEADS = 12
HEAD_DIM = 64
LENGTH = 512
STEP = 10
NVEC = 8 * D + FF
GROUP = 4
STEPS = HEADS // GROUP
SUB = 256

MOMENTUM = 0.9
RATE_MATRIX = 24.0
RATE_PROJECTION = 160.0
RATE_VECTOR = 256.0
EPSILON = 1e-05
MASKED = -1000000000.0

AXES = ("wide", "narrow")
BF = jnp.bfloat16
F32 = jnp.float32
NN = ((1,), (0,))
NT = ((1,), (1,))
TN = ((0,), (0,))

BQ, BV, BO, GA, SA, B1, B2, GB, SB = 0, 1, 2, 3, 4, 5, 9, 10, 11


def dot(left, right, dims):
    return lax.dot_general(left, right, (dims, ((), ())), preferred_element_type=F32)


def mean(rows):
    return jnp.sum(rows, axis=-1, keepdims=True) * (1.0 / D)


def power_of_two(number):
    return number & -number


SMEM = pl.BlockSpec(memory_space=pltpu.SMEM)
ANY = pl.BlockSpec(memory_space=pl.ANY)


def run(kernel, name, grid, ins, outs, scratch=(), cost=(0, 0, 0), mebibytes=24, alias=None):
    scale = 8 if name.endswith("_back") and name != "input_back" else 1
    return pl.pallas_call(
        kernel,
        grid=grid,
        in_specs=[spec for _, spec in ins],
        out_specs=[spec for _, _, spec in outs],
        out_shape=[jax.ShapeDtypeStruct(shape, kind) if kind else shape for shape, kind, _ in outs],
        scratch_shapes=scratch,
        input_output_aliases=alias or {},
        compiler_params=pltpu.CompilerParams(
            vmem_limit_bytes=mebibytes * 1024 * 1024, dimension_semantics=("arbitrary",) * len(grid)
        ),
        cost_estimate=pl.CostEstimate(flops=scale * cost[0], bytes_accessed=scale * cost[1], transcendentals=cost[2]),
        name=name,
    )(*[array for array, _ in ins])


def far_memory(array):
    return pltpu.with_memory_space_constraint(array, pltpu.HBM)


def whole(shape):
    return pl.BlockSpec(shape, lambda *i: (0,) * len(shape))


class Cube:
    def __init__(self, wide, narrow):
        self.wide, self.narrow = wide, narrow
        wide_bits, narrow_bits = wide.bit_length() - 1, narrow.bit_length() - 1
        plane = list(range(1, wide_bits))
        half = len(plane) // 2
        swapped = plane[half:] + plane[:half] if len(plane) % 2 == 0 else plane
        depth = list(range(narrow_bits))
        self.depth = list(zip(reversed(depth), depth))
        self.plane = list(zip(plane, swapped))
        self.wide_at = lax.axis_index("wide")
        self.narrow_at = lax.axis_index("narrow")

    def swap_depth(self, array, step):
        place = lambda w, n: w * self.narrow + n
        pairs = [
            (place(w, n), place(w, n ^ (1 << self.depth[step][w & 1])))
            for w in range(self.wide)
            for n in range(self.narrow)
        ]
        return lax.ppermute(array, AXES, pairs)

    def swap_plane(self, array, step):
        pairs = [(i, i ^ (1 << self.plane[step][i & 1])) for i in range(self.wide)]
        return lax.ppermute(array, "wide", pairs)

    def swap_core(self, array):
        return lax.ppermute(array, "wide", [(i, i ^ 1) for i in range(self.wide)])

    def slots(self, apart, bits, core):
        def placed(which):
            slot = jnp.zeros_like(apart)
            for position, pair in enumerate(bits):
                slot = slot | (((apart >> pair[which]) & 1) << position)
            return slot

        return jnp.where(core == 0, placed(0), placed(1))

    def owners(self, slot, bits, core):
        def placed(which):
            apart = jnp.zeros_like(slot)
            for position, pair in enumerate(bits):
                apart = apart | (((slot >> position) & 1) << pair[which])
            return apart

        return jnp.where(core == 0, placed(0), placed(1))

    def plane_owners(self):
        slot = jnp.arange(self.wide, dtype=jnp.int32)
        other = slot >> len(self.plane)
        return (other | self.owners(slot, self.plane, other ^ (self.wide_at & 1))) ^ self.wide_at

    def depth_slots(self, other):
        place = jnp.arange(self.narrow, dtype=jnp.int32)
        return self.slots(place ^ self.narrow_at, self.depth, (self.wide_at & 1) ^ other)

    def depth_owners(self, other):
        core = (self.wide_at & 1) ^ other
        return self.owners(jnp.arange(self.narrow, dtype=jnp.int32), self.depth, core) ^ self.narrow_at

    def all_owners(self, slot):
        deep, flat = slot % self.narrow, slot // self.narrow
        other = flat >> len(self.plane)
        core = other ^ (self.wide_at & 1)
        wide_place = (other | self.owners(flat, self.plane, core)) ^ self.wide_at
        return wide_place * self.narrow + (self.owners(deep, self.depth, core) ^ self.narrow_at)

    def all_slots(self):
        place = jnp.arange(self.wide * self.narrow, dtype=jnp.int32)
        flat, deep = (place // self.narrow) ^ self.wide_at, (place % self.narrow) ^ self.narrow_at
        core = (flat ^ self.wide_at) & 1
        slot = ((flat & 1) << len(self.plane)) | self.slots(flat, self.plane, core)
        return slot * self.narrow + self.slots(deep, self.depth, core)


def summed(refs, kinds, second):
    refs, value = iter(refs), None
    for pair in kinds:
        part = next(refs)[...].astype(F32)
        if pair:
            part = jnp.where(second, next(refs)[...].astype(F32), part)
        value = part if value is None else value + part
    return value


def flat(parts):
    return [array for part in parts for array in (part if isinstance(part, tuple) else (part,))]


def combine_kernel(kinds, pieces, *refs):
    refs[-1][...] = summed(refs[:-1], kinds, pl.program_id(0) >= pieces).astype(BF)


def combine(parts, axis, first, count, deeps=None):
    pair = isinstance(parts[-1], tuple)
    block = list(parts[-1][0].shape if pair else parts[-1].shape)
    block[axis] = count
    out = tuple([2] + block[1:]) if pair else tuple(block)
    block[0] = 1
    if axis == 1:
        block[1] = 1
    pieces, begin = (count, first) if axis == 1 else (1, 0)
    place = lambda i, start, group, at=0: (group, start + i % pieces) + tuple(
        first // count if k == axis else at if k == 3 else 0 for k in range(2, len(block))
    )
    spec = pl.BlockSpec(tuple(block), lambda i: place(i, begin, i // pieces))
    pair_spec = pl.BlockSpec(tuple(block), lambda i: place(i, begin, 0))
    kinds = [isinstance(part, tuple) for part in parts]
    arrays = [far_memory(parts[0])] + flat(parts[1:])
    specs = [each for kind in kinds for each in ([pair_spec] * 2 if kind else [spec])]
    if deeps:
        specs = [pl.BlockSpec(tuple(block), lambda i, at=at: place(i, begin, i // pieces, at)) for at in deeps]
    return run(
        partial(combine_kernel, kinds, pieces),
        "combine",
        (out[0] * pieces,),
        list(zip(arrays, specs)),
        [(out, BF, pl.BlockSpec(tuple(block), lambda i: (i // pieces, i % pieces) + (0,) * (len(block) - 2)))],
        cost=(D * D, 4 * D * D, 0),
        mebibytes=16,
    )[0]


def finish_kernel(kinds, shards, *refs):
    count, value = len(kinds) + sum(kinds), None
    arrays = iter(refs)
    for pair in kinds:
        part = next(arrays)[...].astype(F32)
        if pair:
            part = jnp.concatenate([part, next(arrays)[...].astype(F32)], axis=0)
        value = part if value is None else value + part
    known, out, squares = refs[count : count + 3]
    out[...] = value
    square = value * value
    square = jnp.sum(square.reshape(-1, D), axis=0, keepdims=True)
    square = jnp.sum(square, axis=1, keepdims=True)
    if known.shape[0] == 1:
        square = square + known[0, :, 0:1]
    else:
        vector = known[0:3]
        for place in range(1, shards):
            vector = vector + known[3 * place : 3 * place + 3]
        refs[-1][...] = vector
        square = square + jnp.sum(jnp.sum(vector * vector, axis=0), axis=1, keepdims=True)
    squares[...] = jnp.broadcast_to(square.reshape(1, 1, 1), squares.shape)


def finish(parts, known, shards):
    shape = parts[-1].shape
    outs = [(shape, F32, whole(shape))]
    if known.shape[0] == 1:
        outs.append(((shards, 1, 128), F32, whole((shards, 1, 128))))
    else:
        outs += [((1, 1, 128), F32, whole((1, 1, 128))), ((3, 1, 128), F32, whole((3, 1, 128)))]
    return run(
        partial(finish_kernel, [isinstance(part, tuple) for part in parts], shards),
        "finish",
        (1,),
        [
            (array, whole((shape[0] // 2 if isinstance(part, tuple) else shape[0],) + shape[1:]))
            for part in parts
            for array in flat([part])
        ]
        + [(known, whole(known.shape))],
        outs,
        cost=(D * D, D * D, 0),
        mebibytes=12,
    )


def tie(array, *others):
    return lax.optimization_barrier((array,) + others)[0]


def vectors(width, owners, shares, table, bias):
    table[...] = jnp.zeros_like(table)
    count = D // width
    for row in range(NVEC // D):
        pieces = []
        for piece in range(row * count, (row + 1) * count):
            lane = 128 * (piece % 3)
            pieces.append(shares[piece // 3, :, lane : lane + 128][:, :width])
        table[row : row + 1, :] = jnp.concatenate(pieces, axis=1)
    count = D // 2 // width
    for place in range(bias.shape[0]):
        pieces = []
        for slot in range(place * count, (place + 1) * count):
            piece = owners[slot] + B1 * (D // width)
            lane = pl.multiple_of(piece % 3 * 128, 128)
            pieces.append(shares[piece // 3, :, pl.ds(lane, 128)][:, :width])
        bias[place] = jnp.concatenate(pieces, axis=1)


def attend_kernel(piece, width, order, owners, hidden_owners, length, x, meeting, *refs):
    parts, (packed, table, weight, context, log_totals, lines, bias, columns, shares, held) = refs[:-10], refs[-10:]
    step = power_of_two(piece)

    @pl.when(pl.program_id(0) == 0)
    def _():
        places = iter(order)
        for ref in parts:
            if len(ref.shape) == 3:
                for slot, owner in enumerate(order):
                    shares[hidden_owners[slot]] = ref[owner]
                continue
            for slot in range(ref.shape[0]):
                for deep in range(ref.shape[1]):
                    owner = owners[next(places)]
                    start = pl.multiple_of(owner * piece, step)
                    for which in range(4):
                        rows = ref[slot, deep, which * piece : (which + 1) * piece, :]
                        held[which, pl.ds(start, piece), :] = rows.astype(F32)
                    if ref.shape[2] > 4 * piece:
                        rows = ref[slot, deep, 4 * piece :, :].astype(F32)
                        shares[owner] = rows[0:1, : shares.shape[2]]
        vectors(width, hidden_owners, shares, lines, bias)
        columns[...] = lines[...].T

    rows = x[...]
    block = GROUP * HEAD_DIM
    span = pl.ds(pl.multiple_of(pl.program_id(0) * block, block), block)
    pieces = [held[which, span, :].astype(BF) for which in range(4)]
    for which in range(3):
        table[which] = pieces[which]
    weight[...] = pieces[3]
    queries = dot(pieces[0], rows, NT) + columns[span, BQ : BQ + 1]
    queries = (queries.astype(BF) * HEAD_DIM ** (-0.5)).astype(BF)
    keys = dot(pieces[1], rows, NT).astype(BF)
    values = (dot(pieces[2], rows, NT) + columns[span, BV : BV + 1]).astype(BF)
    packed[0], packed[1], packed[2] = queries, keys, values
    visible = lax.broadcasted_iota(jnp.int32, (LENGTH, LENGTH), 0) < length[0]
    spans = [slice(HEAD_DIM * head, HEAD_DIM * (head + 1)) for head in range(GROUP)]
    score = lambda head: dot(keys[spans[head]], queries[spans[head]], TN)
    following, done = score(0), []
    for head in range(GROUP):
        scores = jnp.where(visible, following, MASKED)
        if head + 1 < GROUP:
            following = score(head + 1)
        largest = jnp.max(scores, axis=0, keepdims=True)
        powers = jnp.exp(scores - largest)
        totals = jnp.sum(powers, axis=0, keepdims=True)
        done.append(dot(values[spans[head]], powers.astype(BF), NN) * (1.0 / totals))
        log_totals[0, head : head + 1, :] = largest + jnp.log(totals)
    context[...] = jnp.concatenate(done, axis=0).T.astype(BF)


def join_kernel(x, context, weight, table, unit_rows, factor, low, base):
    branch = dot(context[...], weight[...], NN) + table[BO : BO + 1, :]
    rows = x[...].astype(F32) + branch
    center = rows - mean(rows)
    spread = lax.rsqrt(mean(center * center) + EPSILON)
    normed = center * spread
    unit_rows[...] = normed
    factor[...] = spread
    shifted = normed * table[GA : GA + 1, :] + table[SA : SA + 1, :]
    low[...] = shifted.astype(BF)
    base[...] = shifted + table[B2 : B2 + 1, :]


def gelu_pair(value):
    power = jnp.exp(value * value * -0.5)
    part = 1.0 / (1.0 + jnp.abs(value) * (0.3275911 * 0.5**0.5))
    tail = 0.5 * 1.061405429
    for factor in (-1.453152027, 1.421413741, -0.284496736, 0.254829592):
        tail = tail * part + 0.5 * factor
    tail = tail * part * power
    chance = jnp.where(value < 0.0, tail, 1.0 - tail)
    return value * chance, chance + value * power * (2.0 * jnp.pi) ** -0.5


def joined(refs):
    return jnp.concatenate([ref[...].reshape(-1, D) for ref in refs], axis=0)


def ffn_forward_kernel(places, low, *refs):
    bias, start, active, slope, running = refs[8:]
    rows = low[...]
    expand, reduce = joined(refs[:4]), joined(refs[4:8])
    shift = jnp.concatenate([bias[places[0]], bias[places[1]]], axis=1)
    total = start[...]
    for first in range(0, D, SUB):
        span = slice(first, first + SUB)
        value, change = gelu_pair(dot(rows, expand[span], NT) + shift[:, span])
        value = value.astype(BF)
        active[:, span] = value
        slope[:, span] = change.astype(BF)
        total = total + dot(value, reduce[span], NN)
    running[...] = total


def loss_kernel(length, rows, cotangent, table, output, grad, grad_low, sums):
    tile = rows.shape[0]
    value = rows[...]
    center = value - mean(value)
    factor = lax.rsqrt(mean(center * center) + EPSILON)
    normed = center * factor
    gain = table[GB : GB + 1, :]
    output[...] = (normed * gain + table[SB : SB + 1, :]).astype(BF)
    place = pl.program_id(0) * tile + lax.broadcasted_iota(jnp.int32, (tile, 1), 0)
    upstream = jnp.where(place < length[0], cotangent[...].astype(F32), 0.0)
    scaled = upstream * gain
    change = factor * (scaled - mean(scaled) - normed * mean(scaled * normed))
    grad[...] = change
    change_low = change.astype(BF)
    grad_low[...] = change_low

    @pl.when(pl.program_id(0) == 0)
    def _():
        sums[...] = jnp.zeros_like(sums)

    sums[0:1, :] += jnp.sum(upstream * normed, axis=0, keepdims=True)
    sums[1:2, :] += jnp.sum(upstream, axis=0, keepdims=True)
    sums[2:3, :] += jnp.sum(change_low.astype(F32), axis=0, keepdims=True)


def by_slot(grads, which, result):
    _, slots, deep, width, _ = grads.shape
    quarter = slots // 2
    result = jnp.concatenate(result, axis=0).reshape(2, 2, quarter, deep // 2, width, D)
    for place in range(2):
        for side in range(2):
            into = slice(place * quarter, (place + 1) * quarter), slice(side * (deep // 2), (side + 1) * (deep // 2))
            grads[which, into[0], into[1]] = result[place, side]


def reduce_backward_kernel(grad_low, active_a, active_b, grads):
    active = jnp.concatenate([active_a[...], active_b[...]], axis=1)
    by_slot(grads, 0, [dot(active[:, first : first + SUB], grad_low[...], TN).astype(BF) for first in range(0, D, SUB)])


def ffn_backward_kernel(both, grad_low, low, slope_a, slope_b, *refs):
    actives, refs = (refs[:2], refs[2:]) if both else ((), refs)
    start, grads, grad_bias, running = refs[8:]
    upstream, rows = grad_low[...], low[...]
    expand, reduce = joined(refs[:4]), joined(refs[4:8])
    slope = jnp.concatenate([slope_a[...], slope_b[...]], axis=1)
    if both:
        active = jnp.concatenate([actives[0][...], actives[1][...]], axis=1)
    reduced, expanded = [], []
    total = start[...]
    for first in range(0, D, SUB):
        span = slice(first, first + SUB)
        if both:
            reduced.append(dot(active[:, span], upstream, TN).astype(BF))
        change = (dot(upstream, reduce[span], NT) * slope[:, span].astype(F32)).astype(BF)
        grad_bias[:, span] = jnp.sum(change.astype(F32), axis=0, keepdims=True)
        expanded.append(dot(change, rows, TN).astype(BF))
        total = total + dot(change, expand[span], NN)
    running[...] = total
    if both:
        by_slot(grads, 0, reduced)
    by_slot(grads, int(both), expanded)


def sums_kernel(width, owners, sums_in, sums_one, sums_two, *refs):
    biases, out = refs[:4], refs[4]
    out[...] = jnp.zeros_like(out)
    count = D // width
    rows = (
        (BQ, sums_in[0, 0:1]),
        (BV, sums_in[2, 0:1]),
        (BO, sums_one[2:3]),
        (GA, sums_one[0:1]),
        (SA, sums_one[1:2]),
        (B2, sums_two[2:3]),
        (GB, sums_two[0:1]),
        (SB, sums_two[1:2]),
    )
    for row, value in rows:
        for piece in range(count):
            out[row * count + piece, :, :width] = value[:, piece * width : (piece + 1) * width]
    for place, ref in enumerate(biases):
        value = ref[...]
        for piece in range(count):
            into = owners[place * count + piece] + B1 * count
            out[into, :, :width] = value[:, piece * width : (piece + 1) * width]


def branch_kernel(upstream, unit_rows, factor, context, weight, table, grad, grad_context, grad_weight, sums):
    value = upstream[...]
    normed = unit_rows[...]
    scaled = value * table[GA : GA + 1, :]
    change = factor[...] * (scaled - mean(scaled) - normed * mean(scaled * normed))
    grad[...] = change
    change_low = change.astype(BF)

    @pl.when(pl.program_id(0) == 0)
    def _():
        sums[...] = jnp.zeros_like(sums)
        grad_weight[...] = jnp.zeros_like(grad_weight)

    sums[0:1, :] += jnp.sum(value * normed, axis=0, keepdims=True)
    sums[1:2, :] += jnp.sum(value, axis=0, keepdims=True)
    sums[2:3, :] += jnp.sum(change_low.astype(F32), axis=0, keepdims=True)
    grad_context[...] = dot(weight[...], change_low, NT).astype(BF)
    grad_weight[...] += dot(context[...], change_low, TN)


def attend_backward_kernel(count, *refs):
    length, packed, grad_context, log_totals, out = refs[count:]
    visible = lax.broadcasted_iota(jnp.int32, (LENGTH, LENGTH), 0) < length[0]
    spans = [slice(HEAD_DIM * head, HEAD_DIM * (head + 1)) for head in range(GROUP)]

    def score(head):
        span = spans[head]
        return dot(packed[1, span, :], packed[0, span, :], TN), dot(packed[2, span, :], grad_context[span, :], TN)

    following = score(0)
    for head in range(GROUP):
        span = spans[head]
        scores, grad_chances = following
        if head + 1 < GROUP:
            following = score(head + 1)
        chances = jnp.where(visible, jnp.exp(scores - log_totals[0, head : head + 1, :]), 0.0)
        out[2, span, :] = dot(grad_context[span, :], chances.astype(BF), NT).astype(BF)
        inner = jnp.sum(chances * grad_chances, axis=0, keepdims=True)
        grad_scores = (chances * (grad_chances - inner)).astype(BF)
        out[1, span, :] = dot(packed[0, span, :], grad_scores, NT).astype(BF)
        out[0, span, :] = (dot(packed[1, span, :], grad_scores, NN) * HEAD_DIM ** (-0.5)).astype(BF)


def in_grads_kernel(piece, owners, grads, x, grad_out, *refs):
    outs, (sums, held) = refs[:4], refs[4:]
    step = power_of_two(piece)
    which = pl.program_id(0)
    slots, rows = outs[0].shape[1], outs[0].shape[2] // 4

    def place(source, at):
        for side, ref in enumerate(outs):
            for slot in range(slots):
                for first in range(0, rows, piece):
                    index = ((side * slots + slot) * rows + first) // piece
                    start = pl.multiple_of(owners[index] * piece, step)
                    into = slice(at * rows + first, at * rows + first + piece)
                    ref[0, slot, into, :] = source[pl.ds(start, piece), :].astype(BF)

    held[...] = dot(grads[0], x[...], NN)
    sums[0] = dot(jnp.ones((8, LENGTH), BF), grads[0], NT)
    for at in range(3):
        pl.when(which == at)(partial(place, held, at))

    @pl.when(which == 0)
    def _():
        place(grad_out, 3)


def input_grad_kernel(grads, weights, residual, out):
    value = residual[...]
    for which in range(3):
        value = value + dot(grads[which], weights[which], TN)
    out[...] = value.astype(BF)


BLEND = min(0.999, (1 + STEP) / (10 + STEP))
RATES = (RATE_MATRIX, RATE_PROJECTION, RATE_MATRIX, RATE_MATRIX)


def advance(weight, velocity, average, gradient, factor, rate):
    clipped = gradient * factor
    velocity = MOMENTUM * velocity + clipped
    weight = weight - rate * (clipped + MOMENTUM * velocity)
    return weight, velocity, BLEND * average + (1.0 - BLEND) * weight


def update_kernel(squares, near, hidden, *refs):
    states, outs = refs[:12], refs[12:]
    value = squares[...]
    norm = jnp.sqrt(jnp.sum(value, axis=0)[:, 0:1])
    factor = 1.0 / jnp.maximum(norm, 1.0)
    outs[12][...] = norm
    gradients = (near[:3], near[3], hidden[1], hidden[0])
    for at, (gradient, rate) in enumerate(zip(gradients, RATES)):
        weight, velocity, average = states[at][...], states[4 + at][...], states[8 + at][...]
        results = advance(weight, velocity, average, gradient, factor, rate)
        for place, result in enumerate(results):
            outs[4 * place + at][...] = result


def body(
    wide,
    narrow,
    layer_input,
    cotangent,
    lengths,
    attention_in,
    attention_out,
    expand_weight,
    reduce_weight,
    vector_params,
    velocity_in,
    velocity_out,
    velocity_expand,
    velocity_reduce,
    velocity_vector,
    average_in,
    average_out,
    average_expand,
    average_reduce,
    average_vector,
):
    cube = Cube(wide, narrow)
    shards = wide * narrow
    share, width, spare = D // shards, FF // shards, NVEC // shards
    unit = share * narrow
    half = wide // 4
    groups = FF // D
    last = len(cube.plane) - 1
    owners = cube.plane_owners()
    held_kind = BF if unit % 16 == 0 else F32

    quarter, deep = half // 2, narrow // 2
    all_owners = cube.all_owners(jnp.arange(shards, dtype=jnp.int32))
    aligned = share % 8 == 0
    near = jnp.concatenate([attention_in.astype(BF).transpose(0, 2, 1).reshape(3 * share, D), attention_out.astype(BF)])
    vector = jnp.pad(vector_params.astype(BF).reshape(3, width), ((0, 0), (0, 128 - width))).reshape(1, 3 * 128)
    near = jnp.concatenate([near, jnp.pad(vector, ((0, 7), (0, D - 3 * 128)))]).reshape(1, 1, 4 * share + 8, D)
    hidden = jnp.stack([expand_weight.astype(BF).T, reduce_weight.astype(BF)]).reshape(1, 2, 1, width, D)
    final = len(cube.depth) - 1

    def early_slots(slots, axis):
        for step in range(final):
            slots = jnp.concatenate([slots, cube.swap_depth(slots, step)], axis=axis)
        return slots

    def plane_quarter(slots):
        for step in range(last - 1):
            slots = jnp.concatenate([slots, cube.swap_plane(slots, step)])
        return slots

    early = early_slots(near, 1)
    late = cube.swap_depth(early, final)
    hidden_early = early_slots(tie(hidden, late), 2)
    early, late = plane_quarter(early), plane_quarter(late)
    next_early, far_early = cube.swap_plane(early, last - 1), cube.swap_plane(early, last)
    late, next_early, far_early = lax.optimization_barrier((late, next_early, far_early))
    next_late, far_late = cube.swap_plane(late, last - 1), cube.swap_plane(late, last)
    beyond_early = cube.swap_plane(next_early, last)
    meeting = cube.swap_core(hidden_early[0, 0, deep - 1, :8, :128])
    hidden_early, meeting = lax.optimization_barrier((hidden_early, meeting))
    hidden_late = cube.swap_depth(hidden_early, final)
    next_late, beyond_early, far_late, hidden_early = lax.optimization_barrier(
        (next_late, beyond_early, far_late, hidden_early)
    )
    beyond_late = cube.swap_plane(next_late, last)
    hidden_early = plane_quarter(hidden_early)
    hidden_next_early, hidden_far_early = (cube.swap_plane(hidden_early, last - 1), cube.swap_plane(hidden_early, last))
    beyond_late, hidden_late, hidden_next_early = lax.optimization_barrier(
        (beyond_late, hidden_late, hidden_next_early)
    )
    hidden_late = plane_quarter(hidden_late)
    hidden_next_late, hidden_far_late = cube.swap_plane(hidden_late, last - 1), cube.swap_plane(hidden_late, last)
    attention = [early, late, next_early, next_late, far_early, far_late, beyond_early, beyond_late]
    attention += [cube.swap_core(part) for part in attention]
    order = [
        (place * quarter + slot) * narrow + side * deep + k
        for place in range(8)
        for side in range(2)
        for slot in range(quarter)
        for k in range(deep)
    ]
    hidden_owners = cube.all_owners(jnp.array(order, jnp.int32))
    pieces, piece, piece_order, piece_owners = attention, share, order, all_owners
    if not aligned:
        pieces, shares = [], []
        for place in range(8):
            part = jnp.concatenate(attention[2 * place : 2 * place + 2], axis=1)
            shares.append(part[:, :, 4 * share, : 3 * 128].reshape(-1, 1, 3 * 128).astype(F32))
            part = jnp.take(part[:, :, : 4 * share], cube.depth_slots(place // 4), axis=1)
            part = part.reshape(quarter, narrow, 4, share, D).transpose(0, 2, 1, 3, 4)
            pieces.append(part.reshape(quarter, 1, 4 * unit, D))
        pieces.append(jnp.concatenate(shares))
        piece, piece_order, piece_owners = unit, list(range(wide)), owners

    group_spec = pl.BlockSpec((3, GROUP * HEAD_DIM, LENGTH), lambda j: (0, j, 0))
    log_spec = pl.BlockSpec((1, GROUP, LENGTH), lambda j: (j, 0, 0))
    packed, weights_in, weight_out, context, log_totals, table, bias = run(
        partial(attend_kernel, piece, width, piece_order),
        "attend",
        (STEPS,),
        [(piece_owners, SMEM), (hidden_owners, SMEM), (lengths, SMEM)]
        + [(far_memory(layer_input), whole((LENGTH, D))), (meeting, ANY)]
        + [(far_memory(part), whole(part.shape)) for part in pieces],
        [
            (pltpu.HBM((3, D, LENGTH), BF), None, group_spec),
            (pltpu.HBM((3, D, D), BF), None, pl.BlockSpec((3, GROUP * HEAD_DIM, D), lambda j: (0, j, 0))),
            (pltpu.HBM((D, D), BF), None, pl.BlockSpec((GROUP * HEAD_DIM, D), lambda j: (j, 0))),
            ((LENGTH, D), BF, pl.BlockSpec((LENGTH, GROUP * HEAD_DIM), lambda j: (0, j))),
            ((STEPS, GROUP, LENGTH), F32, log_spec),
            ((16, D), F32, whole((16, D))),
            ((8, 1, D // 2), F32, whole((8, 1, D // 2))),
        ],
        scratch=[pltpu.VMEM((D, 16), F32), pltpu.VMEM((shards, 1, 3 * 128), F32), pltpu.VMEM((4, D, D), F32)],
        cost=(10 * D * D * LENGTH, 24 * D * D, HEADS * LENGTH * LENGTH),
        mebibytes=36,
    )
    context, hidden_next_early, hidden_next_late = lax.optimization_barrier((context, hidden_next_early, hidden_next_late))
    hidden = [
        (hidden_early, hidden_late),
        (hidden_next_early, hidden_next_late),
        (hidden_far_early, hidden_far_late),
        (cube.swap_plane(hidden_next_early, last), cube.swap_plane(hidden_next_late, last)),
    ]
    swap_both = lambda parts: tuple(cube.swap_core(part) for part in parts)
    hidden += [swap_both(hidden[0]), swap_both(hidden[1])]
    tile = 256
    row_spec = pl.BlockSpec((tile, D), lambda i: (i, 0))
    one_spec = pl.BlockSpec((tile, 1), lambda i: (i, 0))
    table_spec = whole((16, D))
    unit_rows, factor_one, low, running = run(
        join_kernel,
        "join",
        (LENGTH // tile,),
        [
            (layer_input, row_spec),
            (context, row_spec),
            (far_memory(weight_out), whole((D, D))),
            (table, table_spec),
        ],
        [
            ((LENGTH, D), F32, row_spec),
            ((LENGTH, 1), F32, one_spec),
            ((LENGTH, D), BF, row_spec),
            ((LENGTH, D), F32, row_spec),
        ],
        cost=(2 * D * D * LENGTH, 14 * LENGTH * D, 0),
        mebibytes=16,
    )

    rows_spec = pl.BlockSpec(memory_space=pltpu.VMEM)
    hidden_spec = lambda which: pl.BlockSpec((quarter, 1, deep, width, D), lambda *i: (0, which, 0, 0, 0))
    hidden_ins = lambda first, second: [
        (part, hidden_spec(which)) for which in range(2) for place in (first, second) for part in hidden[place]
    ]

    def forward(first, second, running):
        return run(
            partial(ffn_forward_kernel, (first, second)),
            "expand",
            (1,),
            [
                (low, rows_spec),
                *hidden_ins(first, second),
                (bias, whole((8, 1, D // 2))),
                (running, rows_spec),
            ],
            [
                (pltpu.HBM((LENGTH, D), BF), None, whole((LENGTH, D))),
                (pltpu.HBM((LENGTH, D), BF), None, whole((LENGTH, D))),
                ((LENGTH, D), F32, rows_spec),
            ],
            cost=(4 * D * D * LENGTH, 4 * D * D + 12 * LENGTH * D, 2 * LENGTH * D),
        )

    stored = [None] * 8
    for first, second in ((0, 1), (4, 5), (2, 6), (3, 7)):
        if first == 4:
            hidden[2] = lax.optimization_barrier((*hidden[2], running))[:2]
            hidden += [swap_both(hidden[2])]
        if first == 2:
            beyond_early, beyond_late, running = lax.optimization_barrier((*hidden[3], running))
            hidden[3] = beyond_early, beyond_late
            hidden += [swap_both(hidden[3])]
        active, slope, running = forward(first, second, running)
        stored[first] = (active, slope, 0)
        stored[second] = (active, slope, 1)
    sum_spec = whole((8, D))
    output, grad_two, grad_low, sums_two = run(
        loss_kernel,
        "loss",
        (LENGTH // tile,),
        [(lengths, SMEM), (running, row_spec), (cotangent, row_spec), (table, table_spec)],
        [
            ((LENGTH, D), BF, row_spec),
            ((LENGTH, D), F32, row_spec),
            ((LENGTH, D), BF, row_spec),
            (pltpu.HBM((8, D), F32), None, sum_spec),
        ],
        cost=(40 * LENGTH * D, 14 * LENGTH * D, 0),
    )
    column = lambda place: pl.BlockSpec((LENGTH, D // 2), lambda *i: (0, stored[place][2]))

    def reduce_backward(first):
        shape = (1, half, narrow, width, D)
        return run(
            reduce_backward_kernel,
            "reduce_back",
            (1,),
            [(grad_low, rows_spec)] + [(stored[place][0], column(place)) for place in (first, first + 1)],
            [(pltpu.HBM(shape, BF), None, whole(shape))],
            cost=(2 * D * D * LENGTH, 2 * D * D + 4 * LENGTH * D, 0),
        )[0]

    def backward(both, first, running):
        shape = (1 + both, half, narrow, width, D)
        return run(
            partial(ffn_backward_kernel, both),
            "expand_back",
            (1,),
            [(grad_low, rows_spec), (low, rows_spec)]
            + [(stored[place][1], column(place)) for place in (first, first + 1)]
            + [(stored[place][0], column(place)) for place in (first, first + 1) if both]
            + hidden_ins(first, first + 1)
            + [(running, rows_spec)],
            [
                (pltpu.HBM(shape, BF), None, whole(shape)),
                ((1, D), F32, whole((1, D))),
                ((LENGTH, D), F32, rows_spec),
            ],
            cost=(8 * D * D * LENGTH, 8 * D * D + 12 * LENGTH * D, 0),
        )

    other_reduce = cube.swap_core(reduce_backward(6))
    own_reduce = reduce_backward(2)
    leaving_reduce = combine([own_reduce, other_reduce], 1, 0, half)
    arrived_reduce = cube.swap_plane(leaving_reduce, last)
    grad_two = tie(grad_two, leaving_reduce)
    other_expand, bias_6, running = backward(False, 6, grad_two)
    other_expand = cube.swap_core(other_expand)
    own_expand, bias_2, running = backward(False, 2, running)
    leaving_expand = combine([own_expand, other_expand], 1, 0, half)
    arrived_expand = cube.swap_plane(leaving_expand, last)
    other_near, bias_4, running = backward(True, 4, tie(running, leaving_expand))
    other_near = cube.swap_core(other_near)
    own_near, bias_0, running = backward(True, 0, running)
    hidden_parts = [own_near, tie(other_near, running), (arrived_reduce, arrived_expand)]

    grad_one, grad_context, grad_out, sums_one = run(
        branch_kernel,
        "branch_back",
        (LENGTH // tile,),
        [
            (running, row_spec),
            (unit_rows, row_spec),
            (factor_one, one_spec),
            (context, row_spec),
            (weight_out, whole((D, D))),
            (table, table_spec),
        ],
        [
            (pltpu.HBM((LENGTH, D), F32), None, row_spec),
            ((D, LENGTH), BF, pl.BlockSpec((D, tile), lambda i: (0, i))),
            ((D, D), F32, whole((D, D))),
            (pltpu.HBM((8, D), F32), None, sum_spec),
        ],
        cost=(4 * D * D * LENGTH, 8 * D * D + 16 * LENGTH * D, 0),
    )
    def attend_backward(first, steps, grad_context, *before):
        place = lambda j: (0, j + first, 0)
        block = (3, GROUP * HEAD_DIM, LENGTH)
        return run(
            partial(attend_backward_kernel, len(before)),
            "attend_back",
            (steps,),
            [(array, ANY) for array in before]
            + [
                (lengths, SMEM),
                (packed, pl.BlockSpec(block, place)),
                (grad_context, pl.BlockSpec((GROUP * HEAD_DIM, LENGTH), lambda j: (j + first, 0))),
                (log_totals, pl.BlockSpec((1, GROUP, LENGTH), lambda j: (j + first, 0, 0))),
            ],
            [((3, D, LENGTH), BF, pl.BlockSpec(block, place))],
            cost=(10 * HEADS * LENGTH * LENGTH * HEAD_DIM, 14 * LENGTH * D, HEADS * LENGTH * LENGTH),
            alias={0: 0} if before else None,
        )[0]

    def send(parts, axis):
        middle = flat(parts[-1:])[0].shape[axis] // 2
        return combine(parts, axis, middle, middle)

    grads = attend_backward(0, STEPS - 1, grad_context)
    hidden_parts[0] = tie(hidden_parts[0], grads)
    hidden_leaving = send(hidden_parts, 1)
    grads = attend_backward(STEPS - 1, 1, tie(grad_context, hidden_leaving), grads)
    hidden_parts.append(cube.swap_plane(hidden_leaving, last - 1))
    chunk = (1, half, 4 * unit, D)
    *chunks, sums_in = run(
        partial(in_grads_kernel, share if aligned else unit),
        "project_back",
        (3,),
        [
            (all_owners if aligned else owners, SMEM),
            (grads, pl.BlockSpec((1, D, LENGTH), lambda i: (i, 0, 0))),
            (layer_input, whole((LENGTH, D))),
            (grad_out, whole((D, D))),
        ],
        [(pltpu.HBM(chunk, BF), None, whole(chunk))] * 4
        + [((3, 8, D), F32, pl.BlockSpec((1, 8, D), lambda i: (i, 0, 0)))],
        scratch=[pltpu.VMEM((D, D), F32)],
        cost=(6 * D * D * LENGTH, 12 * D * D, 0),
        mebibytes=32,
    )
    if not aligned:
        for place, part in enumerate(chunks):
            order = cube.depth_owners(place // 2)
            part = jnp.take(part.reshape(half, 4, narrow, share, D), order, axis=2)
            chunks[place] = part.reshape(chunk)
    own_near, own_far, other_near, other_far = chunks
    other_far, other_near = cube.swap_core(other_far), cube.swap_core(other_near)
    (grad_vector,) = run(
        partial(sums_kernel, width),
        "sums",
        (1,),
        [
            (hidden_owners, SMEM),
            (sums_in, whole((3, 8, D))),
            (sums_one, sum_spec),
            (sums_two, sum_spec),
        ]
        + [(part, whole((1, D))) for part in (bias_0, bias_2, bias_4, bias_6)],
        [((3 * shards, 1, 128), F32, whole((3 * shards, 1, 128)))],
        mebibytes=8,
    )
    own_far, hidden_parts[-1] = lax.optimization_barrier((own_far, hidden_parts[-1]))
    for step in reversed(range(last - 1)):
        hidden_parts.append(cube.swap_plane(send(hidden_parts, 1), step))
    view = lambda part: part.reshape(1, half, 4, narrow, share, D)
    own_near, own_far, other_near, other_far = (view(part) for part in (own_near, own_far, other_near, other_far))
    late = cube.swap_plane(combine([own_far, other_far], 3, deep, deep), last)
    early = cube.swap_plane(combine([own_far, other_far], 3, 0, deep), last)
    hidden_going = send(hidden_parts, 2)
    grads = tie(grads, hidden_going)
    (input_grad,) = run(
        input_grad_kernel,
        "input_back",
        (LENGTH // tile,),
        [
            (grads, pl.BlockSpec((3, D, tile), lambda i: (0, 0, i))),
            (far_memory(weights_in), whole((3, D, D))),
            (far_memory(grad_one), row_spec),
        ],
        [((LENGTH, D), BF, row_spec)],
        cost=(6 * D * D * LENGTH, 6 * D * D + 12 * LENGTH * D, 0),
    )
    late, input_grad = lax.optimization_barrier((late, input_grad))
    hidden_parts.append(cube.swap_depth(hidden_going, final))
    late_parts, early_parts = [own_near, other_near, late], [own_near, other_near, early]
    late_deeps = [1, 1, 0]
    for step in reversed(range(last)):
        middle = late_parts[-1].shape[1] // 2
        late_parts.append(cube.swap_plane(combine(late_parts, 1, middle, middle, late_deeps), step))
        late_deeps.append(0)
        early_parts.append(cube.swap_plane(combine(early_parts, 1, middle, middle, [0] * len(early_parts)), step))
    going = combine(late_parts, 1, 0, 1, late_deeps)
    early_parts.append(cube.swap_depth(going, final))
    grad_vector = lax.all_to_all(tie(grad_vector, going), AXES, 0, 0, tiled=True)
    early_parts[-1], grad_vector = lax.optimization_barrier((early_parts[-1], grad_vector))
    for step in reversed(range(final)):
        early_parts.append(cube.swap_depth(send(early_parts, 3), step))
        hidden_parts.append(cube.swap_depth(send(hidden_parts, 2), step))
    parts = early_parts
    owned_hidden, squares, owned_vector = finish(hidden_parts, grad_vector, shards)
    owned_near, squares = finish(parts, squares, shards)
    squares = lax.all_to_all(squares, AXES, 0, 0)

    turn = lambda array: array.transpose(*range(array.ndim - 2), -1, -2)
    states = []
    for first, second, third, fourth in (
        (attention_in, attention_out, expand_weight, reduce_weight),
        (velocity_in, velocity_out, velocity_expand, velocity_reduce),
        (average_in, average_out, average_expand, average_reduce),
    ):
        states += [turn(first), second, turn(third), fourth]
    near, hidden = owned_near.reshape(4, share, D), owned_hidden.reshape(2, width, D)
    vector = owned_vector[:, 0, :width].reshape(spare)
    *states, grad_norm = run(
        update_kernel,
        "update",
        (1,),
        [(squares, whole(squares.shape)), (near, whole(near.shape))]
        + [(far_memory(array), whole(array.shape)) for array in [hidden] + states],
        [(array.shape, F32, whole(array.shape)) for array in states] + [((1, 1), F32, whole((1, 1)))],
        cost=(FF * D, 28 * (share * 4 + width * 2) * D, 0),
    )
    grad_norm = grad_norm.reshape(())
    vectors = advance(
        vector_params, velocity_vector, average_vector, vector, 1.0 / jnp.maximum(grad_norm, 1.0), RATE_VECTOR
    )
    outs = []
    for place in range(3):
        first, second, third, fourth = states[4 * place : 4 * place + 4]
        outs += [turn(first), second, turn(third), fourth, vectors[place]]
    return (output, input_grad, *outs, grad_norm)


def solution(mesh):
    both = ("wide", "narrow")
    first, second, third = P(both, None), P(None, both), P(None, None, both)
    state = (third, first, second, first, P(both))
    return jax.shard_map(
        partial(body, mesh.shape["wide"], mesh.shape["narrow"]),
        mesh=mesh,
        in_specs=(first, first, P(both)) + state * 3,
        out_specs=(first, first) + state * 3 + (P(),),
        check_vma=False,
    )
```

```python
from functools import partial

import jax
import jax.numpy as jnp
from jax import lax
from jax.experimental import pallas as pl
from jax.experimental.pallas import tpu as pltpu
from jax.sharding import PartitionSpec as P

D = 768
FF = 3072
HEADS = 12
HEAD_DIM = 64
LENGTH = 512
STEP = 10
NVEC = 8 * D + FF
GROUP = 4
STEPS = HEADS // GROUP
SUB = 768

MOMENTUM = 0.9
RATE_MATRIX = 24.0
RATE_PROJECTION = 160.0
RATE_VECTOR = 256.0
EPSILON = 1e-05
MASKED = -1000000000.0

AXES = ("wide", "narrow")
BF = jnp.bfloat16
F32 = jnp.float32
NN = ((1,), (0,))
NT = ((1,), (1,))
TN = ((0,), (0,))

BQ, BV, BO, GA, SA, B1, B2, GB, SB = 0, 1, 2, 3, 4, 5, 9, 10, 11


def dot(left, right, dims):
    return lax.dot_general(left, right, (dims, ((), ())), preferred_element_type=F32)


def mean(rows):
    return jnp.sum(rows, axis=-1, keepdims=True) * (1.0 / D)


def power_of_two(number):
    return number & -number


SMEM = pl.BlockSpec(memory_space=pltpu.SMEM)
ANY = pl.BlockSpec(memory_space=pl.ANY)


def run(kernel, name, grid, ins, outs, scratch=(), cost=(0, 0, 0), mebibytes=24, alias=None):
    scale = 8 if name.endswith("_back") and name != "input_back" else 1
    return pl.pallas_call(
        kernel,
        grid=grid,
        in_specs=[spec for _, spec in ins],
        out_specs=[spec for _, _, spec in outs],
        out_shape=[jax.ShapeDtypeStruct(shape, kind) if kind else shape for shape, kind, _ in outs],
        scratch_shapes=scratch,
        input_output_aliases=alias or {},
        compiler_params=pltpu.CompilerParams(
            vmem_limit_bytes=mebibytes * 1024 * 1024, dimension_semantics=("arbitrary",) * len(grid)
        ),
        cost_estimate=pl.CostEstimate(flops=scale * cost[0], bytes_accessed=scale * cost[1], transcendentals=cost[2]),
        name=name,
    )(*[array for array, _ in ins])


def far_memory(array):
    return pltpu.with_memory_space_constraint(array, pltpu.HBM)


def whole(shape):
    return pl.BlockSpec(shape, lambda *i: (0,) * len(shape))


class Cube:
    def __init__(self, wide, narrow):
        self.wide, self.narrow = wide, narrow
        wide_bits, narrow_bits = wide.bit_length() - 1, narrow.bit_length() - 1
        plane = list(range(1, wide_bits))
        half = len(plane) // 2
        swapped = plane[half:] + plane[:half] if len(plane) % 2 == 0 else plane
        depth = list(range(narrow_bits))
        self.depth = list(zip(reversed(depth), depth))
        self.plane = list(zip(plane, swapped))
        self.wide_at = lax.axis_index("wide")
        self.narrow_at = lax.axis_index("narrow")

    def swap_depth(self, array, step):
        place = lambda w, n: w * self.narrow + n
        pairs = [
            (place(w, n), place(w, n ^ (1 << self.depth[step][w & 1])))
            for w in range(self.wide)
            for n in range(self.narrow)
        ]
        return lax.ppermute(array, AXES, pairs)

    def swap_plane(self, array, step):
        pairs = [(i, i ^ (1 << self.plane[step][i & 1])) for i in range(self.wide)]
        return lax.ppermute(array, "wide", pairs)

    def swap_core(self, array):
        return lax.ppermute(array, "wide", [(i, i ^ 1) for i in range(self.wide)])

    def slots(self, apart, bits, core):
        def placed(which):
            slot = jnp.zeros_like(apart)
            for position, pair in enumerate(bits):
                slot = slot | (((apart >> pair[which]) & 1) << position)
            return slot

        return jnp.where(core == 0, placed(0), placed(1))

    def owners(self, slot, bits, core):
        def placed(which):
            apart = jnp.zeros_like(slot)
            for position, pair in enumerate(bits):
                apart = apart | (((slot >> position) & 1) << pair[which])
            return apart

        return jnp.where(core == 0, placed(0), placed(1))

    def plane_owners(self):
        slot = jnp.arange(self.wide, dtype=jnp.int32)
        other = slot >> len(self.plane)
        return (other | self.owners(slot, self.plane, other ^ (self.wide_at & 1))) ^ self.wide_at

    def depth_slots(self, other):
        place = jnp.arange(self.narrow, dtype=jnp.int32)
        return self.slots(place ^ self.narrow_at, self.depth, (self.wide_at & 1) ^ other)

    def depth_owners(self, other):
        core = (self.wide_at & 1) ^ other
        return self.owners(jnp.arange(self.narrow, dtype=jnp.int32), self.depth, core) ^ self.narrow_at

    def all_owners(self, slot):
        deep, flat = slot % self.narrow, slot // self.narrow
        other = flat >> len(self.plane)
        core = other ^ (self.wide_at & 1)
        wide_place = (other | self.owners(flat, self.plane, core)) ^ self.wide_at
        return wide_place * self.narrow + (self.owners(deep, self.depth, core) ^ self.narrow_at)

    def all_slots(self):
        place = jnp.arange(self.wide * self.narrow, dtype=jnp.int32)
        flat, deep = (place // self.narrow) ^ self.wide_at, (place % self.narrow) ^ self.narrow_at
        core = (flat ^ self.wide_at) & 1
        slot = ((flat & 1) << len(self.plane)) | self.slots(flat, self.plane, core)
        return slot * self.narrow + self.slots(deep, self.depth, core)


def summed(refs, kinds, second):
    refs, value = iter(refs), None
    for pair in kinds:
        part = next(refs)[...].astype(F32)
        if pair:
            part = jnp.where(second, next(refs)[...].astype(F32), part)
        value = part if value is None else value + part
    return value


def flat(parts):
    return [array for part in parts for array in (part if isinstance(part, tuple) else (part,))]


def combine_kernel(kinds, pieces, *refs):
    refs[-1][...] = summed(refs[:-1], kinds, pl.program_id(0) >= pieces).astype(BF)


def combine(parts, axis, first, count, deeps=None):
    pair = isinstance(parts[-1], tuple)
    block = list(parts[-1][0].shape if pair else parts[-1].shape)
    block[axis] = count
    out = tuple([2] + block[1:]) if pair else tuple(block)
    block[0] = 1
    if axis == 1:
        block[1] = 1
    pieces, begin = (count, first) if axis == 1 else (1, 0)
    place = lambda i, start, group, at=0: (group, start + i % pieces) + tuple(
        first // count if k == axis else at if k == 3 else 0 for k in range(2, len(block))
    )
    spec = pl.BlockSpec(tuple(block), lambda i: place(i, begin, i // pieces))
    pair_spec = pl.BlockSpec(tuple(block), lambda i: place(i, begin, 0))
    kinds = [isinstance(part, tuple) for part in parts]
    arrays = [far_memory(parts[0])] + flat(parts[1:])
    specs = [each for kind in kinds for each in ([pair_spec] * 2 if kind else [spec])]
    if deeps:
        specs = [pl.BlockSpec(tuple(block), lambda i, at=at: place(i, begin, i // pieces, at)) for at in deeps]
    return run(
        partial(combine_kernel, kinds, pieces),
        "combine",
        (out[0] * pieces,),
        list(zip(arrays, specs)),
        [(out, BF, pl.BlockSpec(tuple(block), lambda i: (i // pieces, i % pieces) + (0,) * (len(block) - 2)))],
        cost=(D * D, 4 * D * D, 0),
        mebibytes=16,
    )[0]


def finish_kernel(kinds, shards, *refs):
    count, value = len(kinds) + sum(kinds), None
    arrays = iter(refs)
    for pair in kinds:
        part = next(arrays)[...].astype(F32)
        if pair:
            part = jnp.concatenate([part, next(arrays)[...].astype(F32)], axis=0)
        value = part if value is None else value + part
    known, out, squares = refs[count : count + 3]
    out[...] = value
    square = value * value
    square = jnp.sum(square.reshape(-1, D), axis=0, keepdims=True)
    square = jnp.sum(square, axis=1, keepdims=True)
    if known.shape[0] == 1:
        square = square + known[0, :, 0:1]
    else:
        vector = known[0:3]
        for place in range(1, shards):
            vector = vector + known[3 * place : 3 * place + 3]
        refs[-1][...] = vector
        square = square + jnp.sum(jnp.sum(vector * vector, axis=0), axis=1, keepdims=True)
    squares[...] = jnp.broadcast_to(square.reshape(1, 1, 1), squares.shape)


def finish(parts, known, shards):
    shape = parts[-1].shape
    outs = [(shape, F32, whole(shape))]
    if known.shape[0] == 1:
        outs.append(((shards, 1, 128), F32, whole((shards, 1, 128))))
    else:
        outs += [((1, 1, 128), F32, whole((1, 1, 128))), ((3, 1, 128), F32, whole((3, 1, 128)))]
    return run(
        partial(finish_kernel, [isinstance(part, tuple) for part in parts], shards),
        "finish",
        (1,),
        [
            (array, whole((shape[0] // 2 if isinstance(part, tuple) else shape[0],) + shape[1:]))
            for part in parts
            for array in flat([part])
        ]
        + [(known, whole(known.shape))],
        outs,
        cost=(D * D, D * D, 0),
        mebibytes=12,
    )


def tie(array, *others):
    return lax.optimization_barrier((array,) + others)[0]


def vectors(width, owners, shares, table, bias):
    table[...] = jnp.zeros_like(table)
    count = D // width
    for row in range(NVEC // D):
        pieces = []
        for piece in range(row * count, (row + 1) * count):
            lane = 128 * (piece % 3)
            pieces.append(shares[piece // 3, :, lane : lane + 128][:, :width])
        table[row : row + 1, :] = jnp.concatenate(pieces, axis=1)
    count = D // 2 // width
    for place in range(bias.shape[0]):
        pieces = []
        for slot in range(place * count, (place + 1) * count):
            piece = owners[slot] + B1 * (D // width)
            lane = pl.multiple_of(piece % 3 * 128, 128)
            pieces.append(shares[piece // 3, :, pl.ds(lane, 128)][:, :width])
        bias[place] = jnp.concatenate(pieces, axis=1)


def attend_kernel(piece, width, order, owners, hidden_owners, length, x, meeting, *refs):
    parts, (packed, table, weight, context, log_totals, lines, bias, columns, shares, held) = refs[:-10], refs[-10:]
    step = power_of_two(piece)

    @pl.when(pl.program_id(0) == 0)
    def _():
        places = iter(order)
        for ref in parts:
            if len(ref.shape) == 3:
                for slot, owner in enumerate(order):
                    shares[hidden_owners[slot]] = ref[owner]
                continue
            for slot in range(ref.shape[0]):
                for deep in range(ref.shape[1]):
                    owner = owners[next(places)]
                    start = pl.multiple_of(owner * piece, step)
                    for which in range(4):
                        rows = ref[slot, deep, which * piece : (which + 1) * piece, :]
                        held[which, pl.ds(start, piece), :] = rows.astype(F32)
                    if ref.shape[2] > 4 * piece:
                        rows = ref[slot, deep, 4 * piece :, :].astype(F32)
                        shares[owner] = rows[0:1, : shares.shape[2]]
        vectors(width, hidden_owners, shares, lines, bias)
        columns[...] = lines[...].T

    rows = x[...]
    block = GROUP * HEAD_DIM
    span = pl.ds(pl.multiple_of(pl.program_id(0) * block, block), block)
    pieces = [held[which, span, :].astype(BF) for which in range(4)]
    for which in range(3):
        table[which] = pieces[which]
    weight[...] = pieces[3]
    queries = dot(pieces[0], rows, NT) + columns[span, BQ : BQ + 1]
    queries = (queries.astype(BF) * HEAD_DIM ** (-0.5)).astype(BF)
    keys = dot(pieces[1], rows, NT).astype(BF)
    values = (dot(pieces[2], rows, NT) + columns[span, BV : BV + 1]).astype(BF)
    packed[0], packed[1], packed[2] = queries, keys, values
    visible = lax.broadcasted_iota(jnp.int32, (LENGTH, LENGTH), 0) < length[0]
    spans = [slice(HEAD_DIM * head, HEAD_DIM * (head + 1)) for head in range(GROUP)]
    score = lambda head: dot(keys[spans[head]], queries[spans[head]], TN)
    following, done = score(0), []
    for head in range(GROUP):
        scores = jnp.where(visible, following, MASKED)
        if head + 1 < GROUP:
            following = score(head + 1)
        largest = jnp.max(scores, axis=0, keepdims=True)
        powers = jnp.exp(scores - largest)
        totals = jnp.sum(powers, axis=0, keepdims=True)
        done.append(dot(values[spans[head]], powers.astype(BF), NN) * (1.0 / totals))
        log_totals[0, head : head + 1, :] = largest + jnp.log(totals)
    context[...] = jnp.concatenate(done, axis=0).T.astype(BF)


def join_kernel(x, context, weight, table, unit_rows, factor, low, base):
    branch = dot(context[...], weight[...], NN) + table[BO : BO + 1, :]
    rows = x[...].astype(F32) + branch
    center = rows - mean(rows)
    spread = lax.rsqrt(mean(center * center) + EPSILON)
    normed = center * spread
    unit_rows[...] = normed
    factor[...] = spread
    shifted = normed * table[GA : GA + 1, :] + table[SA : SA + 1, :]
    low[...] = shifted.astype(BF)
    base[...] = shifted + table[B2 : B2 + 1, :]


def gelu_pair(value):
    power = jnp.exp(value * value * -0.5)
    part = 1.0 / (1.0 + jnp.abs(value) * (0.3275911 * 0.5**0.5))
    tail = 0.5 * 1.061405429
    for factor in (-1.453152027, 1.421413741, -0.284496736, 0.254829592):
        tail = tail * part + 0.5 * factor
    tail = tail * part * power
    chance = jnp.where(value < 0.0, tail, 1.0 - tail)
    return value * chance, chance + value * power * (2.0 * jnp.pi) ** -0.5


def joined(refs):
    return jnp.concatenate([ref[...].reshape(-1, D) for ref in refs], axis=0)


def ffn_forward_kernel(places, low, *refs):
    bias, start, active, slope, running = refs[8:]
    rows = low[...]
    expand, reduce = joined(refs[:4]), joined(refs[4:8])
    shift = jnp.concatenate([bias[places[0]], bias[places[1]]], axis=1)
    total = start[...]
    for first in range(0, D, SUB):
        span = slice(first, first + SUB)
        value, change = gelu_pair(dot(rows, expand[span], NT) + shift[:, span])
        value = value.astype(BF)
        active[:, span] = value
        slope[:, span] = change.astype(BF)
        total = total + dot(value, reduce[span], NN)
    running[...] = total


def loss_kernel(length, rows, cotangent, table, output, grad, grad_low, sums):
    tile = rows.shape[0]
    value = rows[...]
    center = value - mean(value)
    factor = lax.rsqrt(mean(center * center) + EPSILON)
    normed = center * factor
    gain = table[GB : GB + 1, :]
    output[...] = (normed * gain + table[SB : SB + 1, :]).astype(BF)
    place = pl.program_id(0) * tile + lax.broadcasted_iota(jnp.int32, (tile, 1), 0)
    upstream = jnp.where(place < length[0], cotangent[...].astype(F32), 0.0)
    scaled = upstream * gain
    change = factor * (scaled - mean(scaled) - normed * mean(scaled * normed))
    grad[...] = change
    change_low = change.astype(BF)
    grad_low[...] = change_low

    @pl.when(pl.program_id(0) == 0)
    def _():
        sums[...] = jnp.zeros_like(sums)

    sums[0:1, :] += jnp.sum(upstream * normed, axis=0, keepdims=True)
    sums[1:2, :] += jnp.sum(upstream, axis=0, keepdims=True)
    sums[2:3, :] += jnp.sum(change_low.astype(F32), axis=0, keepdims=True)


def by_slot(grads, which, result):
    _, slots, deep, width, _ = grads.shape
    quarter = slots // 2
    result = jnp.concatenate(result, axis=0).reshape(2, 2, quarter, deep // 2, width, D)
    for place in range(2):
        for side in range(2):
            into = slice(place * quarter, (place + 1) * quarter), slice(side * (deep // 2), (side + 1) * (deep // 2))
            grads[which, into[0], into[1]] = result[place, side]


def reduce_backward_kernel(grad_low, active_a, active_b, grads):
    active = jnp.concatenate([active_a[...], active_b[...]], axis=1)
    by_slot(grads, 0, [dot(active[:, first : first + SUB], grad_low[...], TN).astype(BF) for first in range(0, D, SUB)])


def ffn_backward_kernel(both, grad_low, low, slope_a, slope_b, *refs):
    actives, refs = (refs[:2], refs[2:]) if both else ((), refs)
    start, grads, grad_bias, running = refs[8:]
    upstream, rows = grad_low[...], low[...]
    expand, reduce = joined(refs[:4]), joined(refs[4:8])
    slope = jnp.concatenate([slope_a[...], slope_b[...]], axis=1)
    if both:
        active = jnp.concatenate([actives[0][...], actives[1][...]], axis=1)
    reduced, expanded = [], []
    total = start[...]
    for first in range(0, D, SUB):
        span = slice(first, first + SUB)
        if both:
            reduced.append(dot(active[:, span], upstream, TN).astype(BF))
        change = (dot(upstream, reduce[span], NT) * slope[:, span].astype(F32)).astype(BF)
        grad_bias[:, span] = jnp.sum(change.astype(F32), axis=0, keepdims=True)
        expanded.append(dot(change, rows, TN).astype(BF))
        total = total + dot(change, expand[span], NN)
    running[...] = total
    if both:
        by_slot(grads, 0, reduced)
    by_slot(grads, int(both), expanded)


def sums_kernel(width, owners, sums_in, sums_one, sums_two, *refs):
    biases, out = refs[:4], refs[4]
    out[...] = jnp.zeros_like(out)
    count = D // width
    rows = (
        (BQ, sums_in[0, 0:1]),
        (BV, sums_in[2, 0:1]),
        (BO, sums_one[2:3]),
        (GA, sums_one[0:1]),
        (SA, sums_one[1:2]),
        (B2, sums_two[2:3]),
        (GB, sums_two[0:1]),
        (SB, sums_two[1:2]),
    )
    for row, value in rows:
        for piece in range(count):
            out[row * count + piece, :, :width] = value[:, piece * width : (piece + 1) * width]
    for place, ref in enumerate(biases):
        value = ref[...]
        for piece in range(count):
            into = owners[place * count + piece] + B1 * count
            out[into, :, :width] = value[:, piece * width : (piece + 1) * width]


def branch_kernel(upstream, unit_rows, factor, context, weight, table, grad, grad_context, grad_weight, sums):
    value = upstream[...]
    normed = unit_rows[...]
    scaled = value * table[GA : GA + 1, :]
    change = factor[...] * (scaled - mean(scaled) - normed * mean(scaled * normed))
    grad[...] = change
    change_low = change.astype(BF)

    @pl.when(pl.program_id(0) == 0)
    def _():
        sums[...] = jnp.zeros_like(sums)
        grad_weight[...] = jnp.zeros_like(grad_weight)

    sums[0:1, :] += jnp.sum(value * normed, axis=0, keepdims=True)
    sums[1:2, :] += jnp.sum(value, axis=0, keepdims=True)
    sums[2:3, :] += jnp.sum(change_low.astype(F32), axis=0, keepdims=True)
    grad_context[...] = dot(weight[...], change_low, NT).astype(BF)
    grad_weight[...] += dot(context[...], change_low, TN)


def attend_backward_kernel(count, *refs):
    length, packed, grad_context, log_totals, out = refs[count:]
    visible = lax.broadcasted_iota(jnp.int32, (LENGTH, LENGTH), 0) < length[0]
    spans = [slice(HEAD_DIM * head, HEAD_DIM * (head + 1)) for head in range(GROUP)]

    def score(head):
        span = spans[head]
        return dot(packed[1, span, :], packed[0, span, :], TN), dot(packed[2, span, :], grad_context[span, :], TN)

    following = score(0)
    for head in range(GROUP):
        span = spans[head]
        scores, grad_chances = following
        if head + 1 < GROUP:
            following = score(head + 1)
        chances = jnp.where(visible, jnp.exp(scores - log_totals[0, head : head + 1, :]), 0.0)
        out[2, span, :] = dot(grad_context[span, :], chances.astype(BF), NT).astype(BF)
        inner = jnp.sum(chances * grad_chances, axis=0, keepdims=True)
        grad_scores = (chances * (grad_chances - inner)).astype(BF)
        out[1, span, :] = dot(packed[0, span, :], grad_scores, NT).astype(BF)
        out[0, span, :] = (dot(packed[1, span, :], grad_scores, NN) * HEAD_DIM ** (-0.5)).astype(BF)


def in_grads_kernel(piece, owners, grads, x, grad_out, *refs):
    outs, (sums, held) = refs[:4], refs[4:]
    step = power_of_two(piece)
    which = pl.program_id(0)
    slots, rows = outs[0].shape[1], outs[0].shape[2] // 4

    def place(source, at):
        for side, ref in enumerate(outs):
            for slot in range(slots):
                for first in range(0, rows, piece):
                    index = ((side * slots + slot) * rows + first) // piece
                    start = pl.multiple_of(owners[index] * piece, step)
                    into = slice(at * rows + first, at * rows + first + piece)
                    ref[0, slot, into, :] = source[pl.ds(start, piece), :].astype(BF)

    held[...] = dot(grads[0], x[...], NN)
    sums[0] = dot(jnp.ones((8, LENGTH), BF), grads[0], NT)
    for at in range(3):
        pl.when(which == at)(partial(place, held, at))

    @pl.when(which == 0)
    def _():
        place(grad_out, 3)


def input_grad_kernel(grads, weights, residual, out):
    value = residual[...]
    for which in range(3):
        value = value + dot(grads[which], weights[which], TN)
    out[...] = value.astype(BF)


BLEND = min(0.999, (1 + STEP) / (10 + STEP))
RATES = (RATE_MATRIX, RATE_PROJECTION, RATE_MATRIX, RATE_MATRIX)


def advance(weight, velocity, average, gradient, factor, rate):
    clipped = gradient * factor
    velocity = MOMENTUM * velocity + clipped
    weight = weight - rate * (clipped + MOMENTUM * velocity)
    return weight, velocity, BLEND * average + (1.0 - BLEND) * weight


def update_kernel(squares, near, hidden, *refs):
    states, outs = refs[:12], refs[12:]
    value = squares[...]
    norm = jnp.sqrt(jnp.sum(value, axis=0)[:, 0:1])
    factor = 1.0 / jnp.maximum(norm, 1.0)
    outs[12][...] = norm
    gradients = (near[:3], near[3], hidden[1], hidden[0])
    for at, (gradient, rate) in enumerate(zip(gradients, RATES)):
        weight, velocity, average = states[at][...], states[4 + at][...], states[8 + at][...]
        results = advance(weight, velocity, average, gradient, factor, rate)
        for place, result in enumerate(results):
            outs[4 * place + at][...] = result


def body(
    wide,
    narrow,
    layer_input,
    cotangent,
    lengths,
    attention_in,
    attention_out,
    expand_weight,
    reduce_weight,
    vector_params,
    velocity_in,
    velocity_out,
    velocity_expand,
    velocity_reduce,
    velocity_vector,
    average_in,
    average_out,
    average_expand,
    average_reduce,
    average_vector,
):
    cube = Cube(wide, narrow)
    shards = wide * narrow
    share, width, spare = D // shards, FF // shards, NVEC // shards
    unit = share * narrow
    half = wide // 4
    groups = FF // D
    last = len(cube.plane) - 1
    owners = cube.plane_owners()
    held_kind = BF if unit % 16 == 0 else F32

    quarter, deep = half // 2, narrow // 2
    all_owners = cube.all_owners(jnp.arange(shards, dtype=jnp.int32))
    aligned = share % 8 == 0
    near = jnp.concatenate([attention_in.astype(BF).transpose(0, 2, 1).reshape(3 * share, D), attention_out.astype(BF)])
    vector = jnp.pad(vector_params.astype(BF).reshape(3, width), ((0, 0), (0, 128 - width))).reshape(1, 3 * 128)
    near = jnp.concatenate([near, jnp.pad(vector, ((0, 7), (0, D - 3 * 128)))]).reshape(1, 1, 4 * share + 8, D)
    hidden = jnp.stack([expand_weight.astype(BF).T, reduce_weight.astype(BF)]).reshape(1, 2, 1, width, D)
    final = len(cube.depth) - 1

    def early_slots(slots, axis):
        for step in range(final):
            slots = jnp.concatenate([slots, cube.swap_depth(slots, step)], axis=axis)
        return slots

    def plane_quarter(slots):
        for step in range(last - 1):
            slots = jnp.concatenate([slots, cube.swap_plane(slots, step)])
        return slots

    early = early_slots(near, 1)
    late = cube.swap_depth(early, final)
    hidden_early = early_slots(tie(hidden, late), 2)
    early, late = plane_quarter(early), plane_quarter(late)
    next_early, far_early = cube.swap_plane(early, last - 1), cube.swap_plane(early, last)
    late, next_early, far_early = lax.optimization_barrier((late, next_early, far_early))
    next_late, far_late = cube.swap_plane(late, last - 1), cube.swap_plane(late, last)
    beyond_early = cube.swap_plane(next_early, last)
    meeting = cube.swap_core(hidden_early[0, 0, deep - 1, :8, :128])
    hidden_early, meeting = lax.optimization_barrier((hidden_early, meeting))
    hidden_late = cube.swap_depth(hidden_early, final)
    next_late, beyond_early, far_late, hidden_early = lax.optimization_barrier(
        (next_late, beyond_early, far_late, hidden_early)
    )
    beyond_late = cube.swap_plane(next_late, last)
    hidden_early = plane_quarter(hidden_early)
    hidden_next_early, hidden_far_early = (cube.swap_plane(hidden_early, last - 1), cube.swap_plane(hidden_early, last))
    beyond_late, hidden_late, hidden_next_early = lax.optimization_barrier(
        (beyond_late, hidden_late, hidden_next_early)
    )
    hidden_late = plane_quarter(hidden_late)
    hidden_next_late, hidden_far_late = cube.swap_plane(hidden_late, last - 1), cube.swap_plane(hidden_late, last)
    attention = [early, late, next_early, next_late, far_early, far_late, beyond_early, beyond_late]
    attention += [cube.swap_core(part) for part in attention]
    order = [
        (place * quarter + slot) * narrow + side * deep + k
        for place in range(8)
        for side in range(2)
        for slot in range(quarter)
        for k in range(deep)
    ]
    hidden_owners = cube.all_owners(jnp.array(order, jnp.int32))
    pieces, piece, piece_order, piece_owners = attention, share, order, all_owners
    if not aligned:
        pieces, shares = [], []
        for place in range(8):
            part = jnp.concatenate(attention[2 * place : 2 * place + 2], axis=1)
            shares.append(part[:, :, 4 * share, : 3 * 128].reshape(-1, 1, 3 * 128).astype(F32))
            part = jnp.take(part[:, :, : 4 * share], cube.depth_slots(place // 4), axis=1)
            part = part.reshape(quarter, narrow, 4, share, D).transpose(0, 2, 1, 3, 4)
            pieces.append(part.reshape(quarter, 1, 4 * unit, D))
        pieces.append(jnp.concatenate(shares))
        piece, piece_order, piece_owners = unit, list(range(wide)), owners

    group_spec = pl.BlockSpec((3, GROUP * HEAD_DIM, LENGTH), lambda j: (0, j, 0))
    log_spec = pl.BlockSpec((1, GROUP, LENGTH), lambda j: (j, 0, 0))
    packed, weights_in, weight_out, context, log_totals, table, bias = run(
        partial(attend_kernel, piece, width, piece_order),
        "attend",
        (STEPS,),
        [(piece_owners, SMEM), (hidden_owners, SMEM), (lengths, SMEM)]
        + [(far_memory(layer_input), whole((LENGTH, D))), (meeting, ANY)]
        + [(far_memory(part), whole(part.shape)) for part in pieces],
        [
            (pltpu.HBM((3, D, LENGTH), BF), None, group_spec),
            (pltpu.HBM((3, D, D), BF), None, pl.BlockSpec((3, GROUP * HEAD_DIM, D), lambda j: (0, j, 0))),
            (pltpu.HBM((D, D), BF), None, pl.BlockSpec((GROUP * HEAD_DIM, D), lambda j: (j, 0))),
            ((LENGTH, D), BF, pl.BlockSpec((LENGTH, GROUP * HEAD_DIM), lambda j: (0, j))),
            ((STEPS, GROUP, LENGTH), F32, log_spec),
            ((16, D), F32, whole((16, D))),
            ((8, 1, D // 2), F32, whole((8, 1, D // 2))),
        ],
        scratch=[pltpu.VMEM((D, 16), F32), pltpu.VMEM((shards, 1, 3 * 128), F32), pltpu.VMEM((4, D, D), F32)],
        cost=(10 * D * D * LENGTH, 24 * D * D, HEADS * LENGTH * LENGTH),
        mebibytes=36,
    )
    context, hidden_next_early, hidden_next_late = lax.optimization_barrier((context, hidden_next_early, hidden_next_late))
    hidden = [
        (hidden_early, hidden_late),
        (hidden_next_early, hidden_next_late),
        (hidden_far_early, hidden_far_late),
        (cube.swap_plane(hidden_next_early, last), cube.swap_plane(hidden_next_late, last)),
    ]
    swap_both = lambda parts: tuple(cube.swap_core(part) for part in parts)
    hidden += [swap_both(hidden[0]), swap_both(hidden[1])]
    tile = 256
    row_spec = pl.BlockSpec((tile, D), lambda i: (i, 0))
    one_spec = pl.BlockSpec((tile, 1), lambda i: (i, 0))
    table_spec = whole((16, D))
    unit_rows, factor_one, low, running = run(
        join_kernel,
        "join",
        (LENGTH // tile,),
        [
            (layer_input, row_spec),
            (context, row_spec),
            (far_memory(weight_out), whole((D, D))),
            (table, table_spec),
        ],
        [
            ((LENGTH, D), F32, row_spec),
            ((LENGTH, 1), F32, one_spec),
            ((LENGTH, D), BF, row_spec),
            ((LENGTH, D), F32, row_spec),
        ],
        cost=(2 * D * D * LENGTH, 14 * LENGTH * D, 0),
        mebibytes=16,
    )

    rows_spec = pl.BlockSpec(memory_space=pltpu.VMEM)
    hidden_spec = lambda which: pl.BlockSpec((quarter, 1, deep, width, D), lambda *i: (0, which, 0, 0, 0))
    hidden_ins = lambda first, second: [
        (part, hidden_spec(which)) for which in range(2) for place in (first, second) for part in hidden[place]
    ]

    def forward(first, second, running):
        return run(
            partial(ffn_forward_kernel, (first, second)),
            "expand",
            (1,),
            [
                (low, rows_spec),
                *hidden_ins(first, second),
                (bias, whole((8, 1, D // 2))),
                (running, rows_spec),
            ],
            [
                (pltpu.HBM((LENGTH, D), BF), None, whole((LENGTH, D))),
                (pltpu.HBM((LENGTH, D), BF), None, whole((LENGTH, D))),
                ((LENGTH, D), F32, rows_spec),
            ],
            cost=(4 * D * D * LENGTH, 4 * D * D + 12 * LENGTH * D, 2 * LENGTH * D),
        )

    stored = [None] * 8
    for first, second in ((0, 1), (4, 5), (2, 6), (3, 7)):
        if first == 4:
            hidden[2] = lax.optimization_barrier((*hidden[2], running))[:2]
            hidden += [swap_both(hidden[2])]
        if first == 2:
            beyond_early, beyond_late, running = lax.optimization_barrier((*hidden[3], running))
            hidden[3] = beyond_early, beyond_late
            hidden += [swap_both(hidden[3])]
        active, slope, running = forward(first, second, running)
        stored[first] = (active, slope, 0)
        stored[second] = (active, slope, 1)
    sum_spec = whole((8, D))
    output, grad_two, grad_low, sums_two = run(
        loss_kernel,
        "loss",
        (LENGTH // tile,),
        [(lengths, SMEM), (running, row_spec), (cotangent, row_spec), (table, table_spec)],
        [
            ((LENGTH, D), BF, row_spec),
            ((LENGTH, D), F32, row_spec),
            ((LENGTH, D), BF, row_spec),
            (pltpu.HBM((8, D), F32), None, sum_spec),
        ],
        cost=(40 * LENGTH * D, 14 * LENGTH * D, 0),
    )
    column = lambda place: pl.BlockSpec((LENGTH, D // 2), lambda *i: (0, stored[place][2]))

    def reduce_backward(first):
        shape = (1, half, narrow, width, D)
        return run(
            reduce_backward_kernel,
            "reduce_back",
            (1,),
            [(grad_low, rows_spec)] + [(stored[place][0], column(place)) for place in (first, first + 1)],
            [(pltpu.HBM(shape, BF), None, whole(shape))],
            cost=(2 * D * D * LENGTH, 2 * D * D + 4 * LENGTH * D, 0),
        )[0]

    def backward(both, first, running):
        shape = (1 + both, half, narrow, width, D)
        return run(
            partial(ffn_backward_kernel, both),
            "expand_back",
            (1,),
            [(grad_low, rows_spec), (low, rows_spec)]
            + [(stored[place][1], column(place)) for place in (first, first + 1)]
            + [(stored[place][0], column(place)) for place in (first, first + 1) if both]
            + hidden_ins(first, first + 1)
            + [(running, rows_spec)],
            [
                (pltpu.HBM(shape, BF), None, whole(shape)),
                ((1, D), F32, whole((1, D))),
                ((LENGTH, D), F32, rows_spec),
            ],
            cost=(8 * D * D * LENGTH, 8 * D * D + 12 * LENGTH * D, 0),
        )

    other_reduce = cube.swap_core(reduce_backward(6))
    own_reduce = reduce_backward(2)
    leaving_reduce = combine([own_reduce, other_reduce], 1, 0, half)
    arrived_reduce = cube.swap_plane(leaving_reduce, last)
    grad_two = tie(grad_two, leaving_reduce)
    other_expand, bias_6, running = backward(False, 6, grad_two)
    other_expand = cube.swap_core(other_expand)
    own_expand, bias_2, running = backward(False, 2, running)
    leaving_expand = combine([own_expand, other_expand], 1, 0, half)
    arrived_expand = cube.swap_plane(leaving_expand, last)
    other_near, bias_4, running = backward(True, 4, tie(running, leaving_expand))
    other_near = cube.swap_core(other_near)
    own_near, bias_0, running = backward(True, 0, running)
    hidden_parts = [own_near, tie(other_near, running), (arrived_reduce, arrived_expand)]

    grad_one, grad_context, grad_out, sums_one = run(
        branch_kernel,
        "branch_back",
        (LENGTH // tile,),
        [
            (running, row_spec),
            (unit_rows, row_spec),
            (factor_one, one_spec),
            (context, row_spec),
            (weight_out, whole((D, D))),
            (table, table_spec),
        ],
        [
            (pltpu.HBM((LENGTH, D), F32), None, row_spec),
            ((D, LENGTH), BF, pl.BlockSpec((D, tile), lambda i: (0, i))),
            ((D, D), F32, whole((D, D))),
            (pltpu.HBM((8, D), F32), None, sum_spec),
        ],
        cost=(4 * D * D * LENGTH, 8 * D * D + 16 * LENGTH * D, 0),
    )
    def attend_backward(first, steps, grad_context, *before):
        place = lambda j: (0, j + first, 0)
        block = (3, GROUP * HEAD_DIM, LENGTH)
        return run(
            partial(attend_backward_kernel, len(before)),
            "attend_back",
            (steps,),
            [(array, ANY) for array in before]
            + [
                (lengths, SMEM),
                (packed, pl.BlockSpec(block, place)),
                (grad_context, pl.BlockSpec((GROUP * HEAD_DIM, LENGTH), lambda j: (j + first, 0))),
                (log_totals, pl.BlockSpec((1, GROUP, LENGTH), lambda j: (j + first, 0, 0))),
            ],
            [((3, D, LENGTH), BF, pl.BlockSpec(block, place))],
            cost=(10 * HEADS * LENGTH * LENGTH * HEAD_DIM, 14 * LENGTH * D, HEADS * LENGTH * LENGTH),
            alias={0: 0} if before else None,
        )[0]

    def send(parts, axis):
        middle = flat(parts[-1:])[0].shape[axis] // 2
        return combine(parts, axis, middle, middle)

    grads = attend_backward(0, STEPS - 1, grad_context)
    hidden_parts[0] = tie(hidden_parts[0], grads)
    hidden_leaving = send(hidden_parts, 1)
    grads = attend_backward(STEPS - 1, 1, tie(grad_context, hidden_leaving), grads)
    hidden_parts.append(cube.swap_plane(hidden_leaving, last - 1))
    chunk = (1, half, 4 * unit, D)
    *chunks, sums_in = run(
        partial(in_grads_kernel, share if aligned else unit),
        "project_back",
        (3,),
        [
            (all_owners if aligned else owners, SMEM),
            (grads, pl.BlockSpec((1, D, LENGTH), lambda i: (i, 0, 0))),
            (layer_input, whole((LENGTH, D))),
            (grad_out, whole((D, D))),
        ],
        [(pltpu.HBM(chunk, BF), None, whole(chunk))] * 4
        + [((3, 8, D), F32, pl.BlockSpec((1, 8, D), lambda i: (i, 0, 0)))],
        scratch=[pltpu.VMEM((D, D), F32)],
        cost=(6 * D * D * LENGTH, 12 * D * D, 0),
        mebibytes=32,
    )
    if not aligned:
        for place, part in enumerate(chunks):
            order = cube.depth_owners(place // 2)
            part = jnp.take(part.reshape(half, 4, narrow, share, D), order, axis=2)
            chunks[place] = part.reshape(chunk)
    own_near, own_far, other_near, other_far = chunks
    other_far, other_near = cube.swap_core(other_far), cube.swap_core(other_near)
    (grad_vector,) = run(
        partial(sums_kernel, width),
        "sums",
        (1,),
        [
            (hidden_owners, SMEM),
            (sums_in, whole((3, 8, D))),
            (sums_one, sum_spec),
            (sums_two, sum_spec),
        ]
        + [(part, whole((1, D))) for part in (bias_0, bias_2, bias_4, bias_6)],
        [((3 * shards, 1, 128), F32, whole((3 * shards, 1, 128)))],
        mebibytes=8,
    )
    own_far, hidden_parts[-1] = lax.optimization_barrier((own_far, hidden_parts[-1]))
    for step in reversed(range(last - 1)):
        hidden_parts.append(cube.swap_plane(send(hidden_parts, 1), step))
    view = lambda part: part.reshape(1, half, 4, narrow, share, D)
    own_near, own_far, other_near, other_far = (view(part) for part in (own_near, own_far, other_near, other_far))
    late = cube.swap_plane(combine([own_far, other_far], 3, deep, deep), last)
    early = cube.swap_plane(combine([own_far, other_far], 3, 0, deep), last)
    hidden_going = send(hidden_parts, 2)
    grads = tie(grads, hidden_going)
    (input_grad,) = run(
        input_grad_kernel,
        "input_back",
        (LENGTH // tile,),
        [
            (grads, pl.BlockSpec((3, D, tile), lambda i: (0, 0, i))),
            (far_memory(weights_in), whole((3, D, D))),
            (far_memory(grad_one), row_spec),
        ],
        [((LENGTH, D), BF, row_spec)],
        cost=(6 * D * D * LENGTH, 6 * D * D + 12 * LENGTH * D, 0),
    )
    late, input_grad = lax.optimization_barrier((late, input_grad))
    hidden_parts.append(cube.swap_depth(hidden_going, final))
    late_parts, early_parts = [own_near, other_near, late], [own_near, other_near, early]
    late_deeps = [1, 1, 0]
    for step in reversed(range(last)):
        middle = late_parts[-1].shape[1] // 2
        late_parts.append(cube.swap_plane(combine(late_parts, 1, middle, middle, late_deeps), step))
        late_deeps.append(0)
        early_parts.append(cube.swap_plane(combine(early_parts, 1, middle, middle, [0] * len(early_parts)), step))
    going = combine(late_parts, 1, 0, 1, late_deeps)
    early_parts.append(cube.swap_depth(going, final))
    grad_vector = lax.all_to_all(tie(grad_vector, going), AXES, 0, 0, tiled=True)
    early_parts[-1], grad_vector = lax.optimization_barrier((early_parts[-1], grad_vector))
    for step in reversed(range(final)):
        early_parts.append(cube.swap_depth(send(early_parts, 3), step))
        hidden_parts.append(cube.swap_depth(send(hidden_parts, 2), step))
    parts = early_parts
    owned_hidden, squares, owned_vector = finish(hidden_parts, grad_vector, shards)
    owned_near, squares = finish(parts, squares, shards)
    squares = lax.all_to_all(squares, AXES, 0, 0)

    turn = lambda array: array.transpose(*range(array.ndim - 2), -1, -2)
    states = []
    for first, second, third, fourth in (
        (attention_in, attention_out, expand_weight, reduce_weight),
        (velocity_in, velocity_out, velocity_expand, velocity_reduce),
        (average_in, average_out, average_expand, average_reduce),
    ):
        states += [turn(first), second, turn(third), fourth]
    near, hidden = owned_near.reshape(4, share, D), owned_hidden.reshape(2, width, D)
    vector = owned_vector[:, 0, :width].reshape(spare)
    *states, grad_norm = run(
        update_kernel,
        "update",
        (1,),
        [(squares, whole(squares.shape)), (near, whole(near.shape))]
        + [(far_memory(array), whole(array.shape)) for array in [hidden] + states],
        [(array.shape, F32, whole(array.shape)) for array in states] + [((1, 1), F32, whole((1, 1)))],
        cost=(FF * D, 28 * (share * 4 + width * 2) * D, 0),
    )
    grad_norm = grad_norm.reshape(())
    vectors = advance(
        vector_params, velocity_vector, average_vector, vector, 1.0 / jnp.maximum(grad_norm, 1.0), RATE_VECTOR
    )
    outs = []
    for place in range(3):
        first, second, third, fourth = states[4 * place : 4 * place + 4]
        outs += [turn(first), second, turn(third), fourth, vectors[place]]
    return (output, input_grad, *outs, grad_norm)


def solution(mesh):
    both = ("wide", "narrow")
    first, second, third = P(both, None), P(None, both), P(None, None, both)
    state = (third, first, second, first, P(both))
    return jax.shard_map(
        partial(body, mesh.shape["wide"], mesh.shape["narrow"]),
        mesh=mesh,
        in_specs=(first, first, P(both)) + state * 3,
        out_specs=(first, first) + state * 3 + (P(),),
        check_vma=False,
    )
```
